32 devices in a mesh: groups: 2 (over x), sample: 16 (over z, y, core).
Axes of the slice: x: 2, y: 2, z: 4, core: 2. Of those that a mesh axis runs over, the one named last changes fastest.
Arguments:
- prompt_kv: bfloat16 [64, 16, 32, 2048], P('groups', 'sample'), parts along dimension 0, may hold values from -16 to 16
- prompt_blocks: int32 [16], P('groups'), parts along dimension 0, may hold values from 1 to 128, 512 in all
- slot_prompt: int32 [32], P('groups'), parts along dimension 0, may hold values from 0 to 7, as said below
- queries: bfloat16 [256, 4, 8192], P(('groups', 'sample')), parts along dimension 0, may hold values from -24 to 24
- new_kv: bfloat16 [256, 4, 2048], P(('groups', 'sample')), parts along dimension 0, may hold values from -16 to 16
Outputs:
- attention: bfloat16 [256, 4, 8192], P(('groups', 'sample')), parts along dimension 0
- deviation: bfloat16 [256, 4, 8192], P(('groups', 'sample')), parts along dimension 0
The draws below stay inside these ranges and needn't reach their ends.
There are 2 independent parts, one for each index of `groups`. The reference program is written for one: setup_inputs(seed, part) draws one part's arguments, and reference() takes and returns one part's arrays. A program takes and returns all parts, laid end to end along the dimension named above; each array names one. Nothing has to cross between parts.
Inputs may be any that keep to these rules, and one draw needn't show every extreme that they name: `slot_prompt`: slots 2s and 2s + 1 decode the same prompt, and each prompt is decoded by exactly one such pair of slots. `prompt_blocks`: counts of whole blocks of 32 tokens; they sum to 512.
All inputs are finite; a program needn't handle non-finite values.
Results may differ from the reference program's by a relative error of at most 0.0055.
Values may be sent and summed in bfloat16 or wider, within the bound.
No kernel may reach another device: no remote copies, remote signals or barrier semaphores. Data moves between devices by JAX's collectives and lax.ppermute only.
A program may use at most 128 MiB of HBM per device.

```python
import math
import jax
import jax.numpy as jnp
import numpy as np
from jax import lax

HEADS = 64
KVH = 8
HD = 128
STEPS = 4
SAMP_DEV = 8
BLK = 32
MAXB = 128
BLK_DEV = 32
PROMPTS = 8
N_SAMPLE = 16


def draw_prompt_kv(key, part):
    key = jax.random.fold_in(key, 12)
    leading = (BLK_DEV, N_SAMPLE, BLK)
    values = lifted_pairs_from(key, leading)
    return values.reshape(BLK_DEV, N_SAMPLE, BLK, 2 * KVH * HD).astype(jnp.bfloat16)


def lifted_pairs_from(key, leading):
    noise_key = jax.random.fold_in(key, 0)
    values = jnp.clip(jax.random.normal(noise_key, leading + (2, KVH, HD), jnp.float32), -4.0, 4.0)
    return values


def draw_new_kv(key, part):
    key = jax.random.fold_in(key, 14)
    leading = (N_SAMPLE * SAMP_DEV, STEPS)
    values = lifted_pairs_from(key, leading)
    return values.reshape(N_SAMPLE * SAMP_DEV, STEPS, 2 * KVH * HD).astype(jnp.bfloat16)


def draw_queries(key, part):
    key = jax.random.fold_in(key, 11)
    shared_key, single_key = jax.random.split(key, 2)
    pair_count = N_SAMPLE // 2
    shared = jnp.clip(jax.random.normal(shared_key, (pair_count, 1, STEPS, HEADS * HD), jnp.float32), -4.0, 4.0)
    single = jnp.clip(jax.random.normal(single_key, (pair_count, 2 * SAMP_DEV, STEPS, HEADS * HD), jnp.float32), -4.0, 4.0)
    values = 2.0 * (0.7 * shared + 0.7 * single)
    values = values.reshape(N_SAMPLE * SAMP_DEV, STEPS, KVH, HEADS // KVH, HD)
    return values.reshape(N_SAMPLE * SAMP_DEV, STEPS, HEADS * HD).astype(jnp.bfloat16)


def draw_slot_prompt(key, part):
    key = jax.random.fold_in(key, 13)
    order = jax.random.permutation(key, N_SAMPLE // 2)
    return jnp.repeat(order, 2).astype(jnp.int32)


def profile(number_of, total, bound, slope):
    loads = [(1 << 20) // math.isqrt(standing ** slope) + 1 for standing in range(2, number_of + 1)]
    rest, counts = total - bound - (number_of - 1), [1] * (number_of - 1)
    while rest > 0:
        candidates = [i for i in range(number_of - 1) if counts[i] < bound]
        pool, remaining = sum([loads[i] for i in candidates]), rest
        for i in candidates:
            more = min(bound - counts[i], max(1, remaining * loads[i] // pool), rest)
            counts[i] = counts[i] + more
            rest = rest - more
    return np.array([bound] + counts)


def ragged_sizes(key, number_of, total, reach, lean):
    if number_of == 2:
        one = jax.random.randint(key, (), max(1, total - reach), min(reach, total - 1) + 1)
        return jnp.stack([one, total - one])
    sizes = jnp.asarray(profile(number_of, total, reach, lean), jnp.int32)
    couples = (number_of - 1) // 2
    giver, taker = sizes[1:1 + 2 * couples:2], sizes[2:2 + 2 * couples:2]
    room = jnp.minimum(giver - 1, reach - taker)
    moved = jax.random.randint(jax.random.fold_in(key, 1), (couples,), 0, 1 << 20) % (room + 1)
    sizes = sizes.at[1:1 + 2 * couples:2].set(giver - moved).at[2:2 + 2 * couples:2].set(taker + moved)
    return sizes[jax.random.permutation(jax.random.fold_in(key, 2), number_of)]


def setup_inputs(seed: int = 0, part: int = 0) -> dict:
    key_list = jax.random.split(jax.random.key(seed), 6)
    part_splits = jax.random.split(jax.random.fold_in(key_list[5], part), 6)
    return {
        "prompt_kv": draw_prompt_kv(jax.random.fold_in(jax.random.fold_in(key_list[5], part), 71), part),
        "prompt_blocks": ragged_sizes(part_splits[1], PROMPTS, BLK_DEV * N_SAMPLE, MAXB, 2).astype(jnp.int32),
        "slot_prompt": draw_slot_prompt(jax.random.fold_in(jax.random.fold_in(key_list[5], part), 71), part),
        "queries": draw_queries(jax.random.fold_in(jax.random.fold_in(key_list[5], part), 71), part),
        "new_kv": draw_new_kv(jax.random.fold_in(jax.random.fold_in(key_list[5], part), 71), part),
    }


NEG_FILL = -1e+30

def reference(prompt_kv, prompt_blocks, slot_prompt, queries, new_kv):
    group_size = HEADS // KVH
    row_width = 2 * KVH * HD
    window_rows = MAXB * BLK
    token_stream = prompt_kv.reshape(BLK_DEV * N_SAMPLE * BLK, row_width)
    token_stream = jnp.concatenate([token_stream, jnp.zeros((window_rows, row_width), token_stream.dtype)], axis=0)
    block_starts = (jnp.cumsum(prompt_blocks) - prompt_blocks).astype(jnp.int32)
    score_scale = 1.0 / math.sqrt(HD)
    slot_queries = queries.reshape(N_SAMPLE, SAMP_DEV, STEPS, KVH, group_size, HD)
    slot_fresh = new_kv.reshape(N_SAMPLE, SAMP_DEV, STEPS, 2, KVH, HD)
    step_order = jnp.arange(STEPS)
    allowed = step_order[:, None] >= step_order[None, :]
    row_order = jnp.arange(window_rows)

    def one_slot(slot_inputs):
        slot_query, fresh_kv, prompt_id = slot_inputs
        first_row = (block_starts[prompt_id] * BLK).astype(jnp.int32)
        row_count = prompt_blocks[prompt_id] * BLK
        prompt_window = lax.dynamic_slice_in_dim(token_stream, first_row, window_rows, 0)
        prompt_window = prompt_window.reshape(window_rows, 2, KVH, HD)
        usable = row_order < row_count
        query_full = slot_query.astype(jnp.float32)
        prompt_scores = jnp.einsum('stghd,lgd->stghl', query_full, prompt_window[:, 0].astype(jnp.float32)) * score_scale
        prompt_scores = jnp.where(usable[None, None, None, None, :], prompt_scores, NEG_FILL)
        fresh_scores = jnp.einsum('stghd,sugd->stghu', query_full, fresh_kv[:, :, 0].astype(jnp.float32)) * score_scale
        fresh_scores = jnp.where(allowed[None, :, None, None, :], fresh_scores, NEG_FILL)
        row_peak = jnp.maximum(lax.optimization_barrier(jnp.max(prompt_scores, axis=-1)), lax.optimization_barrier(jnp.max(fresh_scores, axis=-1)))
        prompt_raised = jnp.exp(prompt_scores - row_peak[..., None])
        fresh_raised = jnp.exp(fresh_scores - row_peak[..., None])
        weight_sum = lax.optimization_barrier(jnp.sum(prompt_raised, axis=-1)) + lax.optimization_barrier(jnp.sum(fresh_raised, axis=-1))
        prompt_weights = lax.optimization_barrier(prompt_raised.astype(jnp.bfloat16)).astype(jnp.float32)
        fresh_weights = lax.optimization_barrier(fresh_raised.astype(jnp.bfloat16)).astype(jnp.float32)
        weighted = jnp.einsum('stghl,lgd->stghd', prompt_weights, prompt_window[:, 1].astype(jnp.float32))
        weighted = weighted + jnp.einsum('stghu,sugd->stghd', fresh_weights, fresh_kv[:, :, 1].astype(jnp.float32))
        return (weighted / weight_sum[..., None]).reshape(SAMP_DEV, STEPS, HEADS * HD)
    attention_full = lax.map(one_slot, (slot_queries, slot_fresh, slot_prompt))
    paired = attention_full.reshape(N_SAMPLE // 2, 2 * SAMP_DEV, STEPS, HEADS * HD)
    centroid = lax.optimization_barrier(jnp.mean(paired, axis=1, keepdims=True))
    deviation = (paired - centroid).reshape(N_SAMPLE * SAMP_DEV, STEPS, HEADS * HD)
    attention = attention_full.reshape(N_SAMPLE * SAMP_DEV, STEPS, HEADS * HD)
    return (attention.astype(jnp.bfloat16), deviation.astype(jnp.bfloat16))
```

```python
import functools
import math

import jax
import jax.numpy as jnp
from jax import lax
from jax.experimental import pallas as pl
from jax.experimental.pallas import tpu as pltpu
from jax.sharding import PartitionSpec as P

HEADS = 64
KVH = 8
HD = 128
BLK = 32
QUAD = 4
HPD = KVH // QUAD
GROUP = HEADS // KVH
TILE_BLOCKS = 8
TILE = TILE_BLOCKS * BLK
NEG = -1e30
EXP_SCALE = math.log2(math.e) / math.sqrt(HD)
F32 = jnp.float32
BF16 = jnp.bfloat16
ANY = pl.BlockSpec(memory_space=pl.ANY)
VMEM = pl.BlockSpec(memory_space=pltpu.VMEM)
SMEM = pl.BlockSpec(memory_space=pltpu.SMEM)


def lanes(start, size):
    return pl.ds(pl.multiple_of(start, 128), size)


def params(mib):
    return pltpu.CompilerParams(vmem_limit_bytes=mib << 20)


def cost(flops, nbytes, trans=0):
    return pl.CostEstimate(flops=flops, bytes_accessed=nbytes, transcendentals=trans)


def pack_queries_kernel(q_ref, new_ref, *outs):
    mine = lax.rem(lax.axis_index("sample"), QUAD)
    rows = q_ref.shape[0]
    for k, out in enumerate(outs):
        peer = jnp.bitwise_xor(mine, k)
        for h in range(HPD):
            head = peer * HPD + h
            for g in range(GROUP):
                out[h, g * rows:(g + 1) * rows] = q_ref[:, lanes((head * GROUP + g) * HD, HD)]
            base = GROUP * rows
            out[h, base:base + rows] = new_ref[:, lanes(head * HD, HD)]
            out[h, base + rows:base + 2 * rows] = new_ref[:, lanes((KVH + head) * HD, HD)]


def pack_queries(q2, new2):
    rows = q2.shape[0]
    shape = jax.ShapeDtypeStruct((HPD, (GROUP + 2) * rows, HD), BF16)
    return pl.pallas_call(
        pack_queries_kernel,
        out_shape=[shape] * QUAD,
        in_specs=[VMEM, VMEM],
        out_specs=[VMEM] * QUAD,
        compiler_params=params(32),
        cost_estimate=cost(0, 2 << 20),
        name="pack_queries",
    )(q2, new2)


def pack_kv_kernel(kv_ref, *refs):
    outs, sem = refs[:-1], refs[-1]
    mine = lax.rem(lax.axis_index("sample"), QUAD)
    copies = []
    for h in range(HPD):
        for k in range(1, QUAD):
            head = jnp.bitwise_xor(mine, k) * HPD + h
            out = outs[h * (QUAD - 1) + k - 1]
            for part in range(2):
                copies.append(
                    pltpu.make_async_copy(
                        kv_ref.at[:, lanes((part * KVH + head) * HD, HD)],
                        out.at[:, part * HD:(part + 1) * HD],
                        sem.at[len(copies)],
                    )
                )
    for copy in copies:
        copy.start()
    for copy in copies:
        copy.wait()


def pack_kv(kv2):
    count = HPD * (QUAD - 1)
    shape = jax.ShapeDtypeStruct((kv2.shape[0], 2 * HD), BF16)
    return pl.pallas_call(
        pack_kv_kernel,
        out_shape=[shape] * count,
        in_specs=[ANY],
        out_specs=[ANY] * count,
        scratch_shapes=[pltpu.SemaphoreType.DMA((2 * count,))],
        compiler_params=params(16),
        cost_estimate=cost(0, 6 << 20),
        name="pack_kv",
    )(kv2)


def as_rows(column):
    size = column.shape[0]
    out = []
    for i in range(size // 128):
        block = jnp.broadcast_to(column[i * 128:(i + 1) * 128], (128, 128))
        out.append(block.T[0:1])
    return jnp.concatenate(out, axis=0)


def as_columns(rows):
    out = []
    for i in range(rows.shape[0]):
        out.append(jnp.broadcast_to(rows[i:i + 1], (128, 128)).T)
    return jnp.concatenate(out, axis=0)


def dot_t(a, b):
    return lax.dot_general(a, b, (((1,), (1,)), ((), ())), preferred_element_type=F32)


def attend_kernel(h, offsets, fresh, counts_ref, slots_ref, kv_ref, *refs):
    nsample = lax.axis_size("sample")
    quads = nsample // QUAD
    index = lax.axis_index("sample")
    quad, mine = lax.div(index, QUAD), lax.rem(index, QUAD)
    arrived = refs[:QUAD - 1]
    refs = refs[QUAD - 1:]
    nq = QUAD if fresh else len(offsets)
    queries, refs = refs[:nq], refs[nq:]
    outs, (held, sem) = refs[:-2], refs[-2:]
    blocks = kv_ref.shape[0]

    copies = []
    for part in range(2):
        copies.append(
            pltpu.make_async_copy(
                kv_ref.at[:, :, lanes((part * KVH + mine * HPD + h) * HD, HD)],
                held.at[0:blocks, mine, :, part * HD:(part + 1) * HD],
                sem.at[part],
            )
        )
    for k in range(1, QUAD):
        copies.append(
            pltpu.make_async_copy(
                arrived[k - 1], held.at[0:blocks, jnp.bitwise_xor(mine, k)], sem.at[k + 1]
            )
        )
    for copy in copies:
        copy.start()
    held[blocks:] = jnp.zeros_like(held[blocks:])
    for copy in copies:
        copy.wait()
    flat = held.reshape(held.shape[0] * QUAD * BLK, 2 * HD)

    def local_count(block):
        inside = jnp.clip(lax.rem(block, nsample) - QUAD * quad, 0, QUAD)
        return QUAD * lax.div(block, nsample) + inside

    for n, offset in enumerate(offsets):
        home = lax.rem(quad + offset, quads)
        for pair in range(2):
            slot_pair = jnp.bitwise_xor(lax.div(mine, 2), pair)
            prompt = slots_ref[QUAD * home + 2 * slot_pair]
            start = lax.fori_loop(0, prompt, lambda p, total: total + counts_ref[p], jnp.int32(0))
            low, high = local_count(start), local_count(start + counts_ref[prompt])
            if fresh:
                parts = []
                for half in range(2):
                    msg = queries[2 * pair + half]
                    rows = msg.shape[1] // (GROUP + 2)
                    query = msg[h, 0:GROUP * rows]
                    new_k = msg[h, GROUP * rows:(GROUP + 1) * rows]
                    new_v = msg[h, (GROUP + 1) * rows:]
                    s = dot_t(query, new_k)
                    row = lax.rem(lax.broadcasted_iota(jnp.int32, s.shape, 0), rows)
                    col = lax.broadcasted_iota(jnp.int32, s.shape, 1)
                    steps = fresh
                    seen = (lax.div(row, steps) == lax.div(col, steps)) & (
                        lax.rem(row, steps) >= lax.rem(col, steps)
                    )
                    s = jnp.where(seen, s, NEG)
                    m = jnp.max(s, axis=1, keepdims=True)
                    p = jnp.exp2((s - m) * EXP_SCALE)
                    l = jnp.sum(p, axis=1, keepdims=True)
                    acc = jnp.dot(p.astype(BF16), new_v, preferred_element_type=F32)
                    parts.append((query, m, l, acc))
                query, m, l, acc = (jnp.concatenate(x, axis=0) for x in zip(*parts))
            else:
                query = jnp.concatenate([queries[n][2 * pair], queries[n][2 * pair + 1]], axis=0)
                size = query.shape[0]
                m = jnp.full((size, 1), NEG, F32)
                l = jnp.zeros((size, 1), F32)
                acc = jnp.zeros((size, HD), F32)

            def body(t, carry, query=query, low=low, high=high):
                m, l, acc = carry
                first = low + t * TILE_BLOCKS
                row = pl.multiple_of(first * BLK, BLK)
                k = flat[pl.ds(row, TILE), 0:HD]
                v = flat[pl.ds(row, TILE), HD:2 * HD]
                s = dot_t(query, k)
                col = lax.broadcasted_iota(jnp.int32, s.shape, 1)
                s = jnp.where(col < (high - first) * BLK, s, NEG)
                m_new = jnp.maximum(m, jnp.max(s, axis=1, keepdims=True))
                p = jnp.exp2((s - m_new) * EXP_SCALE)
                alpha = jnp.exp2((m - m_new) * EXP_SCALE)
                l = l * alpha + jnp.sum(p, axis=1, keepdims=True)
                acc = acc * alpha + jnp.dot(p.astype(BF16), v, preferred_element_type=F32)
                return m_new, l, acc

            tiles = lax.div(high - low + TILE_BLOCKS - 1, TILE_BLOCKS)
            m, l, acc = lax.fori_loop(0, tiles, body, (m, l, acc))
            some = l > 0.0
            out = acc / jnp.where(some, l, 1.0)
            lse = jnp.where(some, m * EXP_SCALE + jnp.log(jnp.where(some, l, 1.0)) * math.log2(math.e), NEG)
            if fresh:
                outs[0][pair] = out
                outs[1][pair] = jnp.broadcast_to(lse, out.shape)
            else:
                size = out.shape[0]
                stat = as_rows(lse)
                high_part = stat.astype(BF16)
                rest = stat - high_part.astype(F32)
                mid_part = rest.astype(BF16)
                low_part = (rest - mid_part.astype(F32)).astype(BF16)
                pad = jnp.zeros((16 - 3 * stat.shape[0], HD), F32)
                tail = jnp.concatenate(
                    [high_part.astype(F32), mid_part.astype(F32), low_part.astype(F32), pad], axis=0
                )
                outs[n][pair, 0:size] = out.astype(BF16)
                outs[n][pair, size:size + 16] = tail.astype(BF16)


def attend(h, offsets, fresh, counts, slots, kv3, arrived, queries):
    size = 2 * (queries[0].shape[1] * GROUP // (GROUP + 2) if fresh else queries[0].shape[1])
    if fresh:
        out_shape = [jax.ShapeDtypeStruct((2, size, HD), F32)] * 2
    else:
        out_shape = [jax.ShapeDtypeStruct((2, size + 16, HD), BF16)] * len(offsets)
    blocks = kv3.shape[0]
    work = len(offsets) * 2 * size * blocks * BLK // 2
    return pl.pallas_call(
        functools.partial(attend_kernel, h, offsets, fresh),
        out_shape=out_shape,
        in_specs=[SMEM, SMEM, ANY] + [ANY] * len(arrived) + [VMEM] * len(queries),
        out_specs=[VMEM] * len(out_shape),
        scratch_shapes=[
            pltpu.VMEM((blocks + 2, QUAD, BLK, 2 * HD), BF16),
            pltpu.SemaphoreType.DMA((QUAD + 1,)),
        ],
        compiler_params=params(48),
        cost_estimate=cost(4 * work * HD, 4 << 20, work),
        name="attend_own" if fresh else "attend_others",
    )(counts, slots, kv3, *arrived, *queries)


def finish_kernel(steps, own_ref, own_lse_ref, *refs):
    parts, outs = refs[:-QUAD], refs[-QUAD:]
    size = own_ref.shape[1]
    stats = size // 128
    for pair in range(2):
        values, lses = [own_ref[pair]], [own_lse_ref[pair]]
        for ref in parts:
            values.append(ref[pair, 0:size].astype(F32))
            tail = ref[pair, size:size + 16].astype(F32)
            lses.append(
                as_columns(tail[0:stats] + tail[stats:2 * stats] + tail[2 * stats:3 * stats])
            )
        top = functools.reduce(jnp.maximum, lses)
        total, weight = None, None
        for value, lse in zip(values, lses):
            w = jnp.exp2(lse - top)
            total = value * w if total is None else total + value * w
            weight = w if weight is None else weight + w
        full = total / weight
        rows = size // (2 * GROUP)
        wide = full.reshape(2, GROUP, rows // 8, 8, HD)
        mean = jnp.sum(wide, axis=(0, 2)) * (steps / (2.0 * rows))
        if steps == 4:
            flat = mean.reshape(GROUP * 8, HD)
            lane_row = lax.rem(lax.broadcasted_iota(jnp.int32, flat.shape, 0), 8)
            up, down = pltpu.roll(flat, 4, 0), pltpu.roll(flat, GROUP * 8 - 4, 0)
            flat = flat + jnp.where(lane_row < 4, down, up)
            mean = flat.reshape(GROUP, 8, HD)
        dev = wide - mean[None, :, None]
        flat = mean.reshape(GROUP * 8, HD)
        coarse = flat.astype(BF16).astype(F32)
        lane_row = lax.rem(lax.broadcasted_iota(jnp.int32, flat.shape, 0), 8)
        carried = jnp.where(lane_row < 4, coarse, flat - coarse).astype(BF16)
        dev = dev.reshape(2, size // 2, HD).astype(BF16)
        for half in range(2):
            out = outs[2 * pair + half]
            out[0:size // 2] = dev[half]
            out[size // 2:] = carried


def finish(steps, own, own_lse, parts):
    size = own.shape[1]
    shape = jax.ShapeDtypeStruct((size // 2 + GROUP * 8, HD), BF16)
    return pl.pallas_call(
        functools.partial(finish_kernel, steps),
        out_shape=[shape] * QUAD,
        in_specs=[VMEM] * (2 + len(parts)),
        out_specs=[VMEM] * QUAD,
        compiler_params=params(48),
        cost_estimate=cost(1 << 24, 3 << 20),
        name="finish",
    )(own, own_lse, *parts)


def emit_kernel(*refs):
    msgs, (att_ref, dev_ref) = refs[:-2], refs[-2:]
    mine = lax.rem(lax.axis_index("sample"), QUAD)
    rows = att_ref.shape[0]
    for h in range(HPD):
        for k in range(QUAD):
            msg = msgs[h * QUAD + k]
            head = jnp.bitwise_xor(mine, k) * HPD + h
            for g in range(GROUP):
                dev = msg[g * rows:(g + 1) * rows]
                base = GROUP * rows
                pair = msg[base:].astype(F32)[g * 8:(g + 1) * 8]
                mean = pair + pltpu.roll(pair, 4, 0)
                att = dev.astype(F32).reshape(rows // 8, 8, HD) + mean[None]
                cols = lanes((head * GROUP + g) * HD, HD)
                att_ref[:, cols] = att.reshape(rows, HD).astype(BF16)
                dev_ref[:, cols] = dev


def emit(msgs):
    rows = (msgs[0].shape[0] - GROUP * 8) // GROUP
    shape = jax.ShapeDtypeStruct((rows, HEADS * HD), BF16)
    return pl.pallas_call(
        emit_kernel,
        out_shape=[shape] * 2,
        in_specs=[VMEM] * len(msgs),
        out_specs=[VMEM] * 2,
        compiler_params=params(32),
        cost_estimate=cost(1 << 20, 2 << 20),
        name="emit",
    )(*msgs)


def shards(prompt_kv, prompt_blocks, slot_prompt, queries, new_kv):
    nsample = lax.axis_size("sample")
    quads = nsample // QUAD
    samples, steps, width = queries.shape
    rows = samples * steps

    def across(array, k):
        return lax.ppermute(array, "sample", [(i, i ^ k) for i in range(nsample)])

    def along(array, shift):
        return lax.ppermute(
            array, "sample", [(i, (i + shift * QUAD) % nsample) for i in range(nsample)]
        )

    kv3 = prompt_kv.reshape(prompt_kv.shape[0], BLK, prompt_kv.shape[-1])
    kv2 = kv3.reshape(-1, kv3.shape[-1])
    msgs = pack_queries(queries.reshape(rows, width), new_kv.reshape(rows, new_kv.shape[-1]))
    msgs = [msgs[0]] + [across(msgs[k], k) for k in range(1, QUAD)]
    cut = pack_kv(kv2)
    arrived = [
        [
            across(cut[h * (QUAD - 1) + k - 1], k).reshape(kv3.shape[0], BLK, 2 * HD)
            for k in range(1, QUAD)
        ]
        for h in range(HPD)
    ]
    final = []
    for h in range(HPD):
        own = jnp.stack([m[h, :GROUP * rows] for m in msgs])
        ahead = (quads - 1 + (1 - h % 2)) // 2
        held = {}
        block = own
        for s in range(1, ahead + 1):
            block = along(block, -1)
            held[s] = block
        block = own
        for s in range(1, quads - ahead):
            block = along(block, 1)
            held[quads - s] = block
        offsets = tuple(sorted(held))
        partial = attend(
            h, offsets, 0, prompt_blocks, slot_prompt, kv3, arrived[h], [held[o] for o in offsets]
        )
        back = [along(p, o) for o, p in zip(offsets, partial)]
        mine, mine_lse = attend(
            h, (0,), steps, prompt_blocks, slot_prompt, kv3, arrived[h], msgs
        )
        done = finish(steps, mine, mine_lse, back)
        final.append([done[0]] + [across(done[k], k) for k in range(1, QUAD)])
    attention, deviation = emit([m for per_head in final for m in per_head])
    return attention.reshape(queries.shape), deviation.reshape(queries.shape)


def solution(mesh):
    placed = (
        P("groups", "sample", None, None),
        P("groups"),
        P("groups"),
        P(("groups", "sample"), None, None),
        P(("groups", "sample"), None, None),
    )
    return jax.shard_map(
        shards,
        mesh=mesh,
        in_specs=placed,
        out_specs=(P(("groups", "sample"), None, None), P(("groups", "sample"), None, None)),
        check_vma=False,
    )
```

```python
import functools
import math

import jax
import jax.numpy as jnp
from jax import lax
from jax.experimental import pallas as pl
from jax.experimental.pallas import tpu as pltpu
from jax.sharding import PartitionSpec as P

HEADS = 64
KVH = 8
HD = 128
BLK = 32
QUAD = 4
HPD = KVH // QUAD
GROUP = HEADS // KVH
TILE_BLOCKS = 8
TILE = TILE_BLOCKS * BLK
STAT_ROWS = 16
NEG = -1e30
LOG2E = math.log2(math.e)
EXP_SCALE = LOG2E / math.sqrt(HD)
F32 = jnp.float32
BF16 = jnp.bfloat16
ANY = pl.BlockSpec(memory_space=pl.ANY)
VMEM = pl.BlockSpec(memory_space=pltpu.VMEM)
SMEM = pl.BlockSpec(memory_space=pltpu.SMEM)


def params(mib):
    return pltpu.CompilerParams(vmem_limit_bytes=mib << 20)


def cost(flops, nbytes, trans=0):
    return pl.CostEstimate(flops=flops, bytes_accessed=nbytes, transcendentals=trans)


def pack_queries_kernel(q_ref, new_ref, out):
    rows = q_ref.shape[0] * q_ref.shape[1]

    def column(ref, head):
        return ref[:, :, head * HD:(head + 1) * HD].astype(F32).reshape(rows, HD).astype(BF16)

    for p in range(QUAD):
        for h in range(HPD):
            head = p * HPD + h
            for g in range(GROUP):
                out[p, h, g * rows:(g + 1) * rows] = column(q_ref, head * GROUP + g)
            base = GROUP * rows
            out[p, h, base:base + rows] = column(new_ref, head)
            out[p, h, base + rows:base + 2 * rows] = column(new_ref, KVH + head)


def pack_queries(queries, new_kv):
    rows = queries.shape[0] * queries.shape[1]
    return pl.pallas_call(
        pack_queries_kernel,
        out_shape=jax.ShapeDtypeStruct((QUAD, HPD, (GROUP + 2) * rows, HD), BF16),
        in_specs=[VMEM, VMEM],
        out_specs=VMEM,
        compiler_params=params(32),
        cost_estimate=cost(0, 2 << 20),
        name="pack_queries",
    )(queries, new_kv)


def pack_kv_kernel(kv_ref, *refs):
    outs, sem = refs[:-1], refs[-1]
    copies = []
    for h in range(HPD):
        for p in range(QUAD):
            for part in range(2):
                first = (part * KVH + p * HPD + h) * HD
                copies.append(
                    pltpu.make_async_copy(
                        kv_ref.at[:, first:first + HD],
                        outs[h].at[p, :, part * HD:(part + 1) * HD],
                        sem.at[len(copies)],
                    )
                )
    for copy in copies:
        copy.start()
    for copy in copies:
        copy.wait()


def pack_kv(kv2):
    return pl.pallas_call(
        pack_kv_kernel,
        out_shape=[jax.ShapeDtypeStruct((QUAD, kv2.shape[0], 2 * HD), BF16)] * HPD,
        in_specs=[ANY],
        out_specs=[ANY] * HPD,
        scratch_shapes=[pltpu.SemaphoreType.DMA((2 * QUAD * HPD,))],
        compiler_params=params(56),
        cost_estimate=cost(0, 8 << 20),
        name="pack_kv",
    )(kv2)


def scores_of(keys, query):
    return lax.dot_general(keys, query, (((1,), (1,)), ((), ())), preferred_element_type=F32)


def values_by(values, weights):
    return lax.dot_general(values, weights, (((0,), (0,)), ((), ())), preferred_element_type=F32)


def attend_kernel(h, steps, counts_ref, slots_ref, kv_ref, fresh_ref, q_ref, out_ref, held, sem):
    nsample = lax.axis_size("sample")
    quads = nsample // QUAD
    quad = lax.div(lax.axis_index("sample"), QUAD)
    blocks = kv_ref.shape[1]
    size = q_ref.shape[2]
    rows = size // GROUP

    copies = [
        pltpu.make_async_copy(kv_ref.at[b], held.at[0:blocks, b], sem.at[b]) for b in range(QUAD)
    ]
    for copy in copies:
        copy.start()
    held[blocks:] = jnp.zeros_like(held[blocks:])
    for copy in copies:
        copy.wait()
    flat = held.reshape(held.shape[0] * QUAD * BLK, 2 * HD)

    def local_count(block):
        inside = jnp.clip(lax.rem(block, nsample) - QUAD * quad, 0, QUAD)
        return QUAD * lax.div(block, nsample) + inside

    def over_prompt(home, pair, query, state):
        prompt = slots_ref[QUAD * home + 2 * pair]
        start = lax.fori_loop(0, prompt, lambda p, total: total + counts_ref[p], jnp.int32(0))
        low, high = local_count(start), local_count(start + counts_ref[prompt])

        def body(t, carry):
            m, l, acc = carry
            first = low + t * TILE_BLOCKS
            row = pl.multiple_of(first * BLK, BLK)
            s = scores_of(flat[pl.ds(row, TILE), 0:HD], query)
            token = lax.broadcasted_iota(jnp.int32, s.shape, 0)
            s = jnp.where(token < (high - first) * BLK, s, NEG)
            m_new = jnp.maximum(m, jnp.max(s, axis=0, keepdims=True))
            p = jnp.exp2((s - m_new) * EXP_SCALE)
            alpha = jnp.exp2((m - m_new) * EXP_SCALE)
            l = l * alpha + jnp.sum(p, axis=0, keepdims=True)
            v = flat[pl.ds(row, TILE), HD:2 * HD]
            return m_new, l, acc * alpha + values_by(v, p.astype(BF16))

        tiles = lax.div(high - low + TILE_BLOCKS - 1, TILE_BLOCKS)
        m, l, acc = lax.fori_loop(0, tiles, body, state)
        some = l > 0.0
        safe = jnp.where(some, l, 1.0)
        lse = jnp.where(some, m * EXP_SCALE + jnp.log(safe) * LOG2E, NEG)
        coarse = lse.astype(BF16).astype(F32)
        middle = (lse - coarse).astype(BF16).astype(F32)
        rest = lse - coarse - middle
        index = lax.broadcasted_iota(jnp.int32, (STAT_ROWS, lse.shape[1]), 0)
        stats = jnp.where(index == 0, coarse, jnp.where(index == 1, middle, jnp.where(index == 2, rest, 0.0)))
        out_ref[home, pair, 0:HD] = (acc * (1.0 / safe)).astype(BF16)
        out_ref[home, pair, HD:] = stats.astype(BF16)

    def others(s, _):
        home = lax.rem(quad + s, quads)
        for pair in range(2):
            query = jnp.concatenate([q_ref[home, 2 * pair], q_ref[home, 2 * pair + 1]], axis=0)
            wide = query.shape[0]
            empty = (
                jnp.full((1, wide), NEG, F32),
                jnp.zeros((1, wide), F32),
                jnp.zeros((HD, wide), F32),
            )
            over_prompt(home, pair, query, empty)
        return 0

    lax.fori_loop(1, quads, others, 0)
    for pair in range(2):
        states, parts = [], []
        for half in range(2):
            msg = fresh_ref.at[2 * pair + half, h]
            query = msg[0:size]
            new_k, new_v = msg[size:size + rows], msg[size + rows:]
            s = scores_of(new_k, query)
            key = lax.broadcasted_iota(jnp.int32, s.shape, 0)
            row = lax.broadcasted_iota(jnp.int32, s.shape, 1) & (rows - 1)
            shift = steps.bit_length() - 1
            seen = ((row >> shift) == (key >> shift)) & ((row & (steps - 1)) >= (key & (steps - 1)))
            s = jnp.where(seen, s, NEG)
            m = jnp.max(s, axis=0, keepdims=True)
            p = jnp.exp2((s - m) * EXP_SCALE)
            l = jnp.sum(p, axis=0, keepdims=True)
            states.append((m, l, values_by(new_v, p.astype(BF16))))
            parts.append(query)
        state = tuple(jnp.concatenate(x, axis=1) for x in zip(*states))
        over_prompt(quad, pair, jnp.concatenate(parts, axis=0), state)


def attend(h, steps, counts, slots, arrived, fresh, queries):
    quads, _, size, _ = queries.shape
    blocks = arrived.shape[1]
    work = quads * 4 * size * blocks * BLK // 2
    return pl.pallas_call(
        functools.partial(attend_kernel, h, steps),
        out_shape=jax.ShapeDtypeStruct((quads, 2, HD + STAT_ROWS, 2 * size), BF16),
        in_specs=[SMEM, SMEM, ANY, VMEM, VMEM],
        out_specs=VMEM,
        scratch_shapes=[
            pltpu.VMEM((blocks + 2, QUAD, BLK, 2 * HD), BF16),
            pltpu.SemaphoreType.DMA((QUAD,)),
        ],
        compiler_params=params(48),
        cost_estimate=cost(4 * work * HD, 4 << 20, work),
        name="attend",
    )(counts, slots, arrived, fresh, queries)


def finish_kernel(steps, part_ref, out_ref):
    quads, _, _, size = part_ref.shape
    rows = size // (2 * GROUP)
    for pair in range(2):
        def lse_of(i):
            tail = part_ref[i, pair, HD:HD + STAT_ROWS].astype(F32)
            return tail[0:1] + tail[1:2] + tail[2:3]

        top = lax.fori_loop(1, quads, lambda i, t: jnp.maximum(t, lse_of(i)), lse_of(0))

        def add(i, carry):
            total, weight = carry
            w = jnp.exp2(lse_of(i) - top)
            return total + part_ref[i, pair, 0:HD].astype(F32) * w, weight + w

        total, weight = lax.fori_loop(
            0, quads, add, (jnp.zeros((HD, size), F32), jnp.zeros((1, size), F32))
        )
        full = (total * (1.0 / weight)).T
        wide = full.reshape(2, GROUP, rows // 8, 8, HD)
        mean = jnp.sum(wide, axis=(0, 2)) * (steps / (2.0 * rows))
        flat = mean.reshape(GROUP * 8, HD)
        place = lax.broadcasted_iota(jnp.int32, flat.shape, 0) & 7
        if steps == 4:
            up, down = pltpu.roll(flat, 4, 0), pltpu.roll(flat, GROUP * 8 - 4, 0)
            flat = flat + jnp.where(place < 4, down, up)
        dev = wide - flat.reshape(GROUP, 8, HD)[None, :, None]
        coarse = flat.astype(BF16).astype(F32)
        carried = jnp.where(place < 4, coarse, flat - coarse).astype(BF16)
        dev = dev.reshape(2, size // 2, HD).astype(BF16)
        for half in range(2):
            out_ref[2 * pair + half, 0:size // 2] = dev[half]
            out_ref[2 * pair + half, size // 2:] = carried


def finish(steps, parts):
    size = parts.shape[-1]
    return pl.pallas_call(
        functools.partial(finish_kernel, steps),
        out_shape=jax.ShapeDtypeStruct((QUAD, size // 2 + GROUP * 8, HD), BF16),
        in_specs=[VMEM],
        out_specs=VMEM,
        compiler_params=params(48),
        cost_estimate=cost(1 << 24, 3 << 20),
        name="finish",
    )(parts)


def emit_kernel(*refs):
    msgs, (att_ref, dev_ref) = refs[:-2], refs[-2:]
    samples, steps, _ = att_ref.shape
    rows = samples * steps
    for h in range(HPD):
        for p in range(QUAD):
            msg = msgs[h].at[p]
            head = p * HPD + h
            means = msg[GROUP * rows:].astype(F32)
            for g in range(GROUP):
                dev = msg[g * rows:(g + 1) * rows].astype(F32)
                pair = means[g * 8:(g + 1) * 8]
                mean = pair + pltpu.roll(pair, 4, 0)
                att = (dev.reshape(rows // 8, 8, HD) + mean[None]).reshape(samples, steps, HD)
                first = (head * GROUP + g) * HD
                att_ref[:, :, first:first + HD] = att.astype(BF16)
                dev_ref[:, :, first:first + HD] = dev.reshape(samples, steps, HD).astype(BF16)


def emit(msgs, shape):
    return pl.pallas_call(
        emit_kernel,
        out_shape=[jax.ShapeDtypeStruct(shape, BF16)] * 2,
        in_specs=[VMEM] * len(msgs),
        out_specs=[VMEM] * 2,
        compiler_params=params(32),
        cost_estimate=cost(1 << 20, 2 << 20),
        name="emit",
    )(*msgs)


def shards(prompt_kv, prompt_blocks, slot_prompt, queries, new_kv):
    nsample = lax.axis_size("sample")
    quads = nsample // QUAD
    samples, steps, width = queries.shape
    rows = samples * steps
    same_quad = [[q * QUAD + j for j in range(QUAD)] for q in range(quads)]
    same_heads = [[q * QUAD + j for q in range(quads)] for j in range(QUAD)]

    def inside(array):
        return lax.all_to_all(array, "sample", 0, 0, axis_index_groups=same_quad, tiled=True)

    def along(array):
        return lax.all_to_all(array, "sample", 0, 0, axis_index_groups=same_heads, tiled=True)

    def gathered(array):
        return lax.all_gather(array, "sample", axis_index_groups=same_heads)

    kv2 = prompt_kv.reshape(-1, prompt_kv.shape[-1])
    fresh = inside(pack_queries(queries, new_kv))
    cut = pack_kv(kv2)
    final = []
    for h in range(HPD):
        asked = gathered(fresh[:, h, :GROUP * rows])
        arrived = inside(cut[h]).reshape(QUAD, -1, BLK, 2 * HD)
        partial = attend(h, steps, prompt_blocks, slot_prompt, arrived, fresh, asked)
        final.append(inside(finish(steps, along(partial))))
    return tuple(emit(final, queries.shape))


def solution(mesh):
    placed = (
        P("groups", "sample", None, None),
        P("groups"),
        P("groups"),
        P(("groups", "sample"), None, None),
        P(("groups", "sample"), None, None),
    )
    return jax.shard_map(
        shards,
        mesh=mesh,
        in_specs=placed,
        out_specs=(P(("groups", "sample"), None, None), P(("groups", "sample"), None, None)),
        check_vma=False,
    )
```

```python
import functools
import math

import jax
import jax.numpy as jnp
from jax import lax
from jax.experimental import pallas as pl
from jax.experimental.pallas import tpu as pltpu
from jax.sharding import PartitionSpec as P

HEADS = 64
KVH = 8
HD = 128
BLK = 32
QUAD = 4
HPD = KVH // QUAD
GROUP = HEADS // KVH
TILE_BLOCKS = 8
TILE = TILE_BLOCKS * BLK
STAT_ROWS = 16
NEG = -1e30
LOG2E = math.log2(math.e)
EXP_SCALE = LOG2E / math.sqrt(HD)
F32 = jnp.float32
BF16 = jnp.bfloat16
ANY = pl.BlockSpec(memory_space=pl.ANY)
VMEM = pl.BlockSpec(memory_space=pltpu.VMEM)
SMEM = pl.BlockSpec(memory_space=pltpu.SMEM)


def lanes(start, size):
    return pl.ds(pl.multiple_of(start, 128), size)


def params(mib):
    return pltpu.CompilerParams(vmem_limit_bytes=mib << 20)


def cost(flops, nbytes, trans=0):
    return pl.CostEstimate(flops=flops, bytes_accessed=nbytes, transcendentals=trans)


def pack_queries_kernel(q_hbm, new_hbm, *refs):
    outs, (q_ref, new_ref, sem) = refs[:-3], refs[-3:]
    copies = [
        pltpu.make_async_copy(q_hbm, q_ref, sem.at[0]),
        pltpu.make_async_copy(new_hbm, new_ref, sem.at[1]),
    ]
    for copy in copies:
        copy.start()
    for copy in copies:
        copy.wait()
    mine = lax.rem(lax.axis_index("sample"), QUAD)
    rows = q_ref.shape[0] * q_ref.shape[1]

    def column(ref, head):
        return ref[:, :, lanes(head * HD, HD)].astype(F32).reshape(rows, HD).astype(BF16)

    for k in range(QUAD):
        for h in range(HPD):
            head = jnp.bitwise_xor(mine, k) * HPD + h
            for g in range(GROUP):
                outs[k][h, g * rows:(g + 1) * rows] = column(q_ref, head * GROUP + g)
            base = GROUP * rows
            outs[k][h, base:base + rows] = column(new_ref, head)
            outs[k][h, base + rows:base + 2 * rows] = column(new_ref, KVH + head)


def pack_queries(queries, new_kv):
    rows = queries.shape[0] * queries.shape[1]
    return pl.pallas_call(
        pack_queries_kernel,
        out_shape=[jax.ShapeDtypeStruct((HPD, (GROUP + 2) * rows, HD), BF16)] * QUAD,
        in_specs=[ANY, ANY],
        out_specs=[VMEM] * QUAD,
        scratch_shapes=[
            pltpu.VMEM(queries.shape, BF16),
            pltpu.VMEM(new_kv.shape, BF16),
            pltpu.SemaphoreType.DMA((2,)),
        ],
        compiler_params=params(56),
        cost_estimate=cost(0, 2 << 20),
        name="pack_queries",
    )(queries, new_kv)


def pack_kv_kernel(kv_ref, *refs):
    near, far, sem = refs[0], refs[1:-1], refs[-1]
    mine = lax.rem(lax.axis_index("sample"), QUAD)
    copies = []
    for h in range(HPD):
        for k in range(1, QUAD):
            head = jnp.bitwise_xor(mine, k) * HPD + h
            out = near.at[h] if k == 1 else far[h * (QUAD - 2) + k - 2]
            for part in range(2):
                copies.append(
                    pltpu.make_async_copy(
                        kv_ref.at[:, lanes((part * KVH + head) * HD, HD)],
                        out.at[:, part * HD:(part + 1) * HD],
                        sem.at[len(copies)],
                    )
                )
    for copy in copies:
        copy.start()
    for copy in copies:
        copy.wait()


def pack_kv(kv2):
    count = HPD * (QUAD - 2)
    tokens = kv2.shape[0]
    return pl.pallas_call(
        pack_kv_kernel,
        out_shape=[jax.ShapeDtypeStruct((HPD, tokens, 2 * HD), BF16)]
        + [jax.ShapeDtypeStruct((tokens, 2 * HD), BF16)] * count,
        in_specs=[ANY],
        out_specs=[ANY] * (count + 1),
        scratch_shapes=[pltpu.SemaphoreType.DMA((2 * HPD * (QUAD - 1),))],
        compiler_params=params(16),
        cost_estimate=cost(0, 6 << 20),
        name="pack_kv",
    )(kv2)


def scores_of(keys, query):
    return lax.dot_general(keys, query, (((1,), (1,)), ((), ())), preferred_element_type=F32)


def values_by(values, weights):
    return lax.dot_general(values, weights, (((0,), (0,)), ((), ())), preferred_element_type=F32)


def attend_kernel(h, offsets, steps, counts_ref, slots_ref, kv_ref, near, *refs):
    far, refs = refs[:QUAD - 2], refs[QUAD - 2:]
    nq = QUAD if steps else len(offsets)
    queries, refs = refs[:nq], refs[nq:]
    outs, (held, sem) = refs[:-2], refs[-2:]
    nsample = lax.axis_size("sample")
    quads = nsample // QUAD
    index = lax.axis_index("sample")
    quad, mine = lax.div(index, QUAD), lax.rem(index, QUAD)
    blocks = kv_ref.shape[0]

    copies = []
    for part in range(2):
        copies.append(
            pltpu.make_async_copy(
                kv_ref.at[:, :, lanes((part * KVH + mine * HPD + h) * HD, HD)],
                held.at[0:blocks, mine, :, part * HD:(part + 1) * HD],
                sem.at[part],
            )
        )
    for k in range(1, QUAD):
        source = near.at[h] if k == 1 else far[k - 2]
        copies.append(
            pltpu.make_async_copy(source, held.at[0:blocks, jnp.bitwise_xor(mine, k)], sem.at[k + 1])
        )
    for copy in copies:
        copy.start()
    held[blocks:] = jnp.zeros_like(held[blocks:])

    def fresh_state(pair):
        states, parts = [], []
        for half in range(2):
            msg = queries[2 * pair + half].at[h]
            rows = msg.shape[0] // (GROUP + 2)
            size = rows * GROUP
            query = msg[0:size]
            s = scores_of(msg[size:size + rows], query)
            key = lax.broadcasted_iota(jnp.int32, s.shape, 0)
            row = lax.broadcasted_iota(jnp.int32, s.shape, 1) & (rows - 1)
            shift = steps.bit_length() - 1
            seen = ((row >> shift) == (key >> shift)) & ((row & (steps - 1)) >= (key & (steps - 1)))
            s = jnp.where(seen, s, NEG)
            m = jnp.max(s, axis=0, keepdims=True)
            p = jnp.exp2((s - m) * EXP_SCALE)
            l = jnp.sum(p, axis=0, keepdims=True)
            states.append((m, l, values_by(msg[size + rows:], p.astype(BF16))))
            parts.append(query)
        return jnp.concatenate(parts, axis=0), tuple(jnp.concatenate(x, axis=1) for x in zip(*states))

    begun = [fresh_state(pair) for pair in range(2)] if steps else None
    for copy in copies:
        copy.wait()
    flat = held.reshape(held.shape[0] * QUAD * BLK, 2 * HD)

    def local_count(block):
        inside = jnp.clip(lax.rem(block, nsample) - QUAD * quad, 0, QUAD)
        return QUAD * lax.div(block, nsample) + inside

    def over_prompt(home, pair, query, state):
        prompt = slots_ref[QUAD * home + 2 * jnp.bitwise_xor(lax.div(mine, 2), pair)]
        start = lax.fori_loop(0, prompt, lambda p, total: total + counts_ref[p], jnp.int32(0))
        low, high = local_count(start), local_count(start + counts_ref[prompt])

        def body(t, carry):
            m, l, acc = carry
            first = low + t * TILE_BLOCKS
            row = pl.multiple_of(first * BLK, BLK)
            s = scores_of(flat[pl.ds(row, TILE), 0:HD], query)
            token = lax.broadcasted_iota(jnp.int32, s.shape, 0)
            s = jnp.where(token < (high - first) * BLK, s, NEG)
            m_new = jnp.maximum(m, jnp.max(s, axis=0, keepdims=True))
            p = jnp.exp2((s - m_new) * EXP_SCALE)
            alpha = jnp.exp2((m - m_new) * EXP_SCALE)
            l = l * alpha + jnp.sum(p, axis=0, keepdims=True)
            v = flat[pl.ds(row, TILE), HD:2 * HD]
            return m_new, l, acc * alpha + values_by(v, p.astype(BF16))

        tiles = lax.div(high - low + TILE_BLOCKS - 1, TILE_BLOCKS)
        m, l, acc = lax.fori_loop(0, tiles, body, state)
        some = l > 0.0
        safe = jnp.where(some, l, 1.0)
        lse = jnp.where(some, m * EXP_SCALE + jnp.log(safe) * LOG2E, NEG)
        return acc * (1.0 / safe), lse

    for n, offset in enumerate(offsets):
        home = lax.rem(quad + offset, quads)
        for pair in range(2):
            if steps:
                query, state = begun[pair]
                out, lse = over_prompt(home, pair, query, state)
                outs[0][pair] = out
                outs[1][pair] = jnp.broadcast_to(lse, (8, lse.shape[1]))
                continue
            query = jnp.concatenate([queries[n][2 * pair], queries[n][2 * pair + 1]], axis=0)
            wide = query.shape[0]
            empty = (
                jnp.full((1, wide), NEG, F32),
                jnp.zeros((1, wide), F32),
                jnp.zeros((HD, wide), F32),
            )
            out, lse = over_prompt(home, pair, query, empty)
            coarse = lse.astype(BF16).astype(F32)
            middle = (lse - coarse).astype(BF16).astype(F32)
            rest = lse - coarse - middle
            place = lax.broadcasted_iota(jnp.int32, (STAT_ROWS, wide), 0)
            stats = jnp.where(place == 1, middle, jnp.where(place == 2, rest, 0.0))
            outs[n][pair, 0:HD] = out.astype(BF16)
            outs[n][pair, HD:] = jnp.where(place == 0, coarse, stats).astype(BF16)


def attend(h, offsets, steps, counts, slots, kv3, arrived, queries):
    if steps:
        size = queries[0].shape[1] * GROUP // (GROUP + 2)
        out_shape = [
            jax.ShapeDtypeStruct((2, HD, 2 * size), F32),
            jax.ShapeDtypeStruct((2, 8, 2 * size), F32),
        ]
    else:
        size = queries[0].shape[1]
        out_shape = [jax.ShapeDtypeStruct((2, HD + STAT_ROWS, 2 * size), BF16)] * len(offsets)
    blocks = kv3.shape[0]
    work = len(offsets) * 2 * size * blocks * BLK
    return pl.pallas_call(
        functools.partial(attend_kernel, h, offsets, steps),
        out_shape=out_shape,
        in_specs=[SMEM, SMEM, ANY] + [ANY] * len(arrived) + [VMEM] * len(queries),
        out_specs=[VMEM] * len(out_shape),
        scratch_shapes=[
            pltpu.VMEM((blocks + 2, QUAD, BLK, 2 * HD), BF16),
            pltpu.SemaphoreType.DMA((QUAD + 1,)),
        ],
        compiler_params=params(48),
        cost_estimate=cost(4 * work * HD, 4 << 20, work),
        name="attend_own" if steps else "attend_others",
    )(counts, slots, kv3, *arrived, *queries)


def finish_kernel(steps, own_ref, own_lse_ref, *refs):
    parts, outs = refs[:-QUAD], refs[-QUAD:]
    size = own_ref.shape[2]
    rows = size // (2 * GROUP)
    for pair in range(2):
        lses = [own_lse_ref[pair, 0:1]]
        for ref in parts:
            tail = ref[pair, HD:HD + STAT_ROWS].astype(F32)
            lses.append(tail[0:1] + tail[1:2] + tail[2:3])
        top = functools.reduce(jnp.maximum, lses)
        shares = [jnp.exp2(lse - top) for lse in lses]
        scale = 1.0 / functools.reduce(jnp.add, shares)
        total = own_ref[pair] * (shares[0] * scale)
        for ref, share in zip(parts, shares[1:]):
            total = total + ref[pair, 0:HD].astype(F32) * (share * scale)
        wide = total.T.reshape(2, GROUP, rows // 8, 8, HD)
        mean = jnp.sum(wide, axis=(0, 2)) * (steps / (2.0 * rows))
        flat = mean.reshape(GROUP * 8, HD)
        place = lax.broadcasted_iota(jnp.int32, flat.shape, 0) & 7
        up, down = pltpu.roll(flat, 4, 0), pltpu.roll(flat, GROUP * 8 - 4, 0)
        flat = flat + jnp.where(place < 4, down, up)
        dev = wide - flat.reshape(GROUP, 8, HD)[None, :, None]
        coarse = flat.astype(BF16).astype(F32)
        carried = jnp.where(place < 4, coarse, flat - coarse).astype(BF16)
        dev = dev.reshape(2, size // 2, HD).astype(BF16)
        for half in range(2):
            out = outs[2 * pair + half]
            out[0:size // 2] = dev[half]
            out[size // 2:] = carried


def finish(steps, own, own_lse, parts):
    size = own.shape[2]
    return pl.pallas_call(
        functools.partial(finish_kernel, steps),
        out_shape=[jax.ShapeDtypeStruct((size // 2 + GROUP * 8, HD), BF16)] * QUAD,
        in_specs=[VMEM] * (2 + len(parts)),
        out_specs=[VMEM] * QUAD,
        compiler_params=params(48),
        cost_estimate=cost(1 << 24, 3 << 20),
        name="finish",
    )(own, own_lse, *parts)


def emit_kernel(*refs):
    msgs, (att_ref, dev_ref) = refs[:-2], refs[-2:]
    samples, steps, _ = att_ref.shape
    rows = samples * steps
    mine = lax.rem(lax.axis_index("sample"), QUAD)
    for h in range(HPD):
        for k in range(QUAD):
            msg = msgs[h * QUAD + k]
            head = jnp.bitwise_xor(mine, k) * HPD + h
            means = msg[GROUP * rows:].astype(F32)
            for g in range(GROUP):
                dev = msg[g * rows:(g + 1) * rows].astype(F32)
                pair = means[g * 8:(g + 1) * 8]
                mean = pair + pltpu.roll(pair, 4, 0)
                att = (dev.reshape(rows // 8, 8, HD) + mean[None]).reshape(samples, steps, HD)
                cols = lanes((head * GROUP + g) * HD, HD)
                att_ref[:, :, cols] = att.astype(BF16)
                dev_ref[:, :, cols] = dev.reshape(samples, steps, HD).astype(BF16)


def emit(msgs, shape):
    return pl.pallas_call(
        emit_kernel,
        out_shape=[jax.ShapeDtypeStruct(shape, BF16)] * 2,
        in_specs=[VMEM] * len(msgs),
        out_specs=[VMEM] * 2,
        compiler_params=params(32),
        cost_estimate=cost(1 << 20, 2 << 20),
        name="emit",
    )(*msgs)


def shards(prompt_kv, prompt_blocks, slot_prompt, queries, new_kv):
    nsample = lax.axis_size("sample")
    quads = nsample // QUAD
    samples, steps, width = queries.shape
    rows = samples * steps

    def across(array, k):
        return lax.ppermute(array, "sample", [(i, i ^ k) for i in range(nsample)])

    def along(array, shift):
        return lax.ppermute(
            array, "sample", [(i, (i + shift * QUAD) % nsample) for i in range(nsample)]
        )

    kv3 = prompt_kv.reshape(prompt_kv.shape[0], BLK, prompt_kv.shape[-1])
    msgs = pack_queries(queries, new_kv)
    near, *far = pack_kv(kv3.reshape(-1, kv3.shape[-1]))
    msgs = [msgs[0]] + [across(msgs[k], k) for k in range(1, QUAD)]
    near, msgs = lax.optimization_barrier((near, msgs))
    near = across(near, 1).reshape(HPD, -1, BLK, 2 * HD)
    far = [
        across(block, 2 + i % (QUAD - 2)).reshape(-1, BLK, 2 * HD) for i, block in enumerate(far)
    ]
    final = []
    for h in range(HPD):
        arrived = [near] + far[h * (QUAD - 2):(h + 1) * (QUAD - 2)]
        own = jnp.stack([m[h, :GROUP * rows] for m in msgs])
        ahead = (quads - 1 + (1 - h % 2)) // 2
        held = {}
        block = own
        for s in range(1, ahead + 1):
            block = along(block, -1)
            held[s] = block
        block = own
        for s in range(1, quads - ahead):
            block = along(block, 1)
            held[quads - s] = block
        offsets = tuple(sorted(held))
        partial = attend(
            h, offsets, 0, prompt_blocks, slot_prompt, kv3, arrived, [held[o] for o in offsets]
        )
        back = [along(p, o) for o, p in zip(offsets, partial)]
        mine = attend(h, (0,), steps, prompt_blocks, slot_prompt, kv3, arrived, msgs)
        done = finish(steps, *mine, back)
        final.append([done[0]] + [across(done[k], k) for k in range(1, QUAD)])
    return tuple(emit([m for per_head in final for m in per_head], queries.shape))


def solution(mesh):
    placed = (
        P("groups", "sample", None, None),
        P("groups"),
        P("groups"),
        P(("groups", "sample"), None, None),
        P(("groups", "sample"), None, None),
    )
    return jax.shard_map(
        shards,
        mesh=mesh,
        in_specs=placed,
        out_specs=(P(("groups", "sample"), None, None), P(("groups", "sample"), None, None)),
        check_vma=False,
    )
```

```python
import functools
import math

import jax
import jax.numpy as jnp
from jax import lax
from jax.experimental import pallas as pl
from jax.experimental.pallas import tpu as pltpu
from jax.sharding import PartitionSpec as P

HEADS = 64
KVH = 8
HD = 128
BLK = 32
MAXB = 128
QUAD = 4
HPD = KVH // QUAD
GROUP = HEADS // KVH
TILE_BLOCKS = 8
TILE = TILE_BLOCKS * BLK
STAT_ROWS = 16
NEG = -1e30
LOG2E = math.log2(math.e)
EXP_SCALE = LOG2E / math.sqrt(HD)
F32 = jnp.float32
BF16 = jnp.bfloat16
ANY = pl.BlockSpec(memory_space=pl.ANY)
VMEM = pl.BlockSpec(memory_space=pltpu.VMEM)
SMEM = pl.BlockSpec(memory_space=pltpu.SMEM)


def lanes(start, size):
    return pl.ds(pl.multiple_of(start, 128), size)


def params(mib):
    return pltpu.CompilerParams(vmem_limit_bytes=mib << 20)


def cost(flops, nbytes, trans=0):
    return pl.CostEstimate(flops=flops, bytes_accessed=nbytes, transcendentals=trans)


def pack_queries_kernel(q_hbm, new_hbm, *refs):
    outs, (q_ref, new_ref, sem) = refs[:-3], refs[-3:]
    copies = [
        pltpu.make_async_copy(q_hbm, q_ref, sem.at[0]),
        pltpu.make_async_copy(new_hbm, new_ref, sem.at[1]),
    ]
    for copy in copies:
        copy.start()
    for copy in copies:
        copy.wait()
    mine = lax.rem(lax.axis_index("sample"), QUAD)
    rows = q_ref.shape[0] * q_ref.shape[1]

    def column(ref, head):
        return ref[:, :, lanes(head * HD, HD)].astype(F32).reshape(rows, HD).astype(BF16)

    for k in range(QUAD):
        for h in range(HPD):
            head = jnp.bitwise_xor(mine, k) * HPD + h
            for g in range(GROUP):
                outs[k][h, g * rows:(g + 1) * rows] = column(q_ref, head * GROUP + g)
            base = GROUP * rows
            outs[k][h, base:base + rows] = column(new_ref, head)
            outs[k][h, base + rows:base + 2 * rows] = column(new_ref, KVH + head)


def pack_queries(queries, new_kv):
    rows = queries.shape[0] * queries.shape[1]
    return pl.pallas_call(
        pack_queries_kernel,
        out_shape=[jax.ShapeDtypeStruct((HPD, (GROUP + 2) * rows, HD), BF16)] * QUAD,
        in_specs=[ANY, ANY],
        out_specs=[VMEM] * QUAD,
        scratch_shapes=[
            pltpu.VMEM(queries.shape, BF16),
            pltpu.VMEM(new_kv.shape, BF16),
            pltpu.SemaphoreType.DMA((2,)),
        ],
        compiler_params=params(56),
        cost_estimate=cost(0, 2 << 20),
        name="pack_queries",
    )(queries, new_kv)


def pack_kv_kernel(kv_ref, near, *refs):
    far, sem = refs[:-1], refs[-1]
    mine = lax.rem(lax.axis_index("sample"), QUAD)
    copies = []
    for h in range(HPD):
        for k in range(1, QUAD):
            head = jnp.bitwise_xor(mine, k) * HPD + h
            out = near.at[h] if k == 1 else far[h].at[k - 2]
            for part in range(2):
                copies.append(
                    pltpu.make_async_copy(
                        kv_ref.at[:, lanes((part * KVH + head) * HD, HD)],
                        out.at[:, part * HD:(part + 1) * HD],
                        sem.at[len(copies)],
                    )
                )
    for copy in copies:
        copy.start()
    for copy in copies:
        copy.wait()


def pack_kv(kv2):
    shape = jax.ShapeDtypeStruct((2, kv2.shape[0], 2 * HD), BF16)
    return pl.pallas_call(
        pack_kv_kernel,
        out_shape=[shape] * (1 + HPD),
        in_specs=[ANY],
        out_specs=[ANY] * (1 + HPD),
        scratch_shapes=[pltpu.SemaphoreType.DMA((2 * HPD * (QUAD - 1),))],
        compiler_params=params(16),
        cost_estimate=cost(0, 6 << 20),
        name="pack_kv",
    )(kv2)


def scores_of(keys, query):
    return lax.dot_general(keys, query, (((1,), (1,)), ((), ())), preferred_element_type=F32)


def values_by(values, weights):
    return lax.dot_general(values, weights, (((0,), (0,)), ((), ())), preferred_element_type=F32)


def attend_kernel(h, offsets, steps, max_tiles, counts_ref, slots_ref, kv_ref, near, same, passed, *refs):
    count = len(offsets)
    nq = QUAD if steps else count
    queries, refs = refs[:nq], refs[nq:]
    nout = 2 if steps else count
    outs, refs = refs[:nout], refs[nout:]
    held, asked, fresh, state, acc, stage, sem = refs
    nsample = lax.axis_size("sample")
    quads = nsample // QUAD
    index = lax.axis_index("sample")
    quad, mine = lax.div(index, QUAD), lax.rem(index, QUAD)
    blocks = kv_ref.shape[0]
    size = asked.shape[2]

    first_copies = []

    def copied(copies, source, target):
        copies.append(pltpu.make_async_copy(source, target, sem.at[len(first_copies) + len(later)]))
        copies[-1].start()

    later = []
    for n in range(nq):
        if steps:
            copied(first_copies, queries[n].at[h, 0:size], asked.at[0, n])
            copied(first_copies, queries[n].at[h, size:], fresh.at[n])
        else:
            copied(first_copies, queries[n], asked.at[n])
    for part in range(2):
        copied(
            later,
            kv_ref.at[:, :, lanes((part * KVH + mine * HPD + h) * HD, HD)],
            held.at[0:blocks, mine, :, part * HD:(part + 1) * HD],
        )
    for k, source in ((1, near.at[h]), (2, same.at[0]), (3, passed)):
        copied(later, source, held.at[0:blocks, jnp.bitwise_xor(mine, k)])
    held[blocks:] = jnp.zeros_like(held[blocks:])
    for copy in first_copies:
        copy.wait()

    def fresh_state(pair):
        parts = []
        for half in range(2):
            slot = 2 * pair + half
            rows = size // GROUP
            s = scores_of(fresh[slot, 0:rows], asked[0, slot])
            key = lax.broadcasted_iota(jnp.int32, s.shape, 0)
            row = lax.broadcasted_iota(jnp.int32, s.shape, 1) & (rows - 1)
            shift = steps.bit_length() - 1
            seen = ((row >> shift) == (key >> shift)) & ((row & (steps - 1)) >= (key & (steps - 1)))
            s = jnp.where(seen, s, NEG)
            m = jnp.max(s, axis=0, keepdims=True)
            p = jnp.exp2((s - m) * EXP_SCALE)
            l = jnp.sum(p, axis=0, keepdims=True)
            parts.append((m, l, values_by(fresh[slot, rows:], p.astype(BF16))))
        m, l, out = (jnp.concatenate(x, axis=1) for x in zip(*parts))
        state[pair, 0:1] = m
        state[pair, 1:2] = l
        acc[pair] = out

    if steps:
        for pair in range(2):
            fresh_state(pair)
    for copy in later:
        copy.wait()
    flat = held.reshape(held.shape[0] * QUAD * BLK, 2 * HD)

    def local_count(block):
        inside = jnp.clip(lax.rem(block, nsample) - QUAD * quad, 0, QUAD)
        return QUAD * lax.div(block, nsample) + inside

    def one_pass(n, pair, low, high, tiles):
        tokens = tiles * TILE
        query = asked[n, pl.ds(2 * pair, 2)].reshape(2 * size, HD)
        row = pl.multiple_of(low * BLK, BLK)
        s = scores_of(flat[pl.ds(row, tokens), 0:HD], query)
        last = s[tokens - TILE:]
        token = lax.broadcasted_iota(jnp.int32, last.shape, 0)
        last = jnp.where(token < (high - low) * BLK - (tokens - TILE), last, NEG)
        s = last if tiles == 1 else jnp.concatenate([s[:tokens - TILE], last], axis=0)
        m = jnp.max(s, axis=0, keepdims=True)
        if steps:
            before = state[pair, 0:1]
            m = jnp.maximum(m, before)
        p = jnp.exp2((s - m) * EXP_SCALE)
        l = jnp.sum(p, axis=0, keepdims=True)
        out = values_by(flat[pl.ds(row, tokens), HD:2 * HD], p.astype(BF16))
        if steps:
            alpha = jnp.exp2((before - m) * EXP_SCALE)
            l = l + alpha * state[pair, 1:2]
            out = out + alpha * acc[pair]
        state[pair, 0:1] = m
        state[pair, 1:2] = l
        acc[pair] = out

    def chunk(n, _):
        offset = jnp.int32(0) if steps else offset_of(n)
        home = lax.rem(quad + offset, quads)

        def prompt_of(pair, _):
            prompt = slots_ref[QUAD * home + 2 * jnp.bitwise_xor(lax.div(mine, 2), pair)]
            start = lax.fori_loop(0, prompt, lambda p, total: total + counts_ref[p], jnp.int32(0))
            low, high = local_count(start), local_count(start + counts_ref[prompt])
            tiles = lax.div(high - low + TILE_BLOCKS - 1, TILE_BLOCKS)
            if not steps:
                @pl.when(tiles == 0)
                def _():
                    state[pair, 0:1] = jnp.full((1, 2 * size), NEG, F32)
                    state[pair, 1:2] = jnp.zeros((1, 2 * size), F32)
                    acc[pair] = jnp.zeros((HD, 2 * size), F32)

            for t in range(1, max_tiles + 1):
                @pl.when(tiles == t)
                def _(t=t):
                    one_pass(n, pair, low, high, t)

            return 0

        lax.fori_loop(0, 2, prompt_of, 0)
        lses = []
        for pair in range(2):
            m, l = state[pair, 0:1], state[pair, 1:2]
            some = l > 0.0
            safe = jnp.where(some, l, 1.0)
            lses.append(jnp.where(some, m * EXP_SCALE + jnp.log(safe) * LOG2E, NEG))
            out = acc[pair] * (1.0 / safe)
            if steps:
                outs[0][pair] = out
                outs[1][pair] = jnp.broadcast_to(lses[pair], (8, 2 * size))
            else:
                stage[n, pair * HD:(pair + 1) * HD] = out.astype(BF16)
        if not steps:
            stage[n, 2 * HD:] = stat_tile(lses)
        return 0

    def offset_of(n):
        offset = jnp.int32(offsets[0])
        for i in range(1, count):
            offset = jnp.where(n == i, offsets[i], offset)
        return offset

    lax.fori_loop(0, count, chunk, 0)
    if not steps:
        copies = []
        for n in range(count):
            copied(copies, stage.at[n], outs[n])
            later.append(copies[-1])
        for copy in copies:
            copy.wait()


def attend(h, offsets, steps, counts, slots, kv3, arrived, queries):
    count = len(offsets)
    if steps:
        size = queries[0].shape[1] * GROUP // (GROUP + 2)
        out_shape = [
            jax.ShapeDtypeStruct((2, HD, 2 * size), F32),
            jax.ShapeDtypeStruct((2, 8, 2 * size), F32),
        ]
    else:
        size = queries[0].shape[1]
        out_shape = [jax.ShapeDtypeStruct((2 * HD + STAT_ROWS, 2 * size), BF16)] * count
    blocks = kv3.shape[0]
    max_tiles = -(-(-(-MAXB // lax.axis_size("sample")) * QUAD) // TILE_BLOCKS)
    work = count * 2 * size * blocks * BLK
    return pl.pallas_call(
        functools.partial(attend_kernel, h, offsets, steps, max_tiles),
        out_shape=out_shape,
        in_specs=[SMEM, SMEM, ANY] + [ANY] * len(arrived) + [ANY] * len(queries),
        out_specs=[VMEM if steps else ANY] * len(out_shape),
        scratch_shapes=[
            pltpu.VMEM((blocks + max_tiles * TILE_BLOCKS // QUAD, QUAD, BLK, 2 * HD), BF16),
            pltpu.VMEM((count, QUAD, size, HD), BF16),
            pltpu.VMEM((QUAD, 2 * size // GROUP, HD), BF16),
            pltpu.VMEM((2, 8, 2 * size), F32),
            pltpu.VMEM((2, HD, 2 * size), F32),
            pltpu.VMEM((1 if steps else count, 2 * HD + STAT_ROWS, 2 * size), BF16),
            pltpu.SemaphoreType.DMA((2 * QUAD + 2 * count + 8,)),
        ],
        compiler_params=params(48),
        cost_estimate=cost(0, 1024),
        name="attend_own" if steps else "attend_others",
    )(counts, slots, kv3, *arrived, *queries)


def lse_of(ref, pair):
    tail = ref[2 * HD:2 * HD + STAT_ROWS].astype(F32)[3 * pair:3 * pair + 3]
    return tail[0:1] + tail[1:2] + tail[2:3]


def stat_tile(lses):
    place = lax.broadcasted_iota(jnp.int32, (STAT_ROWS, lses[0].shape[1]), 0)
    stats = jnp.zeros(place.shape, F32)
    for pair, lse in enumerate(lses):
        coarse = lse.astype(BF16).astype(F32)
        middle = (lse - coarse).astype(BF16).astype(F32)
        for i, piece in enumerate((coarse, middle, lse - coarse - middle)):
            stats = jnp.where(place == 3 * pair + i, piece, stats)
    return stats.astype(BF16)


def merge_kernel(one_ref, two_ref, out_ref):
    lses = []
    for pair in range(2):
        one, two = lse_of(one_ref, pair), lse_of(two_ref, pair)
        top = jnp.maximum(one, two)
        w1, w2 = jnp.exp2(one - top), jnp.exp2(two - top)
        total = w1 + w2
        scale = 1.0 / total
        rows = slice(pair * HD, (pair + 1) * HD)
        merged = one_ref[rows].astype(F32) * (w1 * scale) + two_ref[rows].astype(F32) * (w2 * scale)
        out_ref[rows] = merged.astype(BF16)
        lses.append(top + jnp.log(total) * LOG2E)
    out_ref[2 * HD:] = stat_tile(lses)


def merge(one, two):
    return pl.pallas_call(
        merge_kernel,
        out_shape=jax.ShapeDtypeStruct(one.shape, BF16),
        in_specs=[VMEM, VMEM],
        out_specs=VMEM,
        compiler_params=params(16),
        cost_estimate=cost(0, 1024),
        name="merge",
    )(one, two)


def finish_kernel(steps, own_ref, own_lse_ref, *refs):
    parts, outs = refs[:-QUAD], refs[-QUAD:]
    size = own_ref.shape[2]
    rows = size // (2 * GROUP)
    for pair in range(2):
        lses = [own_lse_ref[pair, 0:1]]
        for ref in parts:
            lses.append(lse_of(ref, pair))
        top = functools.reduce(jnp.maximum, lses)
        shares = [jnp.exp2(lse - top) for lse in lses]
        scale = 1.0 / functools.reduce(jnp.add, shares)
        total = own_ref[pair] * (shares[0] * scale)
        for ref, share in zip(parts, shares[1:]):
            total = total + ref[pair * HD:(pair + 1) * HD].astype(F32) * (share * scale)
        wide = total.T.reshape(2, GROUP, rows // 8, 8, HD)
        mean = jnp.sum(wide, axis=(0, 2)) * (steps / (2.0 * rows))
        flat = mean.reshape(GROUP * 8, HD)
        place = lax.broadcasted_iota(jnp.int32, flat.shape, 0) & 7
        up, down = pltpu.roll(flat, 4, 0), pltpu.roll(flat, GROUP * 8 - 4, 0)
        flat = flat + jnp.where(place < 4, down, up)
        dev = wide - flat.reshape(GROUP, 8, HD)[None, :, None]
        coarse = flat.astype(BF16).astype(F32)
        carried = jnp.where(place < 4, coarse, flat - coarse).astype(BF16)
        dev = dev.reshape(2, size // 2, HD).astype(BF16)
        for half in range(2):
            out = outs[2 * pair + half]
            out[0:size // 2] = dev[half]
            out[size // 2:] = carried


def finish(steps, own, own_lse, parts):
    size = own.shape[2]
    return pl.pallas_call(
        functools.partial(finish_kernel, steps),
        out_shape=[jax.ShapeDtypeStruct((size // 2 + GROUP * 8, HD), BF16)] * QUAD,
        in_specs=[VMEM] * (2 + len(parts)),
        out_specs=[VMEM] * QUAD,
        compiler_params=params(48),
        cost_estimate=cost(0, 1024),
        name="finish",
    )(own, own_lse, *parts)


def emit_kernel(*refs):
    msgs, (att_ref, dev_ref) = refs[:-2], refs[-2:]
    samples, steps, _ = att_ref.shape
    rows = samples * steps
    mine = lax.rem(lax.axis_index("sample"), QUAD)
    for h in range(HPD):
        for k in range(QUAD):
            msg = msgs[h * QUAD + k]
            head = jnp.bitwise_xor(mine, k) * HPD + h
            means = msg[GROUP * rows:].astype(F32)
            for g in range(GROUP):
                dev = msg[g * rows:(g + 1) * rows].astype(F32)
                pair = means[g * 8:(g + 1) * 8]
                mean = pair + pltpu.roll(pair, 4, 0)
                att = (dev.reshape(rows // 8, 8, HD) + mean[None]).reshape(samples, steps, HD)
                cols = lanes((head * GROUP + g) * HD, HD)
                att_ref[:, :, cols] = att.astype(BF16)
                dev_ref[:, :, cols] = dev.reshape(samples, steps, HD).astype(BF16)


def emit(msgs, shape):
    return pl.pallas_call(
        emit_kernel,
        out_shape=[jax.ShapeDtypeStruct(shape, BF16)] * 2,
        in_specs=[VMEM] * len(msgs),
        out_specs=[VMEM] * 2,
        compiler_params=params(32),
        cost_estimate=cost(1 << 20, 2 << 20),
        name="emit",
    )(*msgs)


def shards(prompt_kv, prompt_blocks, slot_prompt, queries, new_kv):
    nsample = lax.axis_size("sample")
    quads = nsample // QUAD
    samples, steps, width = queries.shape
    rows = samples * steps

    def across(array, k):
        return lax.ppermute(array, "sample", [(i, i ^ k) for i in range(nsample)])

    def along(array, shift):
        return lax.ppermute(
            array, "sample", [(i, (i + shift * QUAD) % nsample) for i in range(nsample)]
        )

    kv3 = prompt_kv.reshape(prompt_kv.shape[0], BLK, prompt_kv.shape[-1])
    msgs = pack_queries(queries, new_kv)
    near, *far = pack_kv(kv3.reshape(-1, kv3.shape[-1]))
    msgs = [msgs[0]] + [across(msgs[k], k) for k in range(1, QUAD)]
    near, msgs = lax.optimization_barrier((near, msgs))
    near = across(near, 1).reshape(HPD, -1, BLK, 2 * HD)

    def gather(h):
        own = jnp.stack([m[h, :GROUP * rows] for m in msgs])
        ahead = (quads - 1 + (1 - h % 2)) // 2
        held = {}
        for shift, hops in ((-1, ahead), (1, quads - 1 - ahead)):
            block = own
            for s in range(1, hops + 1):
                block = along(block, shift)
                held[-shift * s % quads] = block
        return held

    asked = [gather(h) for h in range(HPD)]
    arrived, handed = [], []
    for h in range(HPD):
        source = far[h]
        if h:
            source, arrived[-1], asked[h - 1], near = lax.optimization_barrier(
                (source, arrived[-1], asked[h - 1], near)
            )
        arrived.append(across(source, 2))
        handed.append(arrived[h][1])
    final = []
    for h in range(HPD):
        if h:
            handed[h], asked[h] = lax.optimization_barrier((handed[h], asked[h]))
        passed = across(handed[h], 1).reshape(-1, BLK, 2 * HD)
        blocks = [near, arrived[h].reshape(2, -1, BLK, 2 * HD), passed]
        offsets = tuple(sorted(asked[h]))
        partial = attend(
            h, offsets, 0, prompt_blocks, slot_prompt, kv3, blocks, [asked[h][o] for o in offsets]
        )
        if h:
            back, partial = lax.optimization_barrier((back, partial))
            done = finish(steps, *mine, back)
            final.append([done[0]] + [across(done[k], k) for k in range(1, QUAD)])
            partial, _ = lax.optimization_barrier((partial, done[0]))
        parts = dict(zip(offsets, partial))
        far_right = (quads - 1 + (1 - h % 2)) // 2
        back = []
        for shift, hops in sorted(((1, far_right), (-1, quads - 1 - far_right)), key=lambda x: x[1]):
            for s in range(hops, 0, -1):
                block = parts[shift * s % quads]
                if s < hops:
                    if s == 1:
                        moved, back = lax.optimization_barrier((moved, back))
                    block = merge(block, moved)
                moved = along(block, shift)
            if hops:
                back.append(moved)
        mine = attend(h, (0,), steps, prompt_blocks, slot_prompt, kv3, blocks, msgs)
    done = finish(steps, *mine, back)
    final.append([done[0]] + [across(done[k], k) for k in range(1, QUAD)])
    return tuple(emit([m for per_head in final for m in per_head], queries.shape))


def solution(mesh):
    placed = (
        P("groups", "sample", None, None),
        P("groups"),
        P("groups"),
        P(("groups", "sample"), None, None),
        P(("groups", "sample"), None, None),
    )
    return jax.shard_map(
        shards,
        mesh=mesh,
        in_specs=placed,
        out_specs=(P(("groups", "sample"), None, None), P(("groups", "sample"), None, None)),
        check_vma=False,
    )
```

```python
import functools
import math

import jax
import jax.numpy as jnp
from jax import lax
from jax.experimental import pallas as pl
from jax.experimental.pallas import tpu as pltpu
from jax.sharding import PartitionSpec as P

HEADS = 64
KVH = 8
HD = 128
BLK = 32
MAXB = 128
QUAD = 4
HPD = KVH // QUAD
GROUP = HEADS // KVH
TILE_BLOCKS = 8
TILE = TILE_BLOCKS * BLK
STAT_ROWS = 16
NEG = -1e30
LOG2E = math.log2(math.e)
EXP_SCALE = LOG2E / math.sqrt(HD)
F32 = jnp.float32
BF16 = jnp.bfloat16
ANY = pl.BlockSpec(memory_space=pl.ANY)
VMEM = pl.BlockSpec(memory_space=pltpu.VMEM)
SMEM = pl.BlockSpec(memory_space=pltpu.SMEM)


def lanes(start, size):
    return pl.ds(pl.multiple_of(start, 128), size)


def params(mib):
    return pltpu.CompilerParams(vmem_limit_bytes=mib << 20)


def cost(flops, nbytes, trans=0):
    return pl.CostEstimate(flops=flops, bytes_accessed=nbytes, transcendentals=trans)


def pack_queries_kernel(q_hbm, new_hbm, *refs):
    outs, (q_ref, new_ref, sem) = refs[:-3], refs[-3:]
    copies = [
        pltpu.make_async_copy(q_hbm, q_ref, sem.at[0]),
        pltpu.make_async_copy(new_hbm, new_ref, sem.at[1]),
    ]
    for copy in copies:
        copy.start()
    for copy in copies:
        copy.wait()
    mine = lax.rem(lax.axis_index("sample"), QUAD)
    rows = q_ref.shape[0] * q_ref.shape[1]

    def column(ref, head):
        return ref[:, :, lanes(head * HD, HD)].astype(F32).reshape(rows, HD).astype(BF16)

    for k in range(QUAD):
        for h in range(HPD):
            head = jnp.bitwise_xor(mine, k) * HPD + h
            for g in range(GROUP):
                outs[k][h, g * rows:(g + 1) * rows] = column(q_ref, head * GROUP + g)
            base = GROUP * rows
            outs[k][h, base:base + rows] = column(new_ref, head)
            outs[k][h, base + rows:base + 2 * rows] = column(new_ref, KVH + head)


def pack_queries(queries, new_kv):
    rows = queries.shape[0] * queries.shape[1]
    return pl.pallas_call(
        pack_queries_kernel,
        out_shape=[jax.ShapeDtypeStruct((HPD, (GROUP + 2) * rows, HD), BF16)] * QUAD,
        in_specs=[ANY, ANY],
        out_specs=[VMEM] * QUAD,
        scratch_shapes=[
            pltpu.VMEM(queries.shape, BF16),
            pltpu.VMEM(new_kv.shape, BF16),
            pltpu.SemaphoreType.DMA((2,)),
        ],
        compiler_params=params(56),
        cost_estimate=cost(0, 2 << 20),
        name="pack_queries",
    )(queries, new_kv)


def pack_kv_kernel(kv_ref, near, *refs):
    far, sem = refs[:-1], refs[-1]
    mine = lax.rem(lax.axis_index("sample"), QUAD)
    copies = []
    for h in range(HPD):
        for k in range(1, QUAD):
            head = jnp.bitwise_xor(mine, k) * HPD + h
            out = near.at[h] if k == 1 else far[h].at[k - 2]
            for part in range(2):
                copies.append(
                    pltpu.make_async_copy(
                        kv_ref.at[:, lanes((part * KVH + head) * HD, HD)],
                        out.at[:, part * HD:(part + 1) * HD],
                        sem.at[len(copies)],
                    )
                )
    for copy in copies:
        copy.start()
    for copy in copies:
        copy.wait()


def pack_kv(kv2):
    shape = jax.ShapeDtypeStruct((2, kv2.shape[0], 2 * HD), BF16)
    return pl.pallas_call(
        pack_kv_kernel,
        out_shape=[shape] * (1 + HPD),
        in_specs=[ANY],
        out_specs=[ANY] * (1 + HPD),
        scratch_shapes=[pltpu.SemaphoreType.DMA((2 * HPD * (QUAD - 1),))],
        compiler_params=params(16),
        cost_estimate=cost(0, 6 << 20),
        name="pack_kv",
    )(kv2)


def scores_of(keys, query):
    return lax.dot_general(keys, query, (((1,), (1,)), ((), ())), preferred_element_type=F32)


def values_by(values, weights):
    return lax.dot_general(values, weights, (((0,), (0,)), ((), ())), preferred_element_type=F32)


def attend_kernel(h, offsets, steps, counts_ref, slots_ref, kv_ref, near, same, passed, *refs):
    count = len(offsets)
    nq = QUAD if steps else count
    queries, refs = refs[:nq], refs[nq:]
    nout = 2 if steps else count
    outs, refs = refs[:nout], refs[nout:]
    held, asked, fresh, state, acc, stage, scores, weights, sem = refs
    nsample = lax.axis_size("sample")
    quads = nsample // QUAD
    index = lax.axis_index("sample")
    quad, mine = lax.div(index, QUAD), lax.rem(index, QUAD)
    blocks = kv_ref.shape[0]
    size = asked.shape[2]

    first_copies = []

    def copied(copies, source, target):
        copies.append(pltpu.make_async_copy(source, target, sem.at[len(first_copies) + len(later)]))
        copies[-1].start()

    later = []
    for n in range(nq):
        if steps:
            copied(first_copies, queries[n].at[h, 0:size], asked.at[0, n])
            copied(first_copies, queries[n].at[h, size:], fresh.at[n])
        else:
            copied(first_copies, queries[n], asked.at[n])
    for part in range(2):
        copied(
            later,
            kv_ref.at[:, :, lanes((part * KVH + mine * HPD + h) * HD, HD)],
            held.at[0:blocks, mine, :, part * HD:(part + 1) * HD],
        )
    for k, source in ((1, near.at[h]), (2, same.at[0]), (3, passed)):
        copied(later, source, held.at[0:blocks, jnp.bitwise_xor(mine, k)])
    held[blocks:] = jnp.zeros_like(held[blocks:])
    for copy in first_copies:
        copy.wait()

    def fresh_state(pair):
        parts = []
        for half in range(2):
            slot = 2 * pair + half
            rows = size // GROUP
            s = scores_of(fresh[slot, 0:rows], asked[0, slot])
            key = lax.broadcasted_iota(jnp.int32, s.shape, 0)
            row = lax.broadcasted_iota(jnp.int32, s.shape, 1) & (rows - 1)
            shift = steps.bit_length() - 1
            seen = ((row >> shift) == (key >> shift)) & ((row & (steps - 1)) >= (key & (steps - 1)))
            s = jnp.where(seen, s, NEG)
            m = jnp.max(s, axis=0, keepdims=True)
            p = jnp.exp2((s - m) * EXP_SCALE)
            l = jnp.sum(p, axis=0, keepdims=True)
            parts.append((m, l, values_by(fresh[slot, rows:], p.astype(BF16))))
        m, l, out = (jnp.concatenate(x, axis=1) for x in zip(*parts))
        state[pair, 0:1] = m
        state[pair, 1:2] = l
        acc[pair] = out

    if steps:
        for pair in range(2):
            fresh_state(pair)
    for copy in later:
        copy.wait()
    flat = held.reshape(held.shape[0] * QUAD * BLK, 2 * HD)

    def local_count(block):
        inside = jnp.clip(lax.rem(block, nsample) - QUAD * quad, 0, QUAD)
        return QUAD * lax.div(block, nsample) + inside

    def one_prompt(n, pair, low, high):
        tiles = lax.div(high - low + TILE_BLOCKS - 1, TILE_BLOCKS)
        query = asked[n, pl.ds(2 * pair, 2)].reshape(2 * size, HD)

        def score(t, top):
            row = pl.multiple_of((low + t * TILE_BLOCKS) * BLK, BLK)
            s = scores_of(flat[pl.ds(row, TILE), 0:HD], query)
            token = lax.broadcasted_iota(jnp.int32, s.shape, 0)
            s = jnp.where(token < (high - low - t * TILE_BLOCKS) * BLK, s, NEG)
            scores[pl.ds(pl.multiple_of(t * TILE, TILE), TILE)] = s
            return jnp.maximum(top, jnp.max(s.reshape(TILE // 8, 8, 2 * size), axis=0))

        before = state[pair, 0:1] if steps else jnp.full((1, 2 * size), NEG, F32)
        top = lax.fori_loop(0, tiles, score, jnp.broadcast_to(before, (8, 2 * size)))
        m = jnp.max(top, axis=0, keepdims=True)
        shift = m * EXP_SCALE

        def raise_block(b, total):
            rows = pl.ds(pl.multiple_of(b * BLK, BLK), BLK)
            p = jnp.exp2(scores[rows] * EXP_SCALE - shift)
            weights[rows] = p.astype(BF16)
            return total + jnp.sum(p.reshape(BLK // 8, 8, 2 * size), axis=0)

        def clear_block(b, _):
            weights[pl.ds(pl.multiple_of(b * BLK, BLK), BLK)] = jnp.zeros((BLK, 2 * size), BF16)
            return 0

        total = lax.fori_loop(0, high - low, raise_block, jnp.zeros((8, 2 * size), F32))
        lax.fori_loop(high - low, tiles * TILE_BLOCKS, clear_block, 0)
        l = jnp.sum(total, axis=0, keepdims=True)
        if steps:
            alpha = jnp.exp2(before * EXP_SCALE - shift)
            l = l + alpha * state[pair, 1:2]
            acc[pair] = alpha * acc[pair]
        else:
            acc[pair] = jnp.zeros((HD, 2 * size), F32)
        state[pair, 0:1] = m
        state[pair, 1:2] = l

        def add(t, _):
            row = pl.multiple_of((low + t * TILE_BLOCKS) * BLK, BLK)
            p = weights[pl.ds(pl.multiple_of(t * TILE, TILE), TILE)]
            acc[pair] += values_by(flat[pl.ds(row, TILE), HD:2 * HD], p)
            return 0

        lax.fori_loop(0, tiles, add, 0)

    def chunk(n, _):
        offset = jnp.int32(0) if steps else offset_of(n)
        home = lax.rem(quad + offset, quads)

        def prompt_of(pair, _):
            prompt = slots_ref[QUAD * home + 2 * jnp.bitwise_xor(lax.div(mine, 2), pair)]
            start = lax.fori_loop(0, prompt, lambda p, total: total + counts_ref[p], jnp.int32(0))
            low, high = local_count(start), local_count(start + counts_ref[prompt])
            one_prompt(n, pair, low, high)
            return 0

        lax.fori_loop(0, 2, prompt_of, 0)
        lses = []
        for pair in range(2):
            m, l = state[pair, 0:1], state[pair, 1:2]
            some = l > 0.0
            safe = jnp.where(some, l, 1.0)
            lses.append(jnp.where(some, m * EXP_SCALE + jnp.log(safe) * LOG2E, NEG))
            out = acc[pair] * (1.0 / safe)
            if steps:
                outs[0][pair] = out
                outs[1][pair] = jnp.broadcast_to(lses[pair], (8, 2 * size))
            else:
                stage[n, pair * HD:(pair + 1) * HD] = out.astype(BF16)
        if not steps:
            stage[n, 2 * HD:] = stat_tile(lses)
        return 0

    def offset_of(n):
        offset = jnp.int32(offsets[0])
        for i in range(1, count):
            offset = jnp.where(n == i, offsets[i], offset)
        return offset

    lax.fori_loop(0, count, chunk, 0)
    if not steps:
        copies = []
        for n in range(count):
            copied(copies, stage.at[n], outs[n])
            later.append(copies[-1])
        for copy in copies:
            copy.wait()


def attend(h, offsets, steps, counts, slots, kv3, arrived, queries):
    count = len(offsets)
    if steps:
        size = queries[0].shape[1] * GROUP // (GROUP + 2)
        out_shape = [
            jax.ShapeDtypeStruct((2, HD, 2 * size), F32),
            jax.ShapeDtypeStruct((2, 8, 2 * size), F32),
        ]
    else:
        size = queries[0].shape[1]
        out_shape = [jax.ShapeDtypeStruct((2 * HD + STAT_ROWS, 2 * size), BF16)] * count
    blocks = kv3.shape[0]
    max_tiles = -(-(-(-MAXB // lax.axis_size("sample")) * QUAD) // TILE_BLOCKS)
    work = count * 2 * size * blocks * BLK
    return pl.pallas_call(
        functools.partial(attend_kernel, h, offsets, steps),
        out_shape=out_shape,
        in_specs=[SMEM, SMEM, ANY] + [ANY] * len(arrived) + [ANY] * len(queries),
        out_specs=[VMEM if steps else ANY] * len(out_shape),
        scratch_shapes=[
            pltpu.VMEM((blocks + max_tiles * TILE_BLOCKS // QUAD, QUAD, BLK, 2 * HD), BF16),
            pltpu.VMEM((count, QUAD, size, HD), BF16),
            pltpu.VMEM((QUAD, 2 * size // GROUP, HD), BF16),
            pltpu.VMEM((2, 8, 2 * size), F32),
            pltpu.VMEM((2, HD, 2 * size), F32),
            pltpu.VMEM((1 if steps else count, 2 * HD + STAT_ROWS, 2 * size), BF16),
            pltpu.VMEM((max_tiles * TILE, 2 * size), F32),
            pltpu.VMEM((max_tiles * TILE, 2 * size), BF16),
            pltpu.SemaphoreType.DMA((2 * QUAD + 2 * count + 8,)),
        ],
        compiler_params=params(48),
        cost_estimate=cost(0, 1024),
        name="attend_own" if steps else "attend_others",
    )(counts, slots, kv3, *arrived, *queries)


def lse_of(ref, pair):
    tail = ref[2 * HD:2 * HD + STAT_ROWS].astype(F32)[3 * pair:3 * pair + 3]
    return tail[0:1] + tail[1:2] + tail[2:3]


def stat_tile(lses):
    place = lax.broadcasted_iota(jnp.int32, (STAT_ROWS, lses[0].shape[1]), 0)
    stats = jnp.zeros(place.shape, F32)
    for pair, lse in enumerate(lses):
        coarse = lse.astype(BF16).astype(F32)
        middle = (lse - coarse).astype(BF16).astype(F32)
        for i, piece in enumerate((coarse, middle, lse - coarse - middle)):
            stats = jnp.where(place == 3 * pair + i, piece, stats)
    return stats.astype(BF16)


def merge_kernel(one_ref, two_ref, out_ref):
    lses = []
    for pair in range(2):
        one, two = lse_of(one_ref, pair), lse_of(two_ref, pair)
        top = jnp.maximum(one, two)
        w1, w2 = jnp.exp2(one - top), jnp.exp2(two - top)
        total = w1 + w2
        scale = 1.0 / total
        rows = slice(pair * HD, (pair + 1) * HD)
        merged = one_ref[rows].astype(F32) * (w1 * scale) + two_ref[rows].astype(F32) * (w2 * scale)
        out_ref[rows] = merged.astype(BF16)
        lses.append(top + jnp.log(total) * LOG2E)
    out_ref[2 * HD:] = stat_tile(lses)


def merge(one, two):
    return pl.pallas_call(
        merge_kernel,
        out_shape=jax.ShapeDtypeStruct(one.shape, BF16),
        in_specs=[VMEM, VMEM],
        out_specs=VMEM,
        compiler_params=params(16),
        cost_estimate=cost(0, 1024),
        name="merge",
    )(one, two)


def finish_kernel(steps, own_ref, own_lse_ref, *refs):
    parts, outs = refs[:-QUAD], refs[-QUAD:]
    size = own_ref.shape[2]
    rows = size // (2 * GROUP)
    for pair in range(2):
        lses = [own_lse_ref[pair, 0:1]]
        for ref in parts:
            lses.append(lse_of(ref, pair))
        top = functools.reduce(jnp.maximum, lses)
        shares = [jnp.exp2(lse - top) for lse in lses]
        scale = 1.0 / functools.reduce(jnp.add, shares)
        total = own_ref[pair] * (shares[0] * scale)
        for ref, share in zip(parts, shares[1:]):
            total = total + ref[pair * HD:(pair + 1) * HD].astype(F32) * (share * scale)
        wide = total.T.reshape(2, GROUP, rows // 8, 8, HD)
        mean = jnp.sum(wide, axis=(0, 2)) * (steps / (2.0 * rows))
        flat = mean.reshape(GROUP * 8, HD)
        place = lax.broadcasted_iota(jnp.int32, flat.shape, 0) & 7
        up, down = pltpu.roll(flat, 4, 0), pltpu.roll(flat, GROUP * 8 - 4, 0)
        flat = flat + jnp.where(place < 4, down, up)
        dev = wide - flat.reshape(GROUP, 8, HD)[None, :, None]
        coarse = flat.astype(BF16).astype(F32)
        carried = jnp.where(place < 4, coarse, flat - coarse).astype(BF16)
        dev = dev.reshape(2, size // 2, HD).astype(BF16)
        for half in range(2):
            out = outs[2 * pair + half]
            out[0:size // 2] = dev[half]
            out[size // 2:] = carried


def finish(steps, own, own_lse, parts):
    size = own.shape[2]
    return pl.pallas_call(
        functools.partial(finish_kernel, steps),
        out_shape=[jax.ShapeDtypeStruct((size // 2 + GROUP * 8, HD), BF16)] * QUAD,
        in_specs=[VMEM] * (2 + len(parts)),
        out_specs=[VMEM] * QUAD,
        compiler_params=params(48),
        cost_estimate=cost(0, 1024),
        name="finish",
    )(own, own_lse, *parts)


def emit_kernel(*refs):
    msgs, (att_ref, dev_ref) = refs[:-2], refs[-2:]
    samples, steps, _ = att_ref.shape
    rows = samples * steps
    mine = lax.rem(lax.axis_index("sample"), QUAD)
    for h in range(HPD):
        for k in range(QUAD):
            msg = msgs[h * QUAD + k]
            head = jnp.bitwise_xor(mine, k) * HPD + h
            means = msg[GROUP * rows:].astype(F32)
            for g in range(GROUP):
                dev = msg[g * rows:(g + 1) * rows].astype(F32)
                pair = means[g * 8:(g + 1) * 8]
                mean = pair + pltpu.roll(pair, 4, 0)
                att = (dev.reshape(rows // 8, 8, HD) + mean[None]).reshape(samples, steps, HD)
                cols = lanes((head * GROUP + g) * HD, HD)
                att_ref[:, :, cols] = att.astype(BF16)
                dev_ref[:, :, cols] = dev.reshape(samples, steps, HD).astype(BF16)


def emit(msgs, shape):
    return pl.pallas_call(
        emit_kernel,
        out_shape=[jax.ShapeDtypeStruct(shape, BF16)] * 2,
        in_specs=[VMEM] * len(msgs),
        out_specs=[VMEM] * 2,
        compiler_params=params(32),
        cost_estimate=cost(1 << 20, 2 << 20),
        name="emit",
    )(*msgs)


def shards(prompt_kv, prompt_blocks, slot_prompt, queries, new_kv):
    nsample = lax.axis_size("sample")
    quads = nsample // QUAD
    samples, steps, width = queries.shape
    rows = samples * steps

    def across(array, k):
        return lax.ppermute(array, "sample", [(i, i ^ k) for i in range(nsample)])

    def along(array, shift):
        return lax.ppermute(
            array, "sample", [(i, (i + shift * QUAD) % nsample) for i in range(nsample)]
        )

    kv3 = prompt_kv.reshape(prompt_kv.shape[0], BLK, prompt_kv.shape[-1])
    msgs = pack_queries(queries, new_kv)
    near, *far = pack_kv(kv3.reshape(-1, kv3.shape[-1]))
    msgs = [msgs[0]] + [across(msgs[k], k) for k in range(1, QUAD)]
    near, msgs = lax.optimization_barrier((near, msgs))
    near = across(near, 1).reshape(HPD, -1, BLK, 2 * HD)

    own = jnp.stack([jnp.stack([m[h, :GROUP * rows] for m in msgs]) for h in range(HPD)])
    first_hop = {shift: along(own, shift) for shift in ((-1, 1) if quads > 2 else (-1,))}
    asked = []
    for h in range(HPD):
        ahead = (quads - 1 + (1 - h % 2)) // 2 if quads > 2 else quads - 1
        held = {}
        for shift, hops in ((-1, ahead), (1, quads - 1 - ahead)):
            for s in range(1, hops + 1):
                block = first_hop[shift][h] if s == 1 else along(block, shift)
                held[-shift * s % quads] = block
        asked.append(held)
    arrived, handed = [], []
    for h in range(HPD):
        source = far[h]
        if h:
            source, arrived[-1], first_hop, near = lax.optimization_barrier(
                (source, arrived[-1], first_hop, near)
            )
        arrived.append(across(source, 2))
        handed.append(arrived[h][1])
    final = []
    for h in range(HPD):
        if h:
            handed[h], asked[h] = lax.optimization_barrier((handed[h], asked[h]))
        passed = across(handed[h], 1).reshape(-1, BLK, 2 * HD)
        blocks = [near, arrived[h].reshape(2, -1, BLK, 2 * HD), passed]
        offsets = tuple(sorted(asked[h]))
        partial = attend(
            h, offsets, 0, prompt_blocks, slot_prompt, kv3, blocks, [asked[h][o] for o in offsets]
        )
        if h:
            back, partial = lax.optimization_barrier((back, partial))
            done = finish(steps, *mine, back)
            final.append([done[0]] + [across(done[k], k) for k in range(1, QUAD)])
            partial, _ = lax.optimization_barrier((partial, done[0]))
        parts = dict(zip(offsets, partial))
        far_right = (quads - 1 + (1 - h % 2)) // 2
        back = []
        for shift, hops in sorted(((1, far_right), (-1, quads - 1 - far_right)), key=lambda x: x[1]):
            for s in range(hops, 0, -1):
                block = parts[shift * s % quads]
                if s < hops:
                    if s == 1:
                        moved, back = lax.optimization_barrier((moved, back))
                    block = merge(block, moved)
                moved = along(block, shift)
            if hops:
                back.append(moved)
        mine = attend(h, (0,), steps, prompt_blocks, slot_prompt, kv3, blocks, msgs)
    done = finish(steps, *mine, back)
    final.append([done[0]] + [across(done[k], k) for k in range(1, QUAD)])
    return tuple(emit([m for per_head in final for m in per_head], queries.shape))


def solution(mesh):
    placed = (
        P("groups", "sample", None, None),
        P("groups"),
        P("groups"),
        P(("groups", "sample"), None, None),
        P(("groups", "sample"), None, None),
    )
    return jax.shard_map(
        shards,
        mesh=mesh,
        in_specs=placed,
        out_specs=(P(("groups", "sample"), None, None), P(("groups", "sample"), None, None)),
        check_vma=False,
    )
```

```python
import functools
import math

import jax
import jax.numpy as jnp
from jax import lax
from jax.experimental import pallas as pl
from jax.experimental.pallas import tpu as pltpu
from jax.sharding import PartitionSpec as P

HEADS = 64
KVH = 8
HD = 128
BLK = 32
MAXB = 128
QUAD = 4
HPD = KVH // QUAD
GROUP = HEADS // KVH
TILE_BLOCKS = 8
TILE = TILE_BLOCKS * BLK
STAT_ROWS = 16
NEG = -1e30
LOG2E = math.log2(math.e)
EXP_SCALE = LOG2E / math.sqrt(HD)
F32 = jnp.float32
BF16 = jnp.bfloat16
ANY = pl.BlockSpec(memory_space=pl.ANY)
VMEM = pl.BlockSpec(memory_space=pltpu.VMEM)
SMEM = pl.BlockSpec(memory_space=pltpu.SMEM)


def lanes(start, size):
    return pl.ds(pl.multiple_of(start, 128), size)


def params(mib):
    return pltpu.CompilerParams(vmem_limit_bytes=mib << 20)


def cost(flops, nbytes, trans=0):
    return pl.CostEstimate(flops=flops, bytes_accessed=nbytes, transcendentals=trans)


def pack_queries_kernel(q_hbm, new_hbm, *refs):
    outs, (q_ref, new_ref, sem) = refs[:-3], refs[-3:]
    copies = [
        pltpu.make_async_copy(q_hbm, q_ref, sem.at[0]),
        pltpu.make_async_copy(new_hbm, new_ref, sem.at[1]),
    ]
    for copy in copies:
        copy.start()
    for copy in copies:
        copy.wait()
    mine = lax.rem(lax.axis_index("sample"), QUAD)
    rows = q_ref.shape[0] * q_ref.shape[1]

    def column(ref, head):
        return ref[:, :, lanes(head * HD, HD)].astype(F32).reshape(rows, HD).astype(BF16)

    for k in range(QUAD):
        for h in range(HPD):
            head = jnp.bitwise_xor(mine, k) * HPD + h
            for g in range(GROUP):
                outs[k][h, g * rows:(g + 1) * rows] = column(q_ref, head * GROUP + g)
            base = GROUP * rows
            outs[k][h, base:base + rows] = column(new_ref, head)
            outs[k][h, base + rows:base + 2 * rows] = column(new_ref, KVH + head)


def pack_queries(queries, new_kv):
    rows = queries.shape[0] * queries.shape[1]
    return pl.pallas_call(
        pack_queries_kernel,
        out_shape=[jax.ShapeDtypeStruct((HPD, (GROUP + 2) * rows, HD), BF16)] * QUAD,
        in_specs=[ANY, ANY],
        out_specs=[VMEM] * QUAD,
        scratch_shapes=[
            pltpu.VMEM(queries.shape, BF16),
            pltpu.VMEM(new_kv.shape, BF16),
            pltpu.SemaphoreType.DMA((2,)),
        ],
        compiler_params=params(56),
        cost_estimate=cost(0, 2 << 20),
        name="pack_queries",
    )(queries, new_kv)


def pack_kv_kernel(kv_ref, near, *refs):
    far, sem = refs[:-1], refs[-1]
    mine = lax.rem(lax.axis_index("sample"), QUAD)
    copies = []
    for h in range(HPD):
        for k in range(1, QUAD):
            head = jnp.bitwise_xor(mine, k) * HPD + h
            out = near.at[h] if k == 1 else far[h].at[k - 2]
            for part in range(2):
                copies.append(
                    pltpu.make_async_copy(
                        kv_ref.at[:, lanes((part * KVH + head) * HD, HD)],
                        out.at[:, part * HD:(part + 1) * HD],
                        sem.at[len(copies)],
                    )
                )
    for copy in copies:
        copy.start()
    for copy in copies:
        copy.wait()


def pack_kv(kv2):
    shape = jax.ShapeDtypeStruct((2, kv2.shape[0], 2 * HD), BF16)
    return pl.pallas_call(
        pack_kv_kernel,
        out_shape=[shape] * (1 + HPD),
        in_specs=[ANY],
        out_specs=[ANY] * (1 + HPD),
        scratch_shapes=[pltpu.SemaphoreType.DMA((2 * HPD * (QUAD - 1),))],
        compiler_params=params(16),
        cost_estimate=cost(0, 6 << 20),
        name="pack_kv",
    )(kv2)


def scores_of(keys, query):
    return lax.dot_general(keys, query, (((1,), (1,)), ((), ())), preferred_element_type=F32)


def values_by(values, weights):
    return lax.dot_general(values, weights, (((0,), (0,)), ((), ())), preferred_element_type=F32)


def attend_kernel(h, offsets, steps, max_tiles, counts_ref, slots_ref, kv_ref, near, same, passed, *refs):
    count = len(offsets)
    nq = QUAD if steps else count
    queries, refs = refs[:nq], refs[nq:]
    nout = 2 if steps else count
    outs, refs = refs[:nout], refs[nout:]
    held, asked, fresh, state, acc, stage, scores, weights, sem = refs
    nsample = lax.axis_size("sample")
    quads = nsample // QUAD
    index = lax.axis_index("sample")
    quad, mine = lax.div(index, QUAD), lax.rem(index, QUAD)
    blocks = kv_ref.shape[0]
    size = asked.shape[2]

    first_copies = []

    def copied(copies, source, target):
        copies.append(pltpu.make_async_copy(source, target, sem.at[len(first_copies) + len(later)]))
        copies[-1].start()

    later = []
    for n in range(nq):
        if steps:
            copied(first_copies, queries[n].at[h, 0:size], asked.at[0, n])
            copied(first_copies, queries[n].at[h, size:], fresh.at[n])
        else:
            copied(first_copies, queries[n], asked.at[n])
    for part in range(2):
        copied(
            later,
            kv_ref.at[:, :, lanes((part * KVH + mine * HPD + h) * HD, HD)],
            held.at[0:blocks, mine, :, part * HD:(part + 1) * HD],
        )
    for k, source in ((1, near.at[h]), (2, same.at[0]), (3, passed)):
        copied(later, source, held.at[0:blocks, jnp.bitwise_xor(mine, k)])
    held[blocks:] = jnp.zeros_like(held[blocks:])
    for copy in first_copies:
        copy.wait()

    def fresh_state(pair):
        parts = []
        for half in range(2):
            slot = 2 * pair + half
            rows = size // GROUP
            s = scores_of(fresh[slot, 0:rows], asked[0, slot])
            key = lax.broadcasted_iota(jnp.int32, s.shape, 0)
            row = lax.broadcasted_iota(jnp.int32, s.shape, 1) & (rows - 1)
            shift = steps.bit_length() - 1
            seen = ((row >> shift) == (key >> shift)) & ((row & (steps - 1)) >= (key & (steps - 1)))
            s = jnp.where(seen, s, NEG)
            m = jnp.max(s, axis=0, keepdims=True)
            p = jnp.exp2((s - m) * EXP_SCALE)
            l = jnp.sum(p, axis=0, keepdims=True)
            parts.append((m, l, values_by(fresh[slot, rows:], p.astype(BF16))))
        m, l, out = (jnp.concatenate(x, axis=1) for x in zip(*parts))
        state[pair, 0:1] = m
        state[pair, 1:2] = l
        acc[pair] = out

    if steps:
        for pair in range(2):
            fresh_state(pair)
    for copy in later:
        copy.wait()
    flat = held.reshape(held.shape[0] * QUAD * BLK, 2 * HD)

    def local_count(block):
        inside = jnp.clip(lax.rem(block, nsample) - QUAD * quad, 0, QUAD)
        return QUAD * lax.div(block, nsample) + inside

    def one_pass(n, pair, low, high, tiles):
        tokens = tiles * TILE
        query = asked[n, pl.ds(2 * pair, 2)].reshape(2 * size, HD)
        row = pl.multiple_of(low * BLK, BLK)
        before = state[pair, 0:1] if steps else None
        top = jnp.broadcast_to(before, (8, 2 * size)) if steps else None
        for t in range(tiles):
            s = scores_of(flat[pl.ds(row + t * TILE, TILE), 0:HD], query)
            if t == tiles - 1:
                token = lax.broadcasted_iota(jnp.int32, s.shape, 0)
                s = jnp.where(token < (high - low - t * TILE_BLOCKS) * BLK, s, NEG)
            scores[t * TILE:(t + 1) * TILE] = s
            part = jnp.max(s.reshape(TILE // 8, 8, 2 * size), axis=0)
            top = part if top is None else jnp.maximum(top, part)
        m = jnp.max(top, axis=0, keepdims=True)
        shift = m * EXP_SCALE
        total = None
        for b in range(tokens // BLK):
            p = jnp.exp2(scores[b * BLK:(b + 1) * BLK] * EXP_SCALE - shift)
            weights[b * BLK:(b + 1) * BLK] = p.astype(BF16)
            part = jnp.sum(p.reshape(BLK // 8, 8, 2 * size), axis=0)
            total = part if total is None else total + part
        l = jnp.sum(total, axis=0, keepdims=True)
        out = values_by(flat[pl.ds(row, tokens), HD:2 * HD], weights[0:tokens])
        if steps:
            alpha = jnp.exp2(before * EXP_SCALE - shift)
            l = l + alpha * state[pair, 1:2]
            out = out + alpha * acc[pair]
        state[pair, 0:1] = m
        state[pair, 1:2] = l
        acc[pair] = out

    def chunk(n, _):
        offset = jnp.int32(0) if steps else offset_of(n)
        home = lax.rem(quad + offset, quads)

        def prompt_of(pair, _):
            prompt = slots_ref[QUAD * home + 2 * jnp.bitwise_xor(lax.div(mine, 2), pair)]
            start = lax.fori_loop(0, prompt, lambda p, total: total + counts_ref[p], jnp.int32(0))
            low, high = local_count(start), local_count(start + counts_ref[prompt])
            tiles = lax.div(high - low + TILE_BLOCKS - 1, TILE_BLOCKS)
            if not steps:
                @pl.when(tiles == 0)
                def _():
                    state[pair, 0:1] = jnp.full((1, 2 * size), NEG, F32)
                    state[pair, 1:2] = jnp.zeros((1, 2 * size), F32)
                    acc[pair] = jnp.zeros((HD, 2 * size), F32)

            for t in range(1, max_tiles + 1):
                @pl.when(tiles == t)
                def _(t=t):
                    one_pass(n, pair, low, high, t)

            return 0

        lax.fori_loop(0, 2, prompt_of, 0)
        lses = []
        for pair in range(2):
            m, l = state[pair, 0:1], state[pair, 1:2]
            some = l > 0.0
            safe = jnp.where(some, l, 1.0)
            lses.append(jnp.where(some, m * EXP_SCALE + jnp.log(safe) * LOG2E, NEG))
            out = acc[pair] * (1.0 / safe)
            if steps:
                outs[0][pair] = out
                outs[1][pair] = jnp.broadcast_to(lses[pair], (8, 2 * size))
            else:
                stage[n, pair * HD:(pair + 1) * HD] = out.astype(BF16)
        if not steps:
            stage[n, 2 * HD:] = stat_tile(lses)
        return 0

    def offset_of(n):
        offset = jnp.int32(offsets[0])
        for i in range(1, count):
            offset = jnp.where(n == i, offsets[i], offset)
        return offset

    lax.fori_loop(0, count, chunk, 0)
    if not steps:
        copies = []
        for n in range(count):
            copied(copies, stage.at[n], outs[n])
            later.append(copies[-1])
        for copy in copies:
            copy.wait()


def attend(h, offsets, steps, counts, slots, kv3, arrived, queries):
    count = len(offsets)
    if steps:
        size = queries[0].shape[1] * GROUP // (GROUP + 2)
        out_shape = [
            jax.ShapeDtypeStruct((2, HD, 2 * size), F32),
            jax.ShapeDtypeStruct((2, 8, 2 * size), F32),
        ]
    else:
        size = queries[0].shape[1]
        out_shape = [jax.ShapeDtypeStruct((2 * HD + STAT_ROWS, 2 * size), BF16)] * count
    blocks = kv3.shape[0]
    max_tiles = -(-(-(-MAXB // lax.axis_size("sample")) * QUAD) // TILE_BLOCKS)
    work = count * 2 * size * blocks * BLK
    return pl.pallas_call(
        functools.partial(attend_kernel, h, offsets, steps, max_tiles),
        out_shape=out_shape,
        in_specs=[SMEM, SMEM, ANY] + [ANY] * len(arrived) + [ANY] * len(queries),
        out_specs=[VMEM if steps else ANY] * len(out_shape),
        scratch_shapes=[
            pltpu.VMEM((blocks + max_tiles * TILE_BLOCKS // QUAD, QUAD, BLK, 2 * HD), BF16),
            pltpu.VMEM((count, QUAD, size, HD), BF16),
            pltpu.VMEM((QUAD, 2 * size // GROUP, HD), BF16),
            pltpu.VMEM((2, 8, 2 * size), F32),
            pltpu.VMEM((2, HD, 2 * size), F32),
            pltpu.VMEM((1 if steps else count, 2 * HD + STAT_ROWS, 2 * size), BF16),
            pltpu.VMEM((max_tiles * TILE, 2 * size), F32),
            pltpu.VMEM((max_tiles * TILE, 2 * size), BF16),
            pltpu.SemaphoreType.DMA((2 * QUAD + 2 * count + 8,)),
        ],
        compiler_params=params(48),
        cost_estimate=cost(10**9 if steps else 10**10, 4 << 20),
        name="attend_own" if steps else "attend_others",
    )(counts, slots, kv3, *arrived, *queries)


def lse_of(ref, pair):
    tail = ref[2 * HD:2 * HD + STAT_ROWS].astype(F32)[3 * pair:3 * pair + 3]
    return tail[0:1] + tail[1:2] + tail[2:3]


def stat_tile(lses):
    place = lax.broadcasted_iota(jnp.int32, (STAT_ROWS, lses[0].shape[1]), 0)
    stats = jnp.zeros(place.shape, F32)
    for pair, lse in enumerate(lses):
        coarse = lse.astype(BF16).astype(F32)
        middle = (lse - coarse).astype(BF16).astype(F32)
        for i, piece in enumerate((coarse, middle, lse - coarse - middle)):
            stats = jnp.where(place == 3 * pair + i, piece, stats)
    return stats.astype(BF16)


def merge_kernel(one_ref, two_ref, out_ref):
    lses = []
    for pair in range(2):
        one, two = lse_of(one_ref, pair), lse_of(two_ref, pair)
        top = jnp.maximum(one, two)
        w1, w2 = jnp.exp2(one - top), jnp.exp2(two - top)
        total = w1 + w2
        scale = 1.0 / total
        rows = slice(pair * HD, (pair + 1) * HD)
        merged = one_ref[rows].astype(F32) * (w1 * scale) + two_ref[rows].astype(F32) * (w2 * scale)
        out_ref[rows] = merged.astype(BF16)
        lses.append(top + jnp.log(total) * LOG2E)
    out_ref[2 * HD:] = stat_tile(lses)


def merge(one, two):
    return pl.pallas_call(
        merge_kernel,
        out_shape=jax.ShapeDtypeStruct(one.shape, BF16),
        in_specs=[VMEM, VMEM],
        out_specs=VMEM,
        compiler_params=params(16),
        cost_estimate=cost(0, 1024),
        name="merge",
    )(one, two)


def finish_kernel(steps, own_ref, own_lse_ref, *refs):
    parts, outs = refs[:-QUAD], refs[-QUAD:]
    size = own_ref.shape[2]
    rows = size // (2 * GROUP)
    for pair in range(2):
        lses = [own_lse_ref[pair, 0:1]]
        for ref in parts:
            lses.append(lse_of(ref, pair))
        top = functools.reduce(jnp.maximum, lses)
        shares = [jnp.exp2(lse - top) for lse in lses]
        scale = 1.0 / functools.reduce(jnp.add, shares)
        total = own_ref[pair] * (shares[0] * scale)
        for ref, share in zip(parts, shares[1:]):
            total = total + ref[pair * HD:(pair + 1) * HD].astype(F32) * (share * scale)
        wide = total.T.reshape(2, GROUP, rows // 8, 8, HD)
        mean = jnp.sum(wide, axis=(0, 2)) * (steps / (2.0 * rows))
        flat = mean.reshape(GROUP * 8, HD)
        place = lax.broadcasted_iota(jnp.int32, flat.shape, 0) & 7
        up, down = pltpu.roll(flat, 4, 0), pltpu.roll(flat, GROUP * 8 - 4, 0)
        flat = flat + jnp.where(place < 4, down, up)
        dev = wide - flat.reshape(GROUP, 8, HD)[None, :, None]
        coarse = flat.astype(BF16).astype(F32)
        carried = jnp.where(place < 4, coarse, flat - coarse).astype(BF16)
        dev = dev.reshape(2, size // 2, HD).astype(BF16)
        for half in range(2):
            out = outs[2 * pair + half]
            out[0:size // 2] = dev[half]
            out[size // 2:] = carried


def finish(steps, own, own_lse, parts):
    size = own.shape[2]
    return pl.pallas_call(
        functools.partial(finish_kernel, steps),
        out_shape=[jax.ShapeDtypeStruct((size // 2 + GROUP * 8, HD), BF16)] * QUAD,
        in_specs=[VMEM] * (2 + len(parts)),
        out_specs=[VMEM] * QUAD,
        compiler_params=params(48),
        cost_estimate=cost(0, 1024),
        name="finish",
    )(own, own_lse, *parts)


def emit_kernel(*refs):
    msgs, (att_ref, dev_ref) = refs[:-2], refs[-2:]
    samples, steps, _ = att_ref.shape
    rows = samples * steps
    mine = lax.rem(lax.axis_index("sample"), QUAD)
    for h in range(HPD):
        for k in range(QUAD):
            msg = msgs[h * QUAD + k]
            head = jnp.bitwise_xor(mine, k) * HPD + h
            means = msg[GROUP * rows:].astype(F32)
            for g in range(GROUP):
                dev = msg[g * rows:(g + 1) * rows].astype(F32)
                pair = means[g * 8:(g + 1) * 8]
                mean = pair + pltpu.roll(pair, 4, 0)
                att = (dev.reshape(rows // 8, 8, HD) + mean[None]).reshape(samples, steps, HD)
                cols = lanes((head * GROUP + g) * HD, HD)
                att_ref[:, :, cols] = att.astype(BF16)
                dev_ref[:, :, cols] = dev.reshape(samples, steps, HD).astype(BF16)


def emit(msgs, shape):
    return pl.pallas_call(
        emit_kernel,
        out_shape=[jax.ShapeDtypeStruct(shape, BF16)] * 2,
        in_specs=[VMEM] * len(msgs),
        out_specs=[VMEM] * 2,
        compiler_params=params(32),
        cost_estimate=cost(1 << 20, 2 << 20),
        name="emit",
    )(*msgs)


def shards(prompt_kv, prompt_blocks, slot_prompt, queries, new_kv):
    nsample = lax.axis_size("sample")
    quads = nsample // QUAD
    samples, steps, width = queries.shape
    rows = samples * steps

    def across(array, k):
        return lax.ppermute(array, "sample", [(i, i ^ k) for i in range(nsample)])

    def along(array, shift):
        return lax.ppermute(
            array, "sample", [(i, (i + shift * QUAD) % nsample) for i in range(nsample)]
        )

    kv3 = prompt_kv.reshape(prompt_kv.shape[0], BLK, prompt_kv.shape[-1])
    msgs = pack_queries(queries, new_kv)
    near, *far = pack_kv(kv3.reshape(-1, kv3.shape[-1]))
    msgs = [msgs[0]] + [across(msgs[k], k) for k in range(1, QUAD)]
    near, msgs = lax.optimization_barrier((near, msgs))
    near = across(near, 1).reshape(HPD, -1, BLK, 2 * HD)

    own = jnp.stack([jnp.stack([m[h, :GROUP * rows] for m in msgs]) for h in range(HPD)])
    first_hop = {shift: along(own, shift) for shift in ((-1, 1) if quads > 2 else (-1,))}
    asked = []
    for h in range(HPD):
        ahead = (quads - 1 + (1 - h % 2)) // 2 if quads > 2 else quads - 1
        held = {}
        for shift, hops in ((-1, ahead), (1, quads - 1 - ahead)):
            for s in range(1, hops + 1):
                block = first_hop[shift][h] if s == 1 else block
                if s == 2 and h:
                    block, asked[h - 1] = lax.optimization_barrier((block, asked[h - 1]))
                if s > 1:
                    block = along(block, shift)
                held[-shift * s % quads] = block
        asked.append(held)
    arrived, handed = [], []
    for h in range(HPD):
        source = far[h]
        if h:
            source, arrived[-1], first_hop, near = lax.optimization_barrier(
                (source, arrived[-1], first_hop, near)
            )
        arrived.append(across(source, 2))
        handed.append(arrived[h][1])

    def others(h, gate):
        if gate is not None:
            handed[h], asked[h], _ = lax.optimization_barrier((handed[h], asked[h], gate))
        passed = across(handed[h], 1).reshape(-1, BLK, 2 * HD)
        blocks = [near, arrived[h].reshape(2, -1, BLK, 2 * HD), passed]
        offsets = tuple(sorted(asked[h]))
        partial = attend(
            h, offsets, 0, prompt_blocks, slot_prompt, kv3, blocks, [asked[h][o] for o in offsets]
        )
        return blocks, dict(zip(offsets, partial))

    def chains(h):
        far_right = (quads - 1 + (1 - h % 2)) // 2
        pair = ((1, far_right), (-1, quads - 1 - far_right))
        return [c for c in sorted(pair, key=lambda x: x[1]) if c[1]]

    def sent(h, parts):
        return [along(parts[shift * hops % quads], shift) for shift, hops in chains(h)]

    def summed(h, parts, moved, gate):
        back = []
        for (shift, hops), block in zip(chains(h), moved):
            for s in range(hops - 1, 0, -1):
                if s == hops - 1:
                    block, back, _ = lax.optimization_barrier((block, back, gate))
                block = along(merge(parts[shift * s % quads], block), shift)
            back.append(block)
        return back

    def finished(h, mine, back):
        done = finish(steps, *mine, back)
        return [done[0]] + [across(done[k], k) for k in range(1, QUAD)]

    final = []
    waiting = None
    gate = None
    for h in range(HPD):
        blocks, parts = others(h, gate)
        if waiting is not None:
            back = summed(*waiting[:3], parts)
            final.append(finished(h - 1, waiting[3], back))
        moved = sent(h, parts)
        _, later_msgs = lax.optimization_barrier((parts, msgs))
        mine = attend(h, (0,), steps, prompt_blocks, slot_prompt, kv3, blocks, later_msgs)
        waiting = (h, parts, moved, mine)
        gate = (mine[0], moved[-1]) if moved else (mine[0],)
    final.append(finished(HPD - 1, mine, summed(*waiting[:3], moved)))
    return tuple(emit([m for per_head in final for m in per_head], queries.shape))


def solution(mesh):
    placed = (
        P("groups", "sample", None, None),
        P("groups"),
        P("groups"),
        P(("groups", "sample"), None, None),
        P(("groups", "sample"), None, None),
    )
    return jax.shard_map(
        shards,
        mesh=mesh,
        in_specs=placed,
        out_specs=(P(("groups", "sample"), None, None), P(("groups", "sample"), None, None)),
        check_vma=False,
    )
```

```python
import functools
import math

import jax
import jax.numpy as jnp
from jax import lax
from jax.experimental import pallas as pl
from jax.experimental.pallas import tpu as pltpu
from jax.sharding import PartitionSpec as P

HEADS = 64
KVH = 8
HD = 128
BLK = 32
MAXB = 128
QUAD = 4
HPD = KVH // QUAD
GROUP = HEADS // KVH
TILE_BLOCKS = 4
TILE = TILE_BLOCKS * BLK
STAT_ROWS = 16
NEG = -1e30
LOG2E = math.log2(math.e)
EXP_SCALE = LOG2E / math.sqrt(HD)
F32 = jnp.float32
BF16 = jnp.bfloat16
ANY = pl.BlockSpec(memory_space=pl.ANY)
VMEM = pl.BlockSpec(memory_space=pltpu.VMEM)
SMEM = pl.BlockSpec(memory_space=pltpu.SMEM)


def lanes(start, size):
    return pl.ds(pl.multiple_of(start, 128), size)


def params(mib):
    return pltpu.CompilerParams(vmem_limit_bytes=mib << 20)


def cost(flops, nbytes, trans=0):
    return pl.CostEstimate(flops=flops, bytes_accessed=nbytes, transcendentals=trans)


def pack_queries_kernel(q_hbm, new_hbm, *refs):
    outs, (q_ref, new_ref, sem) = refs[:-3], refs[-3:]
    copies = [
        pltpu.make_async_copy(q_hbm, q_ref, sem.at[0]),
        pltpu.make_async_copy(new_hbm, new_ref, sem.at[1]),
    ]
    for copy in copies:
        copy.start()
    for copy in copies:
        copy.wait()
    mine = lax.rem(lax.axis_index("sample"), QUAD)
    rows = q_ref.shape[0] * q_ref.shape[1]

    def column(ref, head):
        return ref[:, :, lanes(head * HD, HD)].astype(F32).reshape(rows, HD).astype(BF16)

    for k in range(QUAD):
        for h in range(HPD):
            head = jnp.bitwise_xor(mine, k) * HPD + h
            for g in range(GROUP):
                outs[k][h, g * rows:(g + 1) * rows] = column(q_ref, head * GROUP + g)
            base = GROUP * rows
            outs[k][h, base:base + rows] = column(new_ref, head)
            outs[k][h, base + rows:base + 2 * rows] = column(new_ref, KVH + head)


def pack_queries(queries, new_kv):
    rows = queries.shape[0] * queries.shape[1]
    return pl.pallas_call(
        pack_queries_kernel,
        out_shape=[jax.ShapeDtypeStruct((HPD, (GROUP + 2) * rows, HD), BF16)] * QUAD,
        in_specs=[ANY, ANY],
        out_specs=[VMEM] * QUAD,
        scratch_shapes=[
            pltpu.VMEM(queries.shape, BF16),
            pltpu.VMEM(new_kv.shape, BF16),
            pltpu.SemaphoreType.DMA((2,)),
        ],
        compiler_params=params(56),
        cost_estimate=cost(0, 2 << 20),
        name="pack_queries",
    )(queries, new_kv)


def pack_kv_kernel(kv_ref, near, *refs):
    far, sem = refs[:-1], refs[-1]
    mine = lax.rem(lax.axis_index("sample"), QUAD)
    copies = []
    for h in range(HPD):
        for k in range(1, QUAD):
            head = jnp.bitwise_xor(mine, k) * HPD + h
            out = near.at[h] if k == 1 else far[h].at[k - 2]
            for part in range(2):
                copies.append(
                    pltpu.make_async_copy(
                        kv_ref.at[:, lanes((part * KVH + head) * HD, HD)],
                        out.at[:, part * HD:(part + 1) * HD],
                        sem.at[len(copies)],
                    )
                )
    for copy in copies:
        copy.start()
    for copy in copies:
        copy.wait()


def pack_kv(kv2):
    shape = jax.ShapeDtypeStruct((2, kv2.shape[0], 2 * HD), BF16)
    return pl.pallas_call(
        pack_kv_kernel,
        out_shape=[shape] * (1 + HPD),
        in_specs=[ANY],
        out_specs=[ANY] * (1 + HPD),
        scratch_shapes=[pltpu.SemaphoreType.DMA((2 * HPD * (QUAD - 1),))],
        compiler_params=params(16),
        cost_estimate=cost(0, 6 << 20),
        name="pack_kv",
    )(kv2)


def scores_of(keys, query):
    return lax.dot_general(keys, query, (((1,), (1,)), ((), ())), preferred_element_type=F32)


def values_by(values, weights):
    return lax.dot_general(values, weights, (((0,), (0,)), ((), ())), preferred_element_type=F32)


def attend_kernel(h, offsets, steps, max_tiles, counts_ref, slots_ref, kv_ref, near, same, passed, *refs):
    count = len(offsets)
    nq = QUAD if steps else count
    queries, refs = refs[:nq], refs[nq:]
    nout = 2 if steps else count
    outs, refs = refs[:nout], refs[nout:]
    held, asked, fresh, state, acc, stage, scores, weights, sem = refs
    nsample = lax.axis_size("sample")
    quads = nsample // QUAD
    index = lax.axis_index("sample")
    quad, mine = lax.div(index, QUAD), lax.rem(index, QUAD)
    blocks = kv_ref.shape[0]
    size = asked.shape[2]

    first_copies = []

    def copied(copies, source, target):
        copies.append(pltpu.make_async_copy(source, target, sem.at[len(first_copies) + len(later)]))
        copies[-1].start()

    later = []
    for n in range(nq):
        if steps:
            copied(first_copies, queries[n].at[h, 0:size], asked.at[0, n])
            copied(first_copies, queries[n].at[h, size:], fresh.at[n])
        else:
            copied(first_copies, queries[n], asked.at[n])
    for part in range(2):
        copied(
            later,
            kv_ref.at[:, :, lanes((part * KVH + mine * HPD + h) * HD, HD)],
            held.at[0:blocks, mine, :, part * HD:(part + 1) * HD],
        )
    for k, source in ((1, near.at[h]), (2, same.at[0]), (3, passed)):
        copied(later, source, held.at[0:blocks, jnp.bitwise_xor(mine, k)])
    held[blocks:] = jnp.zeros_like(held[blocks:])
    for copy in first_copies:
        copy.wait()

    def fresh_state(pair):
        parts = []
        for half in range(2):
            slot = 2 * pair + half
            rows = size // GROUP
            s = scores_of(fresh[slot, 0:rows], asked[0, slot])
            key = lax.broadcasted_iota(jnp.int32, s.shape, 0)
            row = lax.broadcasted_iota(jnp.int32, s.shape, 1) & (rows - 1)
            shift = steps.bit_length() - 1
            seen = ((row >> shift) == (key >> shift)) & ((row & (steps - 1)) >= (key & (steps - 1)))
            s = jnp.where(seen, s, NEG)
            m = jnp.max(s, axis=0, keepdims=True)
            p = jnp.exp2((s - m) * EXP_SCALE)
            l = jnp.sum(p, axis=0, keepdims=True)
            parts.append((m, l, values_by(fresh[slot, rows:], p.astype(BF16))))
        m, l, out = (jnp.concatenate(x, axis=1) for x in zip(*parts))
        state[pair, 0:1] = m
        state[pair, 1:2] = l
        acc[pair] = out

    if steps:
        for pair in range(2):
            fresh_state(pair)
    for copy in later:
        copy.wait()
    flat = held.reshape(held.shape[0] * QUAD * BLK, 2 * HD)

    def local_count(block):
        inside = jnp.clip(lax.rem(block, nsample) - QUAD * quad, 0, QUAD)
        return QUAD * lax.div(block, nsample) + inside

    def one_pass(n, pair, low, high, tiles):
        tokens = tiles * TILE
        query = asked[n, pl.ds(2 * pair, 2)].reshape(2 * size, HD)
        row = pl.multiple_of(low * BLK, BLK)
        before = state[pair, 0:1] if steps else None
        top = jnp.broadcast_to(before, (8, 2 * size)) if steps else None
        s = scores_of(flat[pl.ds(row, tokens), 0:HD], query)
        for t in range(tiles):
            tile = s[t * TILE:(t + 1) * TILE]
            if t == tiles - 1:
                token = lax.broadcasted_iota(jnp.int32, tile.shape, 0)
                tile = jnp.where(token < (high - low - t * TILE_BLOCKS) * BLK, tile, NEG)
            scores[t * TILE:(t + 1) * TILE] = tile
            part = jnp.max(tile.reshape(TILE // 8, 8, 2 * size), axis=0)
            top = part if top is None else jnp.maximum(top, part)
        m = jnp.max(top, axis=0, keepdims=True)
        shift = m * EXP_SCALE
        total = None
        for b in range(tokens // BLK):
            p = jnp.exp2(scores[b * BLK:(b + 1) * BLK] * EXP_SCALE - shift)
            weights[b * BLK:(b + 1) * BLK] = p.astype(BF16)
            part = jnp.sum(p.reshape(BLK // 8, 8, 2 * size), axis=0)
            total = part if total is None else total + part
        l = jnp.sum(total, axis=0, keepdims=True)
        out = values_by(flat[pl.ds(row, tokens), HD:2 * HD], weights[0:tokens])
        if steps:
            alpha = jnp.exp2(before * EXP_SCALE - shift)
            l = l + alpha * state[pair, 1:2]
            out = out + alpha * acc[pair]
        state[pair, 0:1] = m
        state[pair, 1:2] = l
        acc[pair] = out

    def chunk(n, _):
        offset = jnp.int32(0) if steps else offset_of(n)
        home = lax.rem(quad + offset, quads)

        def prompt_of(pair, _):
            prompt = slots_ref[QUAD * home + 2 * jnp.bitwise_xor(lax.div(mine, 2), pair)]
            start = lax.fori_loop(0, prompt, lambda p, total: total + counts_ref[p], jnp.int32(0))
            low, high = local_count(start), local_count(start + counts_ref[prompt])
            tiles = lax.div(high - low + TILE_BLOCKS - 1, TILE_BLOCKS)
            if not steps:
                @pl.when(tiles == 0)
                def _():
                    state[pair, 0:1] = jnp.full((1, 2 * size), NEG, F32)
                    state[pair, 1:2] = jnp.zeros((1, 2 * size), F32)
                    acc[pair] = jnp.zeros((HD, 2 * size), F32)

            for t in range(1, max_tiles + 1):
                @pl.when(tiles == t)
                def _(t=t):
                    one_pass(n, pair, low, high, t)

            return 0

        lax.fori_loop(0, 2, prompt_of, 0)
        lses = []
        for pair in range(2):
            m, l = state[pair, 0:1], state[pair, 1:2]
            some = l > 0.0
            safe = jnp.where(some, l, 1.0)
            lses.append(jnp.where(some, m * EXP_SCALE + jnp.log(safe) * LOG2E, NEG))
            out = acc[pair] * (1.0 / safe)
            if steps:
                outs[0][pair] = out
                outs[1][pair] = jnp.broadcast_to(lses[pair], (8, 2 * size))
            else:
                stage[n, pair * HD:(pair + 1) * HD] = out.astype(BF16)
        if not steps:
            stage[n, 2 * HD:] = stat_tile(lses)
        return 0

    def offset_of(n):
        offset = jnp.int32(offsets[0])
        for i in range(1, count):
            offset = jnp.where(n == i, offsets[i], offset)
        return offset

    lax.fori_loop(0, count, chunk, 0)
    if not steps:
        copies = []
        for n in range(count):
            copied(copies, stage.at[n], outs[n])
            later.append(copies[-1])
        for copy in copies:
            copy.wait()


def attend(h, offsets, steps, counts, slots, kv3, arrived, queries):
    count = len(offsets)
    if steps:
        size = queries[0].shape[1] * GROUP // (GROUP + 2)
        out_shape = [
            jax.ShapeDtypeStruct((2, HD, 2 * size), F32),
            jax.ShapeDtypeStruct((2, 8, 2 * size), F32),
        ]
    else:
        size = queries[0].shape[1]
        out_shape = [jax.ShapeDtypeStruct((2 * HD + STAT_ROWS, 2 * size), BF16)] * count
    blocks = kv3.shape[0]
    max_tiles = -(-(-(-MAXB // lax.axis_size("sample")) * QUAD) // TILE_BLOCKS)
    work = count * 2 * size * blocks * BLK
    return pl.pallas_call(
        functools.partial(attend_kernel, h, offsets, steps, max_tiles),
        out_shape=out_shape,
        in_specs=[SMEM, SMEM, ANY] + [ANY] * len(arrived) + [ANY] * len(queries),
        out_specs=[VMEM if steps else ANY] * len(out_shape),
        scratch_shapes=[
            pltpu.VMEM((blocks + max_tiles * TILE_BLOCKS // QUAD, QUAD, BLK, 2 * HD), BF16),
            pltpu.VMEM((count, QUAD, size, HD), BF16),
            pltpu.VMEM((QUAD, 2 * size // GROUP, HD), BF16),
            pltpu.VMEM((2, 8, 2 * size), F32),
            pltpu.VMEM((2, HD, 2 * size), F32),
            pltpu.VMEM((1 if steps else count, 2 * HD + STAT_ROWS, 2 * size), BF16),
            pltpu.VMEM((max_tiles * TILE, 2 * size), F32),
            pltpu.VMEM((max_tiles * TILE, 2 * size), BF16),
            pltpu.SemaphoreType.DMA((2 * QUAD + 2 * count + 8,)),
        ],
        compiler_params=params(48),
        cost_estimate=cost(10**9 if steps else 5 * 10**9, 4 << 20),
        name="attend_own" if steps else "attend_others",
    )(counts, slots, kv3, *arrived, *queries)


def lse_of(ref, pair):
    tail = ref[2 * HD:2 * HD + STAT_ROWS].astype(F32)[3 * pair:3 * pair + 3]
    return tail[0:1] + tail[1:2] + tail[2:3]


def stat_tile(lses):
    place = lax.broadcasted_iota(jnp.int32, (STAT_ROWS, lses[0].shape[1]), 0)
    stats = jnp.zeros(place.shape, F32)
    for pair, lse in enumerate(lses):
        coarse = lse.astype(BF16).astype(F32)
        middle = (lse - coarse).astype(BF16).astype(F32)
        for i, piece in enumerate((coarse, middle, lse - coarse - middle)):
            stats = jnp.where(place == 3 * pair + i, piece, stats)
    return stats.astype(BF16)


def merge_kernel(one_ref, two_ref, out_ref):
    lses = []
    for pair in range(2):
        one, two = lse_of(one_ref, pair), lse_of(two_ref, pair)
        top = jnp.maximum(one, two)
        w1, w2 = jnp.exp2(one - top), jnp.exp2(two - top)
        total = w1 + w2
        scale = 1.0 / total
        rows = slice(pair * HD, (pair + 1) * HD)
        merged = one_ref[rows].astype(F32) * (w1 * scale) + two_ref[rows].astype(F32) * (w2 * scale)
        out_ref[rows] = merged.astype(BF16)
        lses.append(top + jnp.log(total) * LOG2E)
    out_ref[2 * HD:] = stat_tile(lses)


def merge(one, two):
    return pl.pallas_call(
        merge_kernel,
        out_shape=jax.ShapeDtypeStruct(one.shape, BF16),
        in_specs=[VMEM, VMEM],
        out_specs=VMEM,
        compiler_params=params(16),
        cost_estimate=cost(0, 1024),
        name="merge",
    )(one, two)


def finish_kernel(steps, own_ref, own_lse_ref, *refs):
    parts, outs = refs[:-QUAD], refs[-QUAD:]
    size = own_ref.shape[2]
    rows = size // (2 * GROUP)
    for pair in range(2):
        lses = [own_lse_ref[pair, 0:1]]
        for ref in parts:
            lses.append(lse_of(ref, pair))
        top = functools.reduce(jnp.maximum, lses)
        shares = [jnp.exp2(lse - top) for lse in lses]
        scale = 1.0 / functools.reduce(jnp.add, shares)
        total = own_ref[pair] * (shares[0] * scale)
        for ref, share in zip(parts, shares[1:]):
            total = total + ref[pair * HD:(pair + 1) * HD].astype(F32) * (share * scale)
        wide = total.T.reshape(2, GROUP, rows // 8, 8, HD)
        mean = jnp.sum(wide, axis=(0, 2)) * (steps / (2.0 * rows))
        flat = mean.reshape(GROUP * 8, HD)
        place = lax.broadcasted_iota(jnp.int32, flat.shape, 0) & 7
        up, down = pltpu.roll(flat, 4, 0), pltpu.roll(flat, GROUP * 8 - 4, 0)
        flat = flat + jnp.where(place < 4, down, up)
        dev = wide - flat.reshape(GROUP, 8, HD)[None, :, None]
        coarse = flat.astype(BF16).astype(F32)
        carried = jnp.where(place < 4, coarse, flat - coarse).astype(BF16)
        dev = dev.reshape(2, size // 2, HD).astype(BF16)
        for half in range(2):
            out = outs[2 * pair + half]
            out[0:size // 2] = dev[half]
            out[size // 2:] = carried


def finish(steps, own, own_lse, parts):
    size = own.shape[2]
    return pl.pallas_call(
        functools.partial(finish_kernel, steps),
        out_shape=[jax.ShapeDtypeStruct((size // 2 + GROUP * 8, HD), BF16)] * QUAD,
        in_specs=[VMEM] * (2 + len(parts)),
        out_specs=[VMEM] * QUAD,
        compiler_params=params(48),
        cost_estimate=cost(0, 1024),
        name="finish",
    )(own, own_lse, *parts)


def emit_kernel(*refs):
    msgs, (att_ref, dev_ref) = refs[:-2], refs[-2:]
    samples, steps, _ = att_ref.shape
    rows = samples * steps
    mine = lax.rem(lax.axis_index("sample"), QUAD)
    for h in range(HPD):
        for k in range(QUAD):
            msg = msgs[h * QUAD + k]
            head = jnp.bitwise_xor(mine, k) * HPD + h
            means = msg[GROUP * rows:].astype(F32)
            for g in range(GROUP):
                dev = msg[g * rows:(g + 1) * rows].astype(F32)
                pair = means[g * 8:(g + 1) * 8]
                mean = pair + pltpu.roll(pair, 4, 0)
                att = (dev.reshape(rows // 8, 8, HD) + mean[None]).reshape(samples, steps, HD)
                cols = lanes((head * GROUP + g) * HD, HD)
                att_ref[:, :, cols] = att.astype(BF16)
                dev_ref[:, :, cols] = dev.reshape(samples, steps, HD).astype(BF16)


def emit(msgs, shape):
    return pl.pallas_call(
        emit_kernel,
        out_shape=[jax.ShapeDtypeStruct(shape, BF16)] * 2,
        in_specs=[VMEM] * len(msgs),
        out_specs=[VMEM] * 2,
        compiler_params=params(32),
        cost_estimate=cost(1 << 20, 2 << 20),
        name="emit",
    )(*msgs)


def shards(prompt_kv, prompt_blocks, slot_prompt, queries, new_kv):
    nsample = lax.axis_size("sample")
    quads = nsample // QUAD
    samples, steps, width = queries.shape
    rows = samples * steps

    def across(array, k):
        return lax.ppermute(array, "sample", [(i, i ^ k) for i in range(nsample)])

    def along(array, shift):
        return lax.ppermute(
            array, "sample", [(i, (i + shift * QUAD) % nsample) for i in range(nsample)]
        )

    kv3 = prompt_kv.reshape(prompt_kv.shape[0], BLK, prompt_kv.shape[-1])
    msgs = pack_queries(queries, new_kv)
    def tied(value, *others):
        return lax.optimization_barrier((value, others))[0]

    near, *far = pack_kv(kv3.reshape(-1, kv3.shape[-1]))
    msgs = [msgs[0]] + [across(msgs[k], k) for k in range(1, QUAD)]
    near = across(tied(near, msgs), 1).reshape(HPD, -1, BLK, 2 * HD)
    own = jnp.stack([jnp.stack([m[h, :GROUP * rows] for m in msgs]) for h in range(HPD)])
    first_hop = {shift: along(own, shift) for shift in ((-1, 1) if quads > 2 else (-1,))}
    asked = []
    for h in range(HPD):
        ahead = (quads - 1 + (1 - h % 2)) // 2 if quads > 2 else quads - 1
        held = {}
        for shift, hops in ((-1, ahead), (1, quads - 1 - ahead)):
            for s in range(1, hops + 1):
                block = first_hop[shift][h] if s == 1 else block
                if s == 2 and h:
                    block = tied(block, asked[h - 1])
                if s > 1:
                    block = along(block, shift)
                held[-shift * s % quads] = block
        asked.append(held)
    arrived = []
    for h in range(HPD):
        source = tied(far[h], arrived[-1], first_hop, near) if h else far[h]
        arrived.append(across(source, 2))

    def others(h, gate):
        handed = arrived[h][1] if gate is None else tied(arrived[h][1], gate, asked[h])
        passed = across(handed, 1).reshape(-1, BLK, 2 * HD)
        blocks = [near, arrived[h].reshape(2, -1, BLK, 2 * HD), passed]
        offsets = tuple(sorted(asked[h]))
        partial = attend(
            h, offsets, 0, prompt_blocks, slot_prompt, kv3, blocks, [asked[h][o] for o in offsets]
        )
        return blocks, dict(zip(offsets, partial))

    def chains(h):
        far_right = (quads - 1 + (1 - h % 2)) // 2
        pair = ((1, far_right), (-1, quads - 1 - far_right))
        return [c for c in sorted(pair, key=lambda x: x[1]) if c[1]]

    def sent(h, parts):
        return [along(parts[shift * hops % quads], shift) for shift, hops in chains(h)]

    def summed(h, parts, moved):
        back, turned = [], parts[min(parts)] if parts else near
        for (shift, hops), block in zip(chains(h), moved):
            for s in range(hops - 1, 0, -1):
                block = merge(parts[shift * s % quads], block)
                turned = block if s == hops - 1 else turned
                block = along(block, shift)
            back.append(block)
        return back, turned

    def finished(h, mine, back):
        done = finish(steps, *mine, back)
        return [done[0]] + [across(done[k], k) for k in range(1, QUAD)]

    final, gate, before = [], None, None
    for h in range(HPD):
        blocks, parts = others(h, gate)
        ready = parts
        if before is not None:
            mine, back = before
            final.append(finished(h - 1, mine, tied(back, parts)))
            ready = tied(parts, final[-1][0])
        moved = sent(h, ready)
        late = tied(msgs, parts, asked[h + 1:h + 2])
        mine = attend(h, (0,), steps, prompt_blocks, slot_prompt, kv3, blocks, late)
        back, turned = summed(h, parts, moved)
        before = mine, back
        gate = mine[0], turned
    final.append(finished(HPD - 1, *before))
    return tuple(emit([m for per_head in final for m in per_head], queries.shape))


def solution(mesh):
    placed = (
        P("groups", "sample", None, None),
        P("groups"),
        P("groups"),
        P(("groups", "sample"), None, None),
        P(("groups", "sample"), None, None),
    )
    return jax.shard_map(
        shards,
        mesh=mesh,
        in_specs=placed,
        out_specs=(P(("groups", "sample"), None, None), P(("groups", "sample"), None, None)),
        check_vma=False,
    )
```

```python
import functools
import math

import jax
import jax.numpy as jnp
from jax import lax
from jax.experimental import pallas as pl
from jax.experimental.pallas import tpu as pltpu
from jax.sharding import PartitionSpec as P

HEADS = 64
KVH = 8
HD = 128
BLK = 32
MAXB = 128
QUAD = 4
HPD = KVH // QUAD
GROUP = HEADS // KVH
TILE_BLOCKS = 4
TILE = TILE_BLOCKS * BLK
STAT_ROWS = 16
NEG = -1e30
LOG2E = math.log2(math.e)
EXP_SCALE = LOG2E / math.sqrt(HD)
F32 = jnp.float32
BF16 = jnp.bfloat16
ANY = pl.BlockSpec(memory_space=pl.ANY)
VMEM = pl.BlockSpec(memory_space=pltpu.VMEM)
SMEM = pl.BlockSpec(memory_space=pltpu.SMEM)


def lanes(start, size):
    return pl.ds(pl.multiple_of(start, 128), size)


def params(mib):
    return pltpu.CompilerParams(vmem_limit_bytes=mib << 20)


def cost(flops, nbytes, trans=0):
    return pl.CostEstimate(flops=flops, bytes_accessed=nbytes, transcendentals=trans)


def pack_queries_kernel(q_hbm, new_hbm, *refs):
    outs, (q_ref, new_ref, sem) = refs[:-3], refs[-3:]
    copies = [
        pltpu.make_async_copy(q_hbm, q_ref, sem.at[0]),
        pltpu.make_async_copy(new_hbm, new_ref, sem.at[1]),
    ]
    for copy in copies:
        copy.start()
    for copy in copies:
        copy.wait()
    mine = lax.rem(lax.axis_index("sample"), QUAD)
    rows = q_ref.shape[0] * q_ref.shape[1]

    def column(ref, head):
        return ref[:, :, lanes(head * HD, HD)].astype(F32).reshape(rows, HD).astype(BF16)

    for k in range(QUAD):
        for h in range(HPD):
            head = jnp.bitwise_xor(mine, k) * HPD + h
            for g in range(GROUP):
                outs[k][h, g * rows:(g + 1) * rows] = column(q_ref, head * GROUP + g)
            base = GROUP * rows
            outs[k][h, base:base + rows] = column(new_ref, head)
            outs[k][h, base + rows:base + 2 * rows] = column(new_ref, KVH + head)


def pack_queries(queries, new_kv):
    rows = queries.shape[0] * queries.shape[1]
    return pl.pallas_call(
        pack_queries_kernel,
        out_shape=[jax.ShapeDtypeStruct((HPD, (GROUP + 2) * rows, HD), BF16)] * QUAD,
        in_specs=[ANY, ANY],
        out_specs=[VMEM] * QUAD,
        scratch_shapes=[
            pltpu.VMEM(queries.shape, BF16),
            pltpu.VMEM(new_kv.shape, BF16),
            pltpu.SemaphoreType.DMA((2,)),
        ],
        compiler_params=params(56),
        cost_estimate=cost(0, 2 << 20),
        name="pack_queries",
    )(queries, new_kv)


def pack_kv_kernel(kv_ref, near, *refs):
    far, sem = refs[:-1], refs[-1]
    mine = lax.rem(lax.axis_index("sample"), QUAD)
    copies = []
    for h in range(HPD):
        for k in range(1, QUAD):
            head = jnp.bitwise_xor(mine, k) * HPD + h
            out = near.at[h] if k == 1 else far[h * (QUAD - 2) + k - 2]
            for part in range(2):
                copies.append(
                    pltpu.make_async_copy(
                        kv_ref.at[:, lanes((part * KVH + head) * HD, HD)],
                        out.at[:, part * HD:(part + 1) * HD],
                        sem.at[len(copies)],
                    )
                )
    for copy in copies:
        copy.start()
    for copy in copies:
        copy.wait()


def pack_kv(kv2):
    tokens, count = kv2.shape[0], HPD * (QUAD - 2)
    return pl.pallas_call(
        pack_kv_kernel,
        out_shape=[jax.ShapeDtypeStruct((HPD, tokens, 2 * HD), BF16)]
        + [jax.ShapeDtypeStruct((tokens, 2 * HD), BF16)] * count,
        in_specs=[ANY],
        out_specs=[ANY] * (1 + count),
        scratch_shapes=[pltpu.SemaphoreType.DMA((2 * HPD * (QUAD - 1),))],
        compiler_params=params(16),
        cost_estimate=cost(0, 6 << 20),
        name="pack_kv",
    )(kv2)


def scores_of(keys, query):
    return lax.dot_general(keys, query, (((1,), (1,)), ((), ())), preferred_element_type=F32)


def values_by(values, weights):
    return lax.dot_general(values, weights, (((0,), (0,)), ((), ())), preferred_element_type=F32)


def attend_kernel(h, offsets, steps, max_tiles, counts_ref, slots_ref, kv_ref, near, *refs):
    far, refs = refs[:QUAD - 2], refs[QUAD - 2:]
    count = len(offsets)
    nq = QUAD if steps else count
    queries, refs = refs[:nq], refs[nq:]
    nout = 2 if steps else count
    outs, refs = refs[:nout], refs[nout:]
    held, asked, fresh, state, acc, stage, scores, weights, sem = refs
    nsample = lax.axis_size("sample")
    quads = nsample // QUAD
    index = lax.axis_index("sample")
    quad, mine = lax.div(index, QUAD), lax.rem(index, QUAD)
    blocks = kv_ref.shape[0]
    size = asked.shape[2]

    first_copies = []

    def copied(copies, source, target):
        copies.append(pltpu.make_async_copy(source, target, sem.at[len(first_copies) + len(later)]))
        copies[-1].start()

    later = []
    for n in range(nq):
        if steps:
            copied(first_copies, queries[n].at[h, 0:size], asked.at[0, n])
            copied(first_copies, queries[n].at[h, size:], fresh.at[n])
        else:
            copied(first_copies, queries[n], asked.at[n])
    for part in range(2):
        copied(
            later,
            kv_ref.at[:, :, lanes((part * KVH + mine * HPD + h) * HD, HD)],
            held.at[0:blocks, mine, :, part * HD:(part + 1) * HD],
        )
    for k in range(1, QUAD):
        source = near.at[h] if k == 1 else far[k - 2]
        copied(later, source, held.at[0:blocks, jnp.bitwise_xor(mine, k)])
    held[blocks:] = jnp.zeros_like(held[blocks:])
    for copy in first_copies:
        copy.wait()

    def fresh_state(pair):
        parts = []
        for half in range(2):
            slot = 2 * pair + half
            rows = size // GROUP
            s = scores_of(fresh[slot, 0:rows], asked[0, slot])
            key = lax.broadcasted_iota(jnp.int32, s.shape, 0)
            row = lax.broadcasted_iota(jnp.int32, s.shape, 1) & (rows - 1)
            shift = steps.bit_length() - 1
            seen = ((row >> shift) == (key >> shift)) & ((row & (steps - 1)) >= (key & (steps - 1)))
            s = jnp.where(seen, s, NEG)
            m = jnp.max(s, axis=0, keepdims=True)
            p = jnp.exp2((s - m) * EXP_SCALE)
            l = jnp.sum(p, axis=0, keepdims=True)
            parts.append((m, l, values_by(fresh[slot, rows:], p.astype(BF16))))
        m, l, out = (jnp.concatenate(x, axis=1) for x in zip(*parts))
        state[pair, 0:1] = m
        state[pair, 1:2] = l
        acc[pair] = out

    if steps:
        for pair in range(2):
            fresh_state(pair)
    for copy in later:
        copy.wait()
    flat = held.reshape(held.shape[0] * QUAD * BLK, 2 * HD)

    def local_count(block):
        inside = jnp.clip(lax.rem(block, nsample) - QUAD * quad, 0, QUAD)
        return QUAD * lax.div(block, nsample) + inside

    def one_pass(n, pair, low, high, tiles):
        tokens = tiles * TILE
        query = asked[n, pl.ds(2 * pair, 2)].reshape(2 * size, HD)
        row = pl.multiple_of(low * BLK, BLK)
        before = state[pair, 0:1] if steps else None
        top = jnp.broadcast_to(before, (8, 2 * size)) if steps else None
        s = scores_of(flat[pl.ds(row, tokens), 0:HD], query)
        for t in range(tiles):
            tile = s[t * TILE:(t + 1) * TILE]
            if t == tiles - 1:
                token = lax.broadcasted_iota(jnp.int32, tile.shape, 0)
                tile = jnp.where(token < (high - low - t * TILE_BLOCKS) * BLK, tile, NEG)
            scores[t * TILE:(t + 1) * TILE] = tile
            part = jnp.max(tile.reshape(TILE // 8, 8, 2 * size), axis=0)
            top = part if top is None else jnp.maximum(top, part)
        m = jnp.max(top, axis=0, keepdims=True)
        shift = m * EXP_SCALE
        total = None
        for b in range(tokens // BLK):
            p = jnp.exp2(scores[b * BLK:(b + 1) * BLK] * EXP_SCALE - shift)
            weights[b * BLK:(b + 1) * BLK] = p.astype(BF16)
            part = jnp.sum(p.reshape(BLK // 8, 8, 2 * size), axis=0)
            total = part if total is None else total + part
        l = jnp.sum(total, axis=0, keepdims=True)
        out = values_by(flat[pl.ds(row, tokens), HD:2 * HD], weights[0:tokens])
        if steps:
            alpha = jnp.exp2(before * EXP_SCALE - shift)
            l = l + alpha * state[pair, 1:2]
            out = out + alpha * acc[pair]
        state[pair, 0:1] = m
        state[pair, 1:2] = l
        acc[pair] = out

    def chunk(n, _):
        offset = jnp.int32(0) if steps else offset_of(n)
        home = lax.rem(quad + offset, quads)

        def prompt_of(pair, _):
            prompt = slots_ref[QUAD * home + 2 * jnp.bitwise_xor(lax.div(mine, 2), pair)]
            start = lax.fori_loop(0, prompt, lambda p, total: total + counts_ref[p], jnp.int32(0))
            low, high = local_count(start), local_count(start + counts_ref[prompt])
            tiles = lax.div(high - low + TILE_BLOCKS - 1, TILE_BLOCKS)
            if not steps:
                @pl.when(tiles == 0)
                def _():
                    state[pair, 0:1] = jnp.full((1, 2 * size), NEG, F32)
                    state[pair, 1:2] = jnp.zeros((1, 2 * size), F32)
                    acc[pair] = jnp.zeros((HD, 2 * size), F32)

            for t in range(1, max_tiles + 1):
                @pl.when(tiles == t)
                def _(t=t):
                    one_pass(n, pair, low, high, t)

            return 0

        lax.fori_loop(0, 2, prompt_of, 0)
        lses = []
        for pair in range(2):
            m, l = state[pair, 0:1], state[pair, 1:2]
            some = l > 0.0
            safe = jnp.where(some, l, 1.0)
            lses.append(jnp.where(some, m * EXP_SCALE + jnp.log(safe) * LOG2E, NEG))
            out = acc[pair] * (1.0 / safe)
            if steps:
                outs[0][pair] = out
                outs[1][pair] = jnp.broadcast_to(lses[pair], (8, 2 * size))
            else:
                stage[n, pair * HD:(pair + 1) * HD] = out.astype(BF16)
        if not steps:
            stage[n, 2 * HD:] = stat_tile(lses)
        return 0

    def offset_of(n):
        offset = jnp.int32(offsets[0])
        for i in range(1, count):
            offset = jnp.where(n == i, offsets[i], offset)
        return offset

    lax.fori_loop(0, count, chunk, 0)
    if not steps:
        copies = []
        for n in range(count):
            copied(copies, stage.at[n], outs[n])
            later.append(copies[-1])
        for copy in copies:
            copy.wait()


def attend(h, offsets, steps, counts, slots, kv3, arrived, queries):
    count = len(offsets)
    if steps:
        size = queries[0].shape[1] * GROUP // (GROUP + 2)
        out_shape = [
            jax.ShapeDtypeStruct((2, HD, 2 * size), F32),
            jax.ShapeDtypeStruct((2, 8, 2 * size), F32),
        ]
    else:
        size = queries[0].shape[1]
        out_shape = [jax.ShapeDtypeStruct((2 * HD + STAT_ROWS, 2 * size), BF16)] * count
    blocks = kv3.shape[0]
    max_tiles = -(-(-(-MAXB // lax.axis_size("sample")) * QUAD) // TILE_BLOCKS)
    work = count * 2 * size * blocks * BLK
    return pl.pallas_call(
        functools.partial(attend_kernel, h, offsets, steps, max_tiles),
        out_shape=out_shape,
        in_specs=[SMEM, SMEM, ANY] + [ANY] * len(arrived) + [ANY] * len(queries),
        out_specs=[VMEM if steps else ANY] * len(out_shape),
        scratch_shapes=[
            pltpu.VMEM((blocks + max_tiles * TILE_BLOCKS // QUAD, QUAD, BLK, 2 * HD), BF16),
            pltpu.VMEM((count, QUAD, size, HD), BF16),
            pltpu.VMEM((QUAD, 2 * size // GROUP, HD), BF16),
            pltpu.VMEM((2, 8, 2 * size), F32),
            pltpu.VMEM((2, HD, 2 * size), F32),
            pltpu.VMEM((1 if steps else count, 2 * HD + STAT_ROWS, 2 * size), BF16),
            pltpu.VMEM((max_tiles * TILE, 2 * size), F32),
            pltpu.VMEM((max_tiles * TILE, 2 * size), BF16),
            pltpu.SemaphoreType.DMA((2 * QUAD + 2 * count + 8,)),
        ],
        compiler_params=params(48),
        cost_estimate=cost(10**9 if steps else 5 * 10**9, 4 << 20),
        name="attend_own" if steps else "attend_others",
    )(counts, slots, kv3, *arrived, *queries)


def lse_of(ref, pair):
    tail = ref[2 * HD:2 * HD + STAT_ROWS].astype(F32)[3 * pair:3 * pair + 3]
    return tail[0:1] + tail[1:2] + tail[2:3]


def stat_tile(lses):
    place = lax.broadcasted_iota(jnp.int32, (STAT_ROWS, lses[0].shape[1]), 0)
    stats = jnp.zeros(place.shape, F32)
    for pair, lse in enumerate(lses):
        coarse = lse.astype(BF16).astype(F32)
        middle = (lse - coarse).astype(BF16).astype(F32)
        for i, piece in enumerate((coarse, middle, lse - coarse - middle)):
            stats = jnp.where(place == 3 * pair + i, piece, stats)
    return stats.astype(BF16)


def merge_kernel(one_ref, two_ref, out_ref):
    lses = []
    for pair in range(2):
        one, two = lse_of(one_ref, pair), lse_of(two_ref, pair)
        top = jnp.maximum(one, two)
        w1, w2 = jnp.exp2(one - top), jnp.exp2(two - top)
        total = w1 + w2
        scale = 1.0 / total
        rows = slice(pair * HD, (pair + 1) * HD)
        merged = one_ref[rows].astype(F32) * (w1 * scale) + two_ref[rows].astype(F32) * (w2 * scale)
        out_ref[rows] = merged.astype(BF16)
        lses.append(top + jnp.log(total) * LOG2E)
    out_ref[2 * HD:] = stat_tile(lses)


def merge(one, two):
    return pl.pallas_call(
        merge_kernel,
        out_shape=jax.ShapeDtypeStruct(one.shape, BF16),
        in_specs=[VMEM, VMEM],
        out_specs=VMEM,
        compiler_params=params(16),
        cost_estimate=cost(0, 1024),
        name="merge",
    )(one, two)


def finish_kernel(steps, own_ref, own_lse_ref, *refs):
    parts, outs = refs[:-QUAD], refs[-QUAD:]
    size = own_ref.shape[2]
    rows = size // (2 * GROUP)
    for pair in range(2):
        lses = [own_lse_ref[pair, 0:1]]
        for ref in parts:
            lses.append(lse_of(ref, pair))
        top = functools.reduce(jnp.maximum, lses)
        shares = [jnp.exp2(lse - top) for lse in lses]
        scale = 1.0 / functools.reduce(jnp.add, shares)
        total = own_ref[pair] * (shares[0] * scale)
        for ref, share in zip(parts, shares[1:]):
            total = total + ref[pair * HD:(pair + 1) * HD].astype(F32) * (share * scale)
        wide = total.T.reshape(2, GROUP, rows // 8, 8, HD)
        mean = jnp.sum(wide, axis=(0, 2)) * (steps / (2.0 * rows))
        flat = mean.reshape(GROUP * 8, HD)
        place = lax.broadcasted_iota(jnp.int32, flat.shape, 0) & 7
        up, down = pltpu.roll(flat, 4, 0), pltpu.roll(flat, GROUP * 8 - 4, 0)
        flat = flat + jnp.where(place < 4, down, up)
        dev = wide - flat.reshape(GROUP, 8, HD)[None, :, None]
        coarse = flat.astype(BF16).astype(F32)
        carried = jnp.where(place < 4, coarse, flat - coarse).astype(BF16)
        dev = dev.reshape(2, size // 2, HD).astype(BF16)
        for half in range(2):
            out = outs[2 * pair + half]
            out[0:size // 2] = dev[half]
            out[size // 2:] = carried


def finish(steps, own, own_lse, parts):
    size = own.shape[2]
    return pl.pallas_call(
        functools.partial(finish_kernel, steps),
        out_shape=[jax.ShapeDtypeStruct((size // 2 + GROUP * 8, HD), BF16)] * QUAD,
        in_specs=[VMEM] * (2 + len(parts)),
        out_specs=[VMEM] * QUAD,
        compiler_params=params(48),
        cost_estimate=cost(0, 1024),
        name="finish",
    )(own, own_lse, *parts)


def emit_kernel(*refs):
    msgs, (att_ref, dev_ref) = refs[:-2], refs[-2:]
    samples, steps, _ = att_ref.shape
    rows = samples * steps
    mine = lax.rem(lax.axis_index("sample"), QUAD)
    for h in range(HPD):
        for k in range(QUAD):
            msg = msgs[h * QUAD + k]
            head = jnp.bitwise_xor(mine, k) * HPD + h
            means = msg[GROUP * rows:].astype(F32)
            for g in range(GROUP):
                dev = msg[g * rows:(g + 1) * rows].astype(F32)
                pair = means[g * 8:(g + 1) * 8]
                mean = pair + pltpu.roll(pair, 4, 0)
                att = (dev.reshape(rows // 8, 8, HD) + mean[None]).reshape(samples, steps, HD)
                cols = lanes((head * GROUP + g) * HD, HD)
                att_ref[:, :, cols] = att.astype(BF16)
                dev_ref[:, :, cols] = dev.reshape(samples, steps, HD).astype(BF16)


def emit(msgs, shape):
    return pl.pallas_call(
        emit_kernel,
        out_shape=[jax.ShapeDtypeStruct(shape, BF16)] * 2,
        in_specs=[VMEM] * len(msgs),
        out_specs=[VMEM] * 2,
        compiler_params=params(32),
        cost_estimate=cost(1 << 20, 2 << 20),
        name="emit",
    )(*msgs)


def shards(prompt_kv, prompt_blocks, slot_prompt, queries, new_kv):
    nsample = lax.axis_size("sample")
    quads = nsample // QUAD
    samples, steps, width = queries.shape
    rows = samples * steps

    def across(array, k):
        return lax.ppermute(array, "sample", [(i, i ^ k) for i in range(nsample)])

    def along(array, shift):
        return lax.ppermute(
            array, "sample", [(i, (i + shift * QUAD) % nsample) for i in range(nsample)]
        )

    kv3 = prompt_kv.reshape(prompt_kv.shape[0], BLK, prompt_kv.shape[-1])
    msgs = pack_queries(queries, new_kv)
    def tied(value, *others):
        return lax.optimization_barrier((value, others))[0]

    near, *far = pack_kv(kv3.reshape(-1, kv3.shape[-1]))
    msgs = [msgs[0]] + [across(msgs[k], k) for k in range(1, QUAD)]
    near = across(tied(near, msgs), 1).reshape(HPD, -1, BLK, 2 * HD)
    own = jnp.stack([jnp.stack([m[h, :GROUP * rows] for m in msgs]) for h in range(HPD)])
    first_hop = {shift: along(own, shift) for shift in ((-1, 1) if quads > 2 else (-1,))}
    asked = []
    for h in range(HPD):
        ahead = (quads - 1 + (1 - h % 2)) // 2 if quads > 2 else quads - 1
        held = {}
        for shift, hops in ((-1, ahead), (1, quads - 1 - ahead)):
            for s in range(1, hops + 1):
                block = first_hop[shift][h] if s == 1 else block
                if s == 2 and h:
                    block = tied(block, asked[h - 1])
                if s > 1:
                    block = along(block, shift)
                held[-shift * s % quads] = block
        asked.append(held)
    arrived = []
    for h in range(HPD):
        sources = far[h * (QUAD - 2):(h + 1) * (QUAD - 2)]
        if h:
            sources = tied(sources, arrived[-1], first_hop, near)
        arrived.append([across(block, 2 + i) for i, block in enumerate(sources)])

    def others(h, gate):
        received = arrived[h] if gate is None else tied(arrived[h], gate, asked[h])
        blocks = [near] + [block.reshape(-1, BLK, 2 * HD) for block in received]
        offsets = tuple(sorted(asked[h]))
        partial = attend(
            h, offsets, 0, prompt_blocks, slot_prompt, kv3, blocks, [asked[h][o] for o in offsets]
        )
        return blocks, dict(zip(offsets, partial))

    def chains(h):
        far_right = (quads - 1 + (1 - h % 2)) // 2
        pair = ((1, far_right), (-1, quads - 1 - far_right))
        return [c for c in sorted(pair, key=lambda x: x[1]) if c[1]]

    def sent(h, parts):
        return [along(parts[shift * hops % quads], shift) for shift, hops in chains(h)]

    def summed(h, parts, moved):
        back, turned = [], parts[min(parts)] if parts else near
        for (shift, hops), block in zip(chains(h), moved):
            for s in range(hops - 1, 0, -1):
                if h + 1 < HPD and s == hops - 1:
                    block = tied(block, moved)
                block = merge(parts[shift * s % quads], block)
                turned = block if s == hops - 1 else turned
                block = along(block, shift)
            back.append(block)
        return back, turned

    def finished(h, mine, back):
        done = finish(steps, *mine, back)
        return [done[0]] + [across(done[k], k) for k in range(1, QUAD)]

    final, gate, before = [], None, None
    for h in range(HPD):
        blocks, parts = others(h, gate)
        ready = parts
        if before is not None:
            mine, back = before
            final.append(finished(h - 1, mine, tied(back, parts)))
            ready = tied(parts, final[-1][0])
        moved = sent(h, ready)
        late = tied(msgs, parts, asked[h + 1:h + 2])
        mine = attend(h, (0,), steps, prompt_blocks, slot_prompt, kv3, blocks, late)
        back, turned = summed(h, parts, moved)
        before = mine, back
        gate = mine[0], turned
    final.append(finished(HPD - 1, *before))
    return tuple(emit([m for per_head in final for m in per_head], queries.shape))


def solution(mesh):
    placed = (
        P("groups", "sample", None, None),
        P("groups"),
        P("groups"),
        P(("groups", "sample"), None, None),
        P(("groups", "sample"), None, None),
    )
    return jax.shard_map(
        shards,
        mesh=mesh,
        in_specs=placed,
        out_specs=(P(("groups", "sample"), None, None), P(("groups", "sample"), None, None)),
        check_vma=False,
    )
```

```python
import functools
import math

import jax
import jax.numpy as jnp
from jax import lax
from jax.experimental import pallas as pl
from jax.experimental.pallas import tpu as pltpu
from jax.sharding import PartitionSpec as P

HEADS = 64
KVH = 8
HD = 128
BLK = 32
MAXB = 128
QUAD = 4
HPD = KVH // QUAD
GROUP = HEADS // KVH
TILE_BLOCKS = 4
TILE = TILE_BLOCKS * BLK
STAT_ROWS = 16
NEG = -1e30
LOG2E = math.log2(math.e)
EXP_SCALE = LOG2E / math.sqrt(HD)
F32 = jnp.float32
BF16 = jnp.bfloat16
ANY = pl.BlockSpec(memory_space=pl.ANY)
VMEM = pl.BlockSpec(memory_space=pltpu.VMEM)
SMEM = pl.BlockSpec(memory_space=pltpu.SMEM)


def lanes(start, size):
    return pl.ds(pl.multiple_of(start, 128), size)


def params(mib):
    return pltpu.CompilerParams(vmem_limit_bytes=mib << 20)


def cost(flops, nbytes, trans=0):
    return pl.CostEstimate(flops=flops, bytes_accessed=nbytes, transcendentals=trans)


def pack_queries_kernel(q_hbm, new_hbm, *refs):
    outs, (q_ref, new_ref, sem) = refs[:-3], refs[-3:]
    copies = [
        pltpu.make_async_copy(q_hbm, q_ref, sem.at[0]),
        pltpu.make_async_copy(new_hbm, new_ref, sem.at[1]),
    ]
    for copy in copies:
        copy.start()
    for copy in copies:
        copy.wait()
    mine = lax.rem(lax.axis_index("sample"), QUAD)
    rows = q_ref.shape[0] * q_ref.shape[1]

    def column(ref, head):
        return ref[:, :, lanes(head * HD, HD)].astype(F32).reshape(rows, HD).astype(BF16)

    for k in range(QUAD):
        for h in range(HPD):
            head = jnp.bitwise_xor(mine, k) * HPD + h
            for g in range(GROUP):
                outs[k][h, g * rows:(g + 1) * rows] = column(q_ref, head * GROUP + g)
            base = GROUP * rows
            outs[k][h, base:base + rows] = column(new_ref, head)
            outs[k][h, base + rows:base + 2 * rows] = column(new_ref, KVH + head)


def pack_queries(queries, new_kv):
    rows = queries.shape[0] * queries.shape[1]
    return pl.pallas_call(
        pack_queries_kernel,
        out_shape=[jax.ShapeDtypeStruct((HPD, (GROUP + 2) * rows, HD), BF16)] * QUAD,
        in_specs=[ANY, ANY],
        out_specs=[VMEM] * QUAD,
        scratch_shapes=[
            pltpu.VMEM(queries.shape, BF16),
            pltpu.VMEM(new_kv.shape, BF16),
            pltpu.SemaphoreType.DMA((2,)),
        ],
        compiler_params=params(56),
        cost_estimate=cost(0, 2 << 20),
        name="pack_queries",
    )(queries, new_kv)


def pack_kv_kernel(kv_ref, near, *refs):
    far, sem = refs[:-1], refs[-1]
    mine = lax.rem(lax.axis_index("sample"), QUAD)
    copies = []
    for h in range(HPD):
        for k in range(1, QUAD):
            head = jnp.bitwise_xor(mine, k) * HPD + h
            out = near.at[h] if k == 1 else far[h * (QUAD - 2) + k - 2]
            for part in range(2):
                copies.append(
                    pltpu.make_async_copy(
                        kv_ref.at[:, lanes((part * KVH + head) * HD, HD)],
                        out.at[:, part * HD:(part + 1) * HD],
                        sem.at[len(copies)],
                    )
                )
    for copy in copies:
        copy.start()
    for copy in copies:
        copy.wait()


def pack_kv(kv2):
    tokens, count = kv2.shape[0], HPD * (QUAD - 2)
    return pl.pallas_call(
        pack_kv_kernel,
        out_shape=[jax.ShapeDtypeStruct((HPD, tokens, 2 * HD), BF16)]
        + [jax.ShapeDtypeStruct((tokens, 2 * HD), BF16)] * count,
        in_specs=[ANY],
        out_specs=[ANY] * (1 + count),
        scratch_shapes=[pltpu.SemaphoreType.DMA((2 * HPD * (QUAD - 1),))],
        compiler_params=params(16),
        cost_estimate=cost(0, 6 << 20),
        name="pack_kv",
    )(kv2)


def scores_of(keys, query):
    return lax.dot_general(keys, query, (((1,), (1,)), ((), ())), preferred_element_type=F32)


def values_by(values, weights):
    return lax.dot_general(values, weights, (((0,), (0,)), ((), ())), preferred_element_type=F32)


def attend_kernel(h, offsets, steps, max_tiles, counts_ref, slots_ref, kv_ref, near, *refs):
    far, refs = refs[:QUAD - 2], refs[QUAD - 2:]
    count = len(offsets)
    nq = QUAD if steps else count
    queries, refs = refs[:nq], refs[nq:]
    nout = 2 if steps else count
    outs, refs = refs[:nout], refs[nout:]
    held, asked, fresh, state, acc, stage, scores, weights, sem = refs
    nsample = lax.axis_size("sample")
    quads = nsample // QUAD
    index = lax.axis_index("sample")
    quad, mine = lax.div(index, QUAD), lax.rem(index, QUAD)
    blocks = kv_ref.shape[0]
    size = asked.shape[2]

    first_copies = []

    def copied(copies, source, target):
        copies.append(pltpu.make_async_copy(source, target, sem.at[len(first_copies) + len(later)]))
        copies[-1].start()

    later = []
    for n in range(nq):
        if steps:
            copied(first_copies, queries[n].at[h, 0:size], asked.at[0, n])
            copied(first_copies, queries[n].at[h, size:], fresh.at[n])
        else:
            copied(first_copies, queries[n], asked.at[n])
    for part in range(2):
        copied(
            later,
            kv_ref.at[:, :, lanes((part * KVH + mine * HPD + h) * HD, HD)],
            held.at[0:blocks, mine, :, part * HD:(part + 1) * HD],
        )
    for k in range(1, QUAD):
        source = near.at[h] if k == 1 else far[k - 2]
        copied(later, source, held.at[0:blocks, jnp.bitwise_xor(mine, k)])
    held[blocks:] = jnp.zeros_like(held[blocks:])
    for copy in first_copies:
        copy.wait()

    def fresh_state(pair):
        parts = []
        for half in range(2):
            slot = 2 * pair + half
            rows = size // GROUP
            s = scores_of(fresh[slot, 0:rows], asked[0, slot])
            key = lax.broadcasted_iota(jnp.int32, s.shape, 0)
            row = lax.broadcasted_iota(jnp.int32, s.shape, 1) & (rows - 1)
            shift = steps.bit_length() - 1
            seen = ((row >> shift) == (key >> shift)) & ((row & (steps - 1)) >= (key & (steps - 1)))
            s = jnp.where(seen, s, NEG)
            m = jnp.max(s, axis=0, keepdims=True)
            p = jnp.exp2((s - m) * EXP_SCALE)
            l = jnp.sum(p, axis=0, keepdims=True)
            parts.append((m, l, values_by(fresh[slot, rows:], p.astype(BF16))))
        m, l, out = (jnp.concatenate(x, axis=1) for x in zip(*parts))
        state[pair, 0:1] = m
        state[pair, 1:2] = l
        acc[pair] = out

    if steps:
        for pair in range(2):
            fresh_state(pair)
    for copy in later:
        copy.wait()
    flat = held.reshape(held.shape[0] * QUAD * BLK, 2 * HD)

    def local_count(block):
        inside = jnp.clip(lax.rem(block, nsample) - QUAD * quad, 0, QUAD)
        return QUAD * lax.div(block, nsample) + inside

    def one_pass(n, pair, low, high, tiles):
        tokens = tiles * TILE
        row = pl.multiple_of(low * BLK, BLK)
        halves = [slice(half * size, (half + 1) * size) for half in range(2)]
        tops = []
        for half, cols in enumerate(halves):
            top = None
            s = scores_of(flat[pl.ds(row, tokens), 0:HD], asked[n, 2 * pair + half])
            for t in range(tiles):
                tile = s[t * TILE:(t + 1) * TILE]
                if t == tiles - 1:
                    token = lax.broadcasted_iota(jnp.int32, tile.shape, 0)
                    tile = jnp.where(token < (high - low - t * TILE_BLOCKS) * BLK, tile, NEG)
                scores[t * TILE:(t + 1) * TILE, cols] = tile
                part = jnp.max(tile.reshape(TILE // 8, 8, size), axis=0)
                top = part if top is None else jnp.maximum(top, part)
            tops.append(top)
        for half, cols in enumerate(halves):
            m = jnp.max(tops[half], axis=0, keepdims=True)
            if steps:
                before = state[pair, 0:1, cols]
                m = jnp.maximum(m, before)
            shift = m * EXP_SCALE
            total = None
            for b in range(tokens // BLK):
                p = jnp.exp2(scores[b * BLK:(b + 1) * BLK, cols] * EXP_SCALE - shift)
                weights[b * BLK:(b + 1) * BLK, cols] = p.astype(BF16)
                part = jnp.sum(p.reshape(BLK // 8, 8, size), axis=0)
                total = part if total is None else total + part
            l = jnp.sum(total, axis=0, keepdims=True)
            out = values_by(flat[pl.ds(row, tokens), HD:2 * HD], weights[0:tokens, cols])
            if steps:
                alpha = jnp.exp2(before * EXP_SCALE - shift)
                l = l + alpha * state[pair, 1:2, cols]
                out = out + alpha * acc[pair, :, cols]
            state[pair, 0:1, cols] = m
            state[pair, 1:2, cols] = l
            acc[pair, :, cols] = out

    def chunk(n, _):
        offset = jnp.int32(0) if steps else offset_of(n)
        home = lax.rem(quad + offset, quads)

        def prompt_of(pair, _):
            prompt = slots_ref[QUAD * home + 2 * jnp.bitwise_xor(lax.div(mine, 2), pair)]
            start = lax.fori_loop(0, prompt, lambda p, total: total + counts_ref[p], jnp.int32(0))
            low, high = local_count(start), local_count(start + counts_ref[prompt])
            tiles = lax.div(high - low + TILE_BLOCKS - 1, TILE_BLOCKS)
            if not steps:
                @pl.when(tiles == 0)
                def _():
                    state[pair, 0:1] = jnp.full((1, 2 * size), NEG, F32)
                    state[pair, 1:2] = jnp.zeros((1, 2 * size), F32)
                    acc[pair] = jnp.zeros((HD, 2 * size), F32)

            for t in range(1, max_tiles + 1):
                @pl.when(tiles == t)
                def _(t=t):
                    one_pass(n, pair, low, high, t)

            return 0

        lax.fori_loop(0, 2, prompt_of, 0)
        lses = []
        for pair in range(2):
            m, l = state[pair, 0:1], state[pair, 1:2]
            some = l > 0.0
            safe = jnp.where(some, l, 1.0)
            lses.append(jnp.where(some, m * EXP_SCALE + jnp.log(safe) * LOG2E, NEG))
            out = acc[pair] * (1.0 / safe)
            if steps:
                outs[0][pair] = out
                outs[1][pair] = jnp.broadcast_to(lses[pair], (8, 2 * size))
            else:
                stage[n, pair * HD:(pair + 1) * HD] = out.astype(BF16)
        if not steps:
            stage[n, 2 * HD:] = stat_tile(lses)
        return 0

    def offset_of(n):
        offset = jnp.int32(offsets[0])
        for i in range(1, count):
            offset = jnp.where(n == i, offsets[i], offset)
        return offset

    lax.fori_loop(0, count, chunk, 0)
    if not steps:
        copies = []
        for n in range(count):
            copied(copies, stage.at[n], outs[n])
            later.append(copies[-1])
        for copy in copies:
            copy.wait()


def attend(h, offsets, steps, counts, slots, kv3, arrived, queries):
    count = len(offsets)
    if steps:
        size = queries[0].shape[1] * GROUP // (GROUP + 2)
        out_shape = [
            jax.ShapeDtypeStruct((2, HD, 2 * size), F32),
            jax.ShapeDtypeStruct((2, 8, 2 * size), F32),
        ]
    else:
        size = queries[0].shape[1]
        out_shape = [jax.ShapeDtypeStruct((2 * HD + STAT_ROWS, 2 * size), BF16)] * count
    blocks = kv3.shape[0]
    max_tiles = -(-(-(-MAXB // lax.axis_size("sample")) * QUAD) // TILE_BLOCKS)
    work = count * 2 * size * blocks * BLK
    return pl.pallas_call(
        functools.partial(attend_kernel, h, offsets, steps, max_tiles),
        out_shape=out_shape,
        in_specs=[SMEM, SMEM, ANY] + [ANY] * len(arrived) + [ANY] * len(queries),
        out_specs=[VMEM if steps else ANY] * len(out_shape),
        scratch_shapes=[
            pltpu.VMEM((blocks + max_tiles * TILE_BLOCKS // QUAD, QUAD, BLK, 2 * HD), BF16),
            pltpu.VMEM((count, QUAD, size, HD), BF16),
            pltpu.VMEM((QUAD, 2 * size // GROUP, HD), BF16),
            pltpu.VMEM((2, 8, 2 * size), F32),
            pltpu.VMEM((2, HD, 2 * size), F32),
            pltpu.VMEM((1 if steps else count, 2 * HD + STAT_ROWS, 2 * size), BF16),
            pltpu.VMEM((max_tiles * TILE, 2 * size), F32),
            pltpu.VMEM((max_tiles * TILE, 2 * size), BF16),
            pltpu.SemaphoreType.DMA((2 * QUAD + 2 * count + 8,)),
        ],
        compiler_params=params(48),
        cost_estimate=cost(5 * 10**8 if steps else (10**10 if h else 2 * 10**9), 4 << 20),
        name="attend_own" if steps else "attend_others",
    )(counts, slots, kv3, *arrived, *queries)


def lse_of(ref, pair):
    tail = ref[2 * HD:2 * HD + STAT_ROWS].astype(F32)[3 * pair:3 * pair + 3]
    return tail[0:1] + tail[1:2] + tail[2:3]


def stat_tile(lses):
    place = lax.broadcasted_iota(jnp.int32, (STAT_ROWS, lses[0].shape[1]), 0)
    stats = jnp.zeros(place.shape, F32)
    for pair, lse in enumerate(lses):
        coarse = lse.astype(BF16).astype(F32)
        middle = (lse - coarse).astype(BF16).astype(F32)
        for i, piece in enumerate((coarse, middle, lse - coarse - middle)):
            stats = jnp.where(place == 3 * pair + i, piece, stats)
    return stats.astype(BF16)


def merge_kernel(one_ref, two_ref, out_ref):
    lses = []
    for pair in range(2):
        one, two = lse_of(one_ref, pair), lse_of(two_ref, pair)
        top = jnp.maximum(one, two)
        w1, w2 = jnp.exp2(one - top), jnp.exp2(two - top)
        total = w1 + w2
        scale = 1.0 / total
        rows = slice(pair * HD, (pair + 1) * HD)
        merged = one_ref[rows].astype(F32) * (w1 * scale) + two_ref[rows].astype(F32) * (w2 * scale)
        out_ref[rows] = merged.astype(BF16)
        lses.append(top + jnp.log(total) * LOG2E)
    out_ref[2 * HD:] = stat_tile(lses)


def merge(one, two):
    return pl.pallas_call(
        merge_kernel,
        out_shape=jax.ShapeDtypeStruct(one.shape, BF16),
        in_specs=[VMEM, VMEM],
        out_specs=VMEM,
        compiler_params=params(16),
        cost_estimate=cost(0, 1024),
        name="merge",
    )(one, two)


def finish_kernel(steps, own_ref, own_lse_ref, *refs):
    parts, outs = refs[:-QUAD], refs[-QUAD:]
    size = own_ref.shape[2]
    rows = size // (2 * GROUP)
    for pair in range(2):
        lses = [own_lse_ref[pair, 0:1]]
        for ref in parts:
            lses.append(lse_of(ref, pair))
        top = functools.reduce(jnp.maximum, lses)
        shares = [jnp.exp2(lse - top) for lse in lses]
        scale = 1.0 / functools.reduce(jnp.add, shares)
        total = own_ref[pair] * (shares[0] * scale)
        for ref, share in zip(parts, shares[1:]):
            total = total + ref[pair * HD:(pair + 1) * HD].astype(F32) * (share * scale)
        wide = total.T.reshape(2, GROUP, rows // 8, 8, HD)
        mean = jnp.sum(wide, axis=(0, 2)) * (steps / (2.0 * rows))
        flat = mean.reshape(GROUP * 8, HD)
        place = lax.broadcasted_iota(jnp.int32, flat.shape, 0) & 7
        up, down = pltpu.roll(flat, 4, 0), pltpu.roll(flat, GROUP * 8 - 4, 0)
        flat = flat + jnp.where(place < 4, down, up)
        dev = wide - flat.reshape(GROUP, 8, HD)[None, :, None]
        coarse = flat.astype(BF16).astype(F32)
        carried = jnp.where(place < 4, coarse, flat - coarse).astype(BF16)
        dev = dev.reshape(2, size // 2, HD).astype(BF16)
        for half in range(2):
            out = outs[2 * pair + half]
            out[0:size // 2] = dev[half]
            out[size // 2:] = carried


def finish(steps, own, own_lse, parts):
    size = own.shape[2]
    return pl.pallas_call(
        functools.partial(finish_kernel, steps),
        out_shape=[jax.ShapeDtypeStruct((size // 2 + GROUP * 8, HD), BF16)] * QUAD,
        in_specs=[VMEM] * (2 + len(parts)),
        out_specs=[VMEM] * QUAD,
        compiler_params=params(48),
        cost_estimate=cost(0, 1024),
        name="finish",
    )(own, own_lse, *parts)


def emit_kernel(*refs):
    msgs, (att_ref, dev_ref) = refs[:-2], refs[-2:]
    samples, steps, _ = att_ref.shape
    rows = samples * steps
    mine = lax.rem(lax.axis_index("sample"), QUAD)
    for h in range(HPD):
        for k in range(QUAD):
            msg = msgs[h * QUAD + k]
            head = jnp.bitwise_xor(mine, k) * HPD + h
            means = msg[GROUP * rows:].astype(F32)
            for g in range(GROUP):
                dev = msg[g * rows:(g + 1) * rows].astype(F32)
                pair = means[g * 8:(g + 1) * 8]
                mean = pair + pltpu.roll(pair, 4, 0)
                att = (dev.reshape(rows // 8, 8, HD) + mean[None]).reshape(samples, steps, HD)
                cols = lanes((head * GROUP + g) * HD, HD)
                att_ref[:, :, cols] = att.astype(BF16)
                dev_ref[:, :, cols] = dev.reshape(samples, steps, HD).astype(BF16)


def emit(msgs, shape):
    return pl.pallas_call(
        emit_kernel,
        out_shape=[jax.ShapeDtypeStruct(shape, BF16)] * 2,
        in_specs=[VMEM] * len(msgs),
        out_specs=[VMEM] * 2,
        compiler_params=params(32),
        cost_estimate=cost(1 << 20, 2 << 20),
        name="emit",
    )(*msgs)


def shards(prompt_kv, prompt_blocks, slot_prompt, queries, new_kv):
    nsample = lax.axis_size("sample")
    quads = nsample // QUAD
    samples, steps, width = queries.shape
    rows = samples * steps

    def across(array, k):
        return lax.ppermute(array, "sample", [(i, i ^ k) for i in range(nsample)])

    def along(array, shift):
        return lax.ppermute(
            array, "sample", [(i, (i + shift * QUAD) % nsample) for i in range(nsample)]
        )

    kv3 = prompt_kv.reshape(prompt_kv.shape[0], BLK, prompt_kv.shape[-1])
    msgs = pack_queries(queries, new_kv)
    def tied(value, *others):
        return lax.optimization_barrier((value, others))[0]

    near, *far = pack_kv(kv3.reshape(-1, kv3.shape[-1]))
    msgs = [msgs[0]] + [across(msgs[k], k) for k in range(1, QUAD)]
    near = across(tied(near, msgs), 1).reshape(HPD, -1, BLK, 2 * HD)
    own = jnp.stack([jnp.stack([m[h, :GROUP * rows] for m in msgs]) for h in range(HPD)])
    first_hop = {shift: along(own, shift) for shift in ((-1, 1) if quads > 2 else (-1,))}
    asked = []
    for h in range(HPD):
        ahead = (quads - 1 + (1 - h % 2)) // 2 if quads > 2 else quads - 1
        held = {}
        for shift, hops in ((-1, ahead), (1, quads - 1 - ahead)):
            for s in range(1, hops + 1):
                block = first_hop[shift][h] if s == 1 else block
                if s == 2 and h:
                    block = tied(block, asked[h - 1])
                if s > 1:
                    block = along(block, shift)
                held[-shift * s % quads] = block
        asked.append(held)
    arrived = []
    for h in range(HPD):
        sources = far[h * (QUAD - 2):(h + 1) * (QUAD - 2)]
        if h:
            sources = tied(sources, arrived[-1], first_hop, near)
        arrived.append([across(block, 2 + i) for i, block in enumerate(sources)])

    def chains(h):
        far_right = (quads - 1 + (1 - h % 2)) // 2
        pair = ((1, far_right), (-1, quads - 1 - far_right))
        return [c for c in sorted(pair, key=lambda x: x[1]) if c[1]]

    def others(h, gate):
        received = arrived[h] if gate is None else tied(arrived[h], gate, asked[h])
        blocks = [near] + [block.reshape(-1, BLK, 2 * HD) for block in received]

        def some(offsets, inputs):
            partial = attend(h, offsets, 0, prompt_blocks, slot_prompt, kv3, blocks, inputs)
            return dict(zip(offsets, partial))

        shift, hops = chains(h)[-1]
        lead = shift * hops % quads
        parts = some((lead,), [asked[h][lead]])
        ahead = along(parts[lead], shift)
        rest = tuple(o for o in sorted(asked[h]) if o != lead)
        if rest:
            parts.update(some(rest, tied([asked[h][o] for o in rest], parts[lead])))
        return blocks, parts, ahead

    def summed(h, parts, ahead):
        back, turned = [], ahead
        for shift, hops in chains(h)[::-1]:
            block = ahead if not back else along(parts[shift * hops % quads], shift)
            for s in range(hops - 1, 0, -1):
                block = merge(parts[shift * s % quads], block)
                if s == hops - 1 and not back:
                    turned = block
                block = along(block, shift)
            back.append(block)
        return back, turned

    def finished(h, mine, back):
        done = finish(steps, *mine, back)
        return [done[0]] + [across(done[k], k) for k in range(1, QUAD)]

    final, gate, before = [], None, None
    for h in range(HPD):
        blocks, parts, ahead = others(h, gate)
        if before is not None:
            mine, back = before
            final.append(finished(h - 1, mine, tied(back, parts)))
        late = tied(msgs, parts, asked[h + 1:h + 2], final[-1:])
        mine = attend(h, (0,), steps, prompt_blocks, slot_prompt, kv3, blocks, late)
        back, turned = summed(h, parts, ahead)
        before = mine, back
        gate = mine[0], turned
    final.append(finished(HPD - 1, *before))
    return tuple(emit([m for per_head in final for m in per_head], queries.shape))


def solution(mesh):
    placed = (
        P("groups", "sample", None, None),
        P("groups"),
        P("groups"),
        P(("groups", "sample"), None, None),
        P(("groups", "sample"), None, None),
    )
    return jax.shard_map(
        shards,
        mesh=mesh,
        in_specs=placed,
        out_specs=(P(("groups", "sample"), None, None), P(("groups", "sample"), None, None)),
        check_vma=False,
    )
```

```python
import functools
import math

import jax
import jax.numpy as jnp
from jax import lax
from jax.experimental import pallas as pl
from jax.experimental.pallas import tpu as pltpu
from jax.sharding import PartitionSpec as P

HEADS = 64
KVH = 8
HD = 128
BLK = 32
MAXB = 128
QUAD = 4
HPD = KVH // QUAD
GROUP = HEADS // KVH
TILE_BLOCKS = 4
TILE = TILE_BLOCKS * BLK
STAT_ROWS = 16
NEG = -1e30
LOG2E = math.log2(math.e)
EXP_SCALE = LOG2E / math.sqrt(HD)
F32 = jnp.float32
BF16 = jnp.bfloat16
ANY = pl.BlockSpec(memory_space=pl.ANY)
VMEM = pl.BlockSpec(memory_space=pltpu.VMEM)
SMEM = pl.BlockSpec(memory_space=pltpu.SMEM)


def lanes(start, size):
    return pl.ds(pl.multiple_of(start, 128), size)


def params(mib):
    return pltpu.CompilerParams(vmem_limit_bytes=mib << 20)


def cost(flops, nbytes, trans=0):
    return pl.CostEstimate(flops=flops, bytes_accessed=nbytes, transcendentals=trans)


def pack_queries_kernel(q_hbm, new_hbm, *refs):
    outs, (q_ref, new_ref, sem) = refs[:-3], refs[-3:]
    copies = [
        pltpu.make_async_copy(q_hbm, q_ref, sem.at[0]),
        pltpu.make_async_copy(new_hbm, new_ref, sem.at[1]),
    ]
    for copy in copies:
        copy.start()
    for copy in copies:
        copy.wait()
    mine = lax.rem(lax.axis_index("sample"), QUAD)
    rows = q_ref.shape[0] * q_ref.shape[1]

    def column(ref, head):
        return ref[:, :, lanes(head * HD, HD)].astype(F32).reshape(rows, HD).astype(BF16)

    for k in range(QUAD):
        for h in range(HPD):
            head = jnp.bitwise_xor(mine, k) * HPD + h
            for g in range(GROUP):
                outs[k][h, g * rows:(g + 1) * rows] = column(q_ref, head * GROUP + g)
            base = GROUP * rows
            outs[k][h, base:base + rows] = column(new_ref, head)
            outs[k][h, base + rows:base + 2 * rows] = column(new_ref, KVH + head)


def pack_queries(queries, new_kv):
    rows = queries.shape[0] * queries.shape[1]
    return pl.pallas_call(
        pack_queries_kernel,
        out_shape=[jax.ShapeDtypeStruct((HPD, (GROUP + 2) * rows, HD), BF16)] * QUAD,
        in_specs=[ANY, ANY],
        out_specs=[VMEM] * QUAD,
        scratch_shapes=[
            pltpu.VMEM(queries.shape, BF16),
            pltpu.VMEM(new_kv.shape, BF16),
            pltpu.SemaphoreType.DMA((2,)),
        ],
        compiler_params=params(56),
        cost_estimate=cost(0, 2 << 20),
        name="pack_queries",
    )(queries, new_kv)


def pack_kv_kernel(kv_ref, near, *refs):
    far, sem = refs[:-1], refs[-1]
    mine = lax.rem(lax.axis_index("sample"), QUAD)
    copies = []
    for h in range(HPD):
        for k in range(1, QUAD):
            head = jnp.bitwise_xor(mine, k) * HPD + h
            out = near.at[h] if k == 1 else far[h * (QUAD - 2) + k - 2]
            for part in range(2):
                copies.append(
                    pltpu.make_async_copy(
                        kv_ref.at[:, lanes((part * KVH + head) * HD, HD)],
                        out.at[:, part * HD:(part + 1) * HD],
                        sem.at[len(copies)],
                    )
                )
    for copy in copies:
        copy.start()
    for copy in copies:
        copy.wait()


def pack_kv(kv2):
    tokens, count = kv2.shape[0], HPD * (QUAD - 2)
    return pl.pallas_call(
        pack_kv_kernel,
        out_shape=[jax.ShapeDtypeStruct((HPD, tokens, 2 * HD), BF16)]
        + [jax.ShapeDtypeStruct((tokens, 2 * HD), BF16)] * count,
        in_specs=[ANY],
        out_specs=[ANY] * (1 + count),
        scratch_shapes=[pltpu.SemaphoreType.DMA((2 * HPD * (QUAD - 1),))],
        compiler_params=params(16),
        cost_estimate=cost(0, 6 << 20),
        name="pack_kv",
    )(kv2)


def scores_of(keys, query):
    return lax.dot_general(keys, query, (((1,), (1,)), ((), ())), preferred_element_type=F32)


def values_by(values, weights):
    return lax.dot_general(values, weights, (((0,), (0,)), ((), ())), preferred_element_type=F32)


def attend_kernel(h, offsets, steps, max_tiles, counts_ref, slots_ref, kv_ref, near, *refs):
    far, refs = refs[:QUAD - 2], refs[QUAD - 2:]
    count = len(offsets)
    nq = QUAD if steps else count
    queries, refs = refs[:nq], refs[nq:]
    nout = 2 if steps else count
    outs, refs = refs[:nout], refs[nout:]
    held, asked, fresh, state, acc, stage, scores, weights, sem = refs
    nsample = lax.axis_size("sample")
    quads = nsample // QUAD
    index = lax.axis_index("sample")
    quad, mine = lax.div(index, QUAD), lax.rem(index, QUAD)
    blocks = kv_ref.shape[0]
    size = asked.shape[2]

    first_copies = []

    def copied(copies, source, target):
        copies.append(pltpu.make_async_copy(source, target, sem.at[len(first_copies) + len(later)]))
        copies[-1].start()

    later = []
    for n in range(nq):
        if steps:
            copied(first_copies, queries[n].at[h, 0:size], asked.at[0, n])
            copied(first_copies, queries[n].at[h, size:], fresh.at[n])
        else:
            copied(first_copies, queries[n], asked.at[n])
    for part in range(2):
        copied(
            later,
            kv_ref.at[:, :, lanes((part * KVH + mine * HPD + h) * HD, HD)],
            held.at[0:blocks, mine, :, part * HD:(part + 1) * HD],
        )
    for k in range(1, QUAD):
        source = near.at[h] if k == 1 else far[k - 2]
        copied(later, source, held.at[0:blocks, jnp.bitwise_xor(mine, k)])
    held[blocks:] = jnp.zeros_like(held[blocks:])
    for copy in first_copies:
        copy.wait()

    def fresh_state(pair):
        parts = []
        for half in range(2):
            slot = 2 * pair + half
            rows = size // GROUP
            s = scores_of(fresh[slot, 0:rows], asked[0, slot])
            key = lax.broadcasted_iota(jnp.int32, s.shape, 0)
            row = lax.broadcasted_iota(jnp.int32, s.shape, 1) & (rows - 1)
            shift = steps.bit_length() - 1
            seen = ((row >> shift) == (key >> shift)) & ((row & (steps - 1)) >= (key & (steps - 1)))
            s = jnp.where(seen, s, NEG)
            m = jnp.max(s, axis=0, keepdims=True)
            p = jnp.exp2((s - m) * EXP_SCALE)
            l = jnp.sum(p, axis=0, keepdims=True)
            parts.append((m, l, values_by(fresh[slot, rows:], p.astype(BF16))))
        m, l, out = (jnp.concatenate(x, axis=1) for x in zip(*parts))
        state[pair, 0:1] = m
        state[pair, 1:2] = l
        acc[pair] = out

    if steps:
        for pair in range(2):
            fresh_state(pair)
    for copy in later:
        copy.wait()
    flat = held.reshape(held.shape[0] * QUAD * BLK, 2 * HD)

    def local_count(block):
        inside = jnp.clip(lax.rem(block, nsample) - QUAD * quad, 0, QUAD)
        return QUAD * lax.div(block, nsample) + inside

    def one_pass(n, pair, low, high, tiles):
        tokens = tiles * TILE
        row = pl.multiple_of(low * BLK, BLK)
        halves = [slice(half * size, (half + 1) * size) for half in range(2)]
        tops = []
        for half, cols in enumerate(halves):
            top = None
            s = scores_of(flat[pl.ds(row, tokens), 0:HD], asked[n, 2 * pair + half])
            for t in range(tiles):
                tile = s[t * TILE:(t + 1) * TILE]
                if t == tiles - 1:
                    token = lax.broadcasted_iota(jnp.int32, tile.shape, 0)
                    tile = jnp.where(token < (high - low - t * TILE_BLOCKS) * BLK, tile, NEG)
                scores[t * TILE:(t + 1) * TILE, cols] = tile
                part = jnp.max(tile.reshape(TILE // 8, 8, size), axis=0)
                top = part if top is None else jnp.maximum(top, part)
            tops.append(top)
        for half, cols in enumerate(halves):
            m = jnp.max(tops[half], axis=0, keepdims=True)
            if steps:
                before = state[pair, 0:1, cols]
                m = jnp.maximum(m, before)
            shift = m * EXP_SCALE
            total = None
            for b in range(tokens // BLK):
                p = jnp.exp2(scores[b * BLK:(b + 1) * BLK, cols] * EXP_SCALE - shift)
                weights[b * BLK:(b + 1) * BLK, cols] = p.astype(BF16)
                part = jnp.sum(p.reshape(BLK // 8, 8, size), axis=0)
                total = part if total is None else total + part
            l = jnp.sum(total, axis=0, keepdims=True)
            out = values_by(flat[pl.ds(row, tokens), HD:2 * HD], weights[0:tokens, cols])
            if steps:
                alpha = jnp.exp2(before * EXP_SCALE - shift)
                l = l + alpha * state[pair, 1:2, cols]
                out = out + alpha * acc[pair, :, cols]
            state[pair, 0:1, cols] = m
            state[pair, 1:2, cols] = l
            acc[pair, :, cols] = out

    def chunk(n, _):
        offset = jnp.int32(0) if steps else offset_of(n)
        home = lax.rem(quad + offset, quads)

        def prompt_of(pair, _):
            prompt = slots_ref[QUAD * home + 2 * jnp.bitwise_xor(lax.div(mine, 2), pair)]
            start = lax.fori_loop(0, prompt, lambda p, total: total + counts_ref[p], jnp.int32(0))
            low, high = local_count(start), local_count(start + counts_ref[prompt])
            tiles = lax.div(high - low + TILE_BLOCKS - 1, TILE_BLOCKS)
            if not steps:
                @pl.when(tiles == 0)
                def _():
                    state[pair, 0:1] = jnp.full((1, 2 * size), NEG, F32)
                    state[pair, 1:2] = jnp.zeros((1, 2 * size), F32)
                    acc[pair] = jnp.zeros((HD, 2 * size), F32)

            for t in range(1, max_tiles + 1):
                @pl.when(tiles == t)
                def _(t=t):
                    one_pass(n, pair, low, high, t)

            return 0

        lax.fori_loop(0, 2, prompt_of, 0)
        lses = []
        for pair in range(2):
            m, l = state[pair, 0:1], state[pair, 1:2]
            some = l > 0.0
            safe = jnp.where(some, l, 1.0)
            lses.append(jnp.where(some, m * EXP_SCALE + jnp.log(safe) * LOG2E, NEG))
            out = acc[pair] * (1.0 / safe)
            if steps:
                outs[0][pair] = out
                outs[1][pair] = jnp.broadcast_to(lses[pair], (8, 2 * size))
            else:
                stage[n, pair * HD:(pair + 1) * HD] = out.astype(BF16)
        if not steps:
            stage[n, 2 * HD:] = stat_tile(lses)
        return 0

    def offset_of(n):
        offset = jnp.int32(offsets[0])
        for i in range(1, count):
            offset = jnp.where(n == i, offsets[i], offset)
        return offset

    lax.fori_loop(0, count, chunk, 0)
    if not steps:
        copies = []
        for n in range(count):
            copied(copies, stage.at[n], outs[n])
            later.append(copies[-1])
        for copy in copies:
            copy.wait()


def attend(h, offsets, steps, counts, slots, kv3, arrived, queries):
    count = len(offsets)
    if steps:
        size = queries[0].shape[1] * GROUP // (GROUP + 2)
        out_shape = [
            jax.ShapeDtypeStruct((2, HD, 2 * size), F32),
            jax.ShapeDtypeStruct((2, 8, 2 * size), F32),
        ]
    else:
        size = queries[0].shape[1]
        out_shape = [jax.ShapeDtypeStruct((2 * HD + STAT_ROWS, 2 * size), BF16)] * count
    blocks = kv3.shape[0]
    max_tiles = -(-(-(-MAXB // lax.axis_size("sample")) * QUAD) // TILE_BLOCKS)
    work = count * 2 * size * blocks * BLK
    return pl.pallas_call(
        functools.partial(attend_kernel, h, offsets, steps, max_tiles),
        out_shape=out_shape,
        in_specs=[SMEM, SMEM, ANY] + [ANY] * len(arrived) + [ANY] * len(queries),
        out_specs=[VMEM if steps else ANY] * len(out_shape),
        scratch_shapes=[
            pltpu.VMEM((blocks + max_tiles * TILE_BLOCKS // QUAD, QUAD, BLK, 2 * HD), BF16),
            pltpu.VMEM((count, QUAD, size, HD), BF16),
            pltpu.VMEM((QUAD, 2 * size // GROUP, HD), BF16),
            pltpu.VMEM((2, 8, 2 * size), F32),
            pltpu.VMEM((2, HD, 2 * size), F32),
            pltpu.VMEM((1 if steps else count, 2 * HD + STAT_ROWS, 2 * size), BF16),
            pltpu.VMEM((max_tiles * TILE, 2 * size), F32),
            pltpu.VMEM((max_tiles * TILE, 2 * size), BF16),
            pltpu.SemaphoreType.DMA((2 * QUAD + 2 * count + 8,)),
        ],
        compiler_params=params(48),
        cost_estimate=cost((10**10 if h else 5 * 10**8) if steps else (10**10 if h else 2 * 10**9), 4 << 20),
        name="attend_own" if steps else "attend_others",
    )(counts, slots, kv3, *arrived, *queries)


def lse_of(ref, pair):
    tail = ref[2 * HD:2 * HD + STAT_ROWS].astype(F32)[3 * pair:3 * pair + 3]
    return tail[0:1] + tail[1:2] + tail[2:3]


def stat_tile(lses):
    place = lax.broadcasted_iota(jnp.int32, (STAT_ROWS, lses[0].shape[1]), 0)
    stats = jnp.zeros(place.shape, F32)
    for pair, lse in enumerate(lses):
        coarse = lse.astype(BF16).astype(F32)
        middle = (lse - coarse).astype(BF16).astype(F32)
        for i, piece in enumerate((coarse, middle, lse - coarse - middle)):
            stats = jnp.where(place == 3 * pair + i, piece, stats)
    return stats.astype(BF16)


def merge_kernel(one_ref, two_ref, out_ref):
    lses = []
    for pair in range(2):
        one, two = lse_of(one_ref, pair), lse_of(two_ref, pair)
        top = jnp.maximum(one, two)
        w1, w2 = jnp.exp2(one - top), jnp.exp2(two - top)
        total = w1 + w2
        scale = 1.0 / total
        rows = slice(pair * HD, (pair + 1) * HD)
        merged = one_ref[rows].astype(F32) * (w1 * scale) + two_ref[rows].astype(F32) * (w2 * scale)
        out_ref[rows] = merged.astype(BF16)
        lses.append(top + jnp.log(total) * LOG2E)
    out_ref[2 * HD:] = stat_tile(lses)


def merge(one, two):
    return pl.pallas_call(
        merge_kernel,
        out_shape=jax.ShapeDtypeStruct(one.shape, BF16),
        in_specs=[VMEM, VMEM],
        out_specs=VMEM,
        compiler_params=params(16),
        cost_estimate=cost(0, 1024),
        name="merge",
    )(one, two)


def finish_kernel(steps, own_ref, own_lse_ref, *refs):
    parts, outs = refs[:-QUAD], refs[-QUAD:]
    size = own_ref.shape[2]
    rows = size // (2 * GROUP)
    for pair in range(2):
        lses = [own_lse_ref[pair, 0:1]]
        for ref in parts:
            lses.append(lse_of(ref, pair))
        top = functools.reduce(jnp.maximum, lses)
        shares = [jnp.exp2(lse - top) for lse in lses]
        scale = 1.0 / functools.reduce(jnp.add, shares)
        total = own_ref[pair] * (shares[0] * scale)
        for ref, share in zip(parts, shares[1:]):
            total = total + ref[pair * HD:(pair + 1) * HD].astype(F32) * (share * scale)
        wide = total.T.reshape(2, GROUP, rows // 8, 8, HD)
        mean = jnp.sum(wide, axis=(0, 2)) * (steps / (2.0 * rows))
        flat = mean.reshape(GROUP * 8, HD)
        place = lax.broadcasted_iota(jnp.int32, flat.shape, 0) & 7
        up, down = pltpu.roll(flat, 4, 0), pltpu.roll(flat, GROUP * 8 - 4, 0)
        flat = flat + jnp.where(place < 4, down, up)
        dev = wide - flat.reshape(GROUP, 8, HD)[None, :, None]
        coarse = flat.astype(BF16).astype(F32)
        carried = jnp.where(place < 4, coarse, flat - coarse).astype(BF16)
        dev = dev.reshape(2, size // 2, HD).astype(BF16)
        for half in range(2):
            out = outs[2 * pair + half]
            out[0:size // 2] = dev[half]
            out[size // 2:] = carried


def finish(steps, own, own_lse, parts):
    size = own.shape[2]
    return pl.pallas_call(
        functools.partial(finish_kernel, steps),
        out_shape=[jax.ShapeDtypeStruct((size // 2 + GROUP * 8, HD), BF16)] * QUAD,
        in_specs=[VMEM] * (2 + len(parts)),
        out_specs=[VMEM] * QUAD,
        compiler_params=params(48),
        cost_estimate=cost(0, 1024),
        name="finish",
    )(own, own_lse, *parts)


def emit_kernel(*refs):
    msgs, (att_ref, dev_ref) = refs[:-2], refs[-2:]
    samples, steps, _ = att_ref.shape
    rows = samples * steps
    mine = lax.rem(lax.axis_index("sample"), QUAD)
    for h in range(HPD):
        for k in range(QUAD):
            msg = msgs[h * QUAD + k]
            head = jnp.bitwise_xor(mine, k) * HPD + h
            means = msg[GROUP * rows:].astype(F32)
            for g in range(GROUP):
                dev = msg[g * rows:(g + 1) * rows].astype(F32)
                pair = means[g * 8:(g + 1) * 8]
                mean = pair + pltpu.roll(pair, 4, 0)
                att = (dev.reshape(rows // 8, 8, HD) + mean[None]).reshape(samples, steps, HD)
                cols = lanes((head * GROUP + g) * HD, HD)
                att_ref[:, :, cols] = att.astype(BF16)
                dev_ref[:, :, cols] = dev.reshape(samples, steps, HD).astype(BF16)


def emit(msgs, shape):
    return pl.pallas_call(
        emit_kernel,
        out_shape=[jax.ShapeDtypeStruct(shape, BF16)] * 2,
        in_specs=[VMEM] * len(msgs),
        out_specs=[VMEM] * 2,
        compiler_params=params(32),
        cost_estimate=cost(1 << 20, 2 << 20),
        name="emit",
    )(*msgs)


def shards(prompt_kv, prompt_blocks, slot_prompt, queries, new_kv):
    nsample = lax.axis_size("sample")
    quads = nsample // QUAD
    samples, steps, width = queries.shape
    rows = samples * steps

    def across(array, k):
        return lax.ppermute(array, "sample", [(i, i ^ k) for i in range(nsample)])

    def along(array, shift):
        return lax.ppermute(
            array, "sample", [(i, (i + shift * QUAD) % nsample) for i in range(nsample)]
        )

    kv3 = prompt_kv.reshape(prompt_kv.shape[0], BLK, prompt_kv.shape[-1])
    msgs = pack_queries(queries, new_kv)
    def tied(value, *others):
        return lax.optimization_barrier((value, others))[0]

    near, *far = pack_kv(kv3.reshape(-1, kv3.shape[-1]))
    msgs = [msgs[0]] + [across(msgs[k], k) for k in range(1, QUAD)]
    near = across(tied(near, msgs), 1).reshape(HPD, -1, BLK, 2 * HD)
    own = jnp.stack([jnp.stack([m[h, :GROUP * rows] for m in msgs]) for h in range(HPD)])
    first_hop = {shift: along(own, shift) for shift in ((-1, 1) if quads > 2 else (-1,))}
    asked = []
    for h in range(HPD):
        ahead = (quads - 1 + (1 - h % 2)) // 2 if quads > 2 else quads - 1
        held = {}
        for shift, hops in ((-1, ahead), (1, quads - 1 - ahead)):
            for s in range(1, hops + 1):
                block = first_hop[shift][h] if s == 1 else block
                if s == 2 and h:
                    block = tied(block, asked[h - 1])
                if s > 1:
                    block = along(block, shift)
                held[-shift * s % quads] = block
        asked.append(held)
    arrived = []
    for h in range(HPD):
        sources = far[h * (QUAD - 2):(h + 1) * (QUAD - 2)]
        if h:
            sources = tied(sources, arrived[-1], first_hop, near)
        arrived.append([across(block, 2 + i) for i, block in enumerate(sources)])

    def chains(h):
        far_right = (quads - 1 + (1 - h % 2)) // 2
        pair = ((1, far_right), (-1, quads - 1 - far_right))
        return [c for c in sorted(pair, key=lambda x: x[1]) if c[1]]

    def others(h, gate):
        received = arrived[h] if gate is None else tied(arrived[h], gate, asked[h])
        blocks = [near] + [block.reshape(-1, BLK, 2 * HD) for block in received]

        def some(offsets, inputs):
            partial = attend(h, offsets, 0, prompt_blocks, slot_prompt, kv3, blocks, inputs)
            return dict(zip(offsets, partial))

        shift, hops = chains(h)[-1]
        lead = shift * hops % quads
        parts = some((lead,), [asked[h][lead]])
        ahead = along(parts[lead], shift)
        rest = tuple(o for o in sorted(asked[h]) if o != lead)
        if rest:
            parts.update(some(rest, tied([asked[h][o] for o in rest], parts[lead])))
        return blocks, parts, ahead

    def summed(h, parts, ahead):
        back, turned = [], ahead
        for shift, hops in chains(h)[::-1]:
            block = ahead if not back else along(parts[shift * hops % quads], shift)
            for s in range(hops - 1, 0, -1):
                block = merge(parts[shift * s % quads], block)
                if s == hops - 1 and not back:
                    turned = block
                block = along(block, shift)
            back.append(block)
        return back, turned

    def finished(h, mine, back):
        done = finish(steps, *mine, back)
        if final:
            done = tied(done, final[-1])
        return [done[0]] + [across(done[k], k) for k in range(1, QUAD)]

    final, gate, before = [], None, None
    for h in range(HPD):
        blocks, parts, ahead = others(h, gate)
        if before is not None:
            mine, back = before
            final.append(finished(h - 1, mine, tied(back, parts)))
        late = tied(msgs, parts, asked[h + 1:h + 2])
        mine = attend(h, (0,), steps, prompt_blocks, slot_prompt, kv3, blocks, late)
        back, turned = summed(h, parts, ahead)
        before = mine, back
        gate = mine[0], turned
    final.append(finished(HPD - 1, *before))
    return tuple(emit([m for per_head in final for m in per_head], queries.shape))


def solution(mesh):
    placed = (
        P("groups", "sample", None, None),
        P("groups"),
        P("groups"),
        P(("groups", "sample"), None, None),
        P(("groups", "sample"), None, None),
    )
    return jax.shard_map(
        shards,
        mesh=mesh,
        in_specs=placed,
        out_specs=(P(("groups", "sample"), None, None), P(("groups", "sample"), None, None)),
        check_vma=False,
    )
```

```python
import functools
import math

import jax
import jax.numpy as jnp
from jax import lax
from jax.experimental import pallas as pl
from jax.experimental.pallas import tpu as pltpu
from jax.sharding import PartitionSpec as P

HEADS = 64
KVH = 8
HD = 128
BLK = 32
MAXB = 128
QUAD = 4
HPD = KVH // QUAD
GROUP = HEADS // KVH
TILE_BLOCKS = 4
TILE = TILE_BLOCKS * BLK
STAT_ROWS = 16
NEG = -1e30
LOG2E = math.log2(math.e)
EXP_SCALE = LOG2E / math.sqrt(HD)
F32 = jnp.float32
BF16 = jnp.bfloat16
ANY = pl.BlockSpec(memory_space=pl.ANY)
VMEM = pl.BlockSpec(memory_space=pltpu.VMEM)
SMEM = pl.BlockSpec(memory_space=pltpu.SMEM)


def lanes(start, size):
    return pl.ds(pl.multiple_of(start, 128), size)


def params(mib):
    return pltpu.CompilerParams(vmem_limit_bytes=mib << 20)


def cost(flops, nbytes, trans=0):
    return pl.CostEstimate(flops=flops, bytes_accessed=nbytes, transcendentals=trans)


def pack_queries_kernel(q_hbm, new_hbm, *refs):
    outs, (q_ref, new_ref, sem) = refs[:-3], refs[-3:]
    copies = [
        pltpu.make_async_copy(q_hbm, q_ref, sem.at[0]),
        pltpu.make_async_copy(new_hbm, new_ref, sem.at[1]),
    ]
    for copy in copies:
        copy.start()
    for copy in copies:
        copy.wait()
    mine = lax.rem(lax.axis_index("sample"), QUAD)
    rows = q_ref.shape[0] * q_ref.shape[1]

    def column(ref, head):
        return ref[:, :, lanes(head * HD, HD)].astype(F32).reshape(rows, HD).astype(BF16)

    for k in range(QUAD):
        for h in range(HPD):
            head = jnp.bitwise_xor(mine, k) * HPD + h
            for g in range(GROUP):
                outs[k][h, g * rows:(g + 1) * rows] = column(q_ref, head * GROUP + g)
            base = GROUP * rows
            outs[k][h, base:base + rows] = column(new_ref, head)
            outs[k][h, base + rows:base + 2 * rows] = column(new_ref, KVH + head)


def pack_queries(queries, new_kv):
    rows = queries.shape[0] * queries.shape[1]
    return pl.pallas_call(
        pack_queries_kernel,
        out_shape=[jax.ShapeDtypeStruct((HPD, (GROUP + 2) * rows, HD), BF16)] * QUAD,
        in_specs=[ANY, ANY],
        out_specs=[VMEM] * QUAD,
        scratch_shapes=[
            pltpu.VMEM(queries.shape, BF16),
            pltpu.VMEM(new_kv.shape, BF16),
            pltpu.SemaphoreType.DMA((2,)),
        ],
        compiler_params=params(56),
        cost_estimate=cost(0, 2 << 20),
        name="pack_queries",
    )(queries, new_kv)


def pack_kv_kernel(kv_ref, near, *refs):
    far, sem = refs[:-1], refs[-1]
    mine = lax.rem(lax.axis_index("sample"), QUAD)
    copies = []
    for h in range(HPD):
        for k in range(1, QUAD):
            head = jnp.bitwise_xor(mine, k) * HPD + h
            out = near.at[h] if k == 1 else far[h * (QUAD - 2) + k - 2]
            for part in range(2):
                copies.append(
                    pltpu.make_async_copy(
                        kv_ref.at[:, lanes((part * KVH + head) * HD, HD)],
                        out.at[:, part * HD:(part + 1) * HD],
                        sem.at[len(copies)],
                    )
                )
    for copy in copies:
        copy.start()
    for copy in copies:
        copy.wait()


def pack_kv(kv2):
    tokens, count = kv2.shape[0], HPD * (QUAD - 2)
    return pl.pallas_call(
        pack_kv_kernel,
        out_shape=[jax.ShapeDtypeStruct((HPD, tokens, 2 * HD), BF16)]
        + [jax.ShapeDtypeStruct((tokens, 2 * HD), BF16)] * count,
        in_specs=[ANY],
        out_specs=[ANY] * (1 + count),
        scratch_shapes=[pltpu.SemaphoreType.DMA((2 * HPD * (QUAD - 1),))],
        compiler_params=params(16),
        cost_estimate=cost(0, 6 << 20),
        name="pack_kv",
    )(kv2)


def scores_of(keys, query):
    return lax.dot_general(keys, query, (((1,), (1,)), ((), ())), preferred_element_type=F32)


def values_by(values, weights):
    return lax.dot_general(values, weights, (((0,), (0,)), ((), ())), preferred_element_type=F32)


def attend_kernel(h, offsets, steps, max_tiles, counts_ref, slots_ref, kv_ref, near, *refs):
    far, refs = refs[:QUAD - 2], refs[QUAD - 2:]
    count = len(offsets)
    nq = QUAD if steps else count
    queries, refs = refs[:nq], refs[nq:]
    nout = 2 if steps else count
    outs, refs = refs[:nout], refs[nout:]
    held, asked, fresh, state, acc, stage, scores, weights, sem = refs
    nsample = lax.axis_size("sample")
    quads = nsample // QUAD
    index = lax.axis_index("sample")
    quad, mine = lax.div(index, QUAD), lax.rem(index, QUAD)
    blocks = kv_ref.shape[0]
    size = asked.shape[2]

    first_copies = []

    def copied(copies, source, target):
        copies.append(pltpu.make_async_copy(source, target, sem.at[len(first_copies) + len(later)]))
        copies[-1].start()

    later = []
    for n in range(nq):
        if steps:
            copied(first_copies, queries[n].at[h, 0:size], asked.at[0, n])
            copied(first_copies, queries[n].at[h, size:], fresh.at[n])
        else:
            copied(first_copies, queries[n], asked.at[n])
    for part in range(2):
        copied(
            later,
            kv_ref.at[:, :, lanes((part * KVH + mine * HPD + h) * HD, HD)],
            held.at[0:blocks, mine, :, part * HD:(part + 1) * HD],
        )
    for k in range(1, QUAD):
        source = near.at[h] if k == 1 else far[k - 2]
        copied(later, source, held.at[0:blocks, jnp.bitwise_xor(mine, k)])
    held[blocks:] = jnp.zeros_like(held[blocks:])
    for copy in first_copies:
        copy.wait()

    def fresh_state(pair):
        parts = []
        for half in range(2):
            slot = 2 * pair + half
            rows = size // GROUP
            s = scores_of(fresh[slot, 0:rows], asked[0, slot])
            key = lax.broadcasted_iota(jnp.int32, s.shape, 0)
            row = lax.broadcasted_iota(jnp.int32, s.shape, 1) & (rows - 1)
            shift = steps.bit_length() - 1
            seen = ((row >> shift) == (key >> shift)) & ((row & (steps - 1)) >= (key & (steps - 1)))
            s = jnp.where(seen, s, NEG)
            m = jnp.max(s, axis=0, keepdims=True)
            p = jnp.exp2((s - m) * EXP_SCALE)
            l = jnp.sum(p, axis=0, keepdims=True)
            parts.append((m, l, values_by(fresh[slot, rows:], p.astype(BF16))))
        m, l, out = (jnp.concatenate(x, axis=1) for x in zip(*parts))
        state[pair, 0:1] = m
        state[pair, 1:2] = l
        acc[pair] = out

    if steps:
        for pair in range(2):
            fresh_state(pair)
    for copy in later:
        copy.wait()
    flat = held.reshape(held.shape[0] * QUAD * BLK, 2 * HD)

    def local_count(block):
        inside = jnp.clip(lax.rem(block, nsample) - QUAD * quad, 0, QUAD)
        return QUAD * lax.div(block, nsample) + inside

    def one_pass(n, pair, low, high, tiles):
        tokens = tiles * TILE
        row = pl.multiple_of(low * BLK, BLK)
        halves = [slice(half * size, (half + 1) * size) for half in range(2)]
        tops = []
        for half, cols in enumerate(halves):
            top = None
            s = scores_of(flat[pl.ds(row, tokens), 0:HD], asked[n, 2 * pair + half])
            for t in range(tiles):
                tile = s[t * TILE:(t + 1) * TILE]
                if t == tiles - 1:
                    token = lax.broadcasted_iota(jnp.int32, tile.shape, 0)
                    tile = jnp.where(token < (high - low - t * TILE_BLOCKS) * BLK, tile, NEG)
                scores[t * TILE:(t + 1) * TILE, cols] = tile
                part = jnp.max(tile.reshape(TILE // 8, 8, size), axis=0)
                top = part if top is None else jnp.maximum(top, part)
            tops.append(top)
        for half, cols in enumerate(halves):
            m = jnp.max(tops[half], axis=0, keepdims=True)
            if steps:
                before = state[pair, 0:1, cols]
                m = jnp.maximum(m, before)
            shift = m * EXP_SCALE
            total = None
            for b in range(tokens // BLK):
                p = jnp.exp2(scores[b * BLK:(b + 1) * BLK, cols] * EXP_SCALE - shift)
                weights[b * BLK:(b + 1) * BLK, cols] = p.astype(BF16)
                part = jnp.sum(p.reshape(BLK // 8, 8, size), axis=0)
                total = part if total is None else total + part
            l = jnp.sum(total, axis=0, keepdims=True)
            out = values_by(flat[pl.ds(row, tokens), HD:2 * HD], weights[0:tokens, cols])
            if steps:
                alpha = jnp.exp2(before * EXP_SCALE - shift)
                l = l + alpha * state[pair, 1:2, cols]
                out = out + alpha * acc[pair, :, cols]
            state[pair, 0:1, cols] = m
            state[pair, 1:2, cols] = l
            acc[pair, :, cols] = out

    def chunk(n, _):
        offset = jnp.int32(0) if steps else offset_of(n)
        home = lax.rem(quad + offset, quads)

        def prompt_of(pair, _):
            prompt = slots_ref[QUAD * home + 2 * jnp.bitwise_xor(lax.div(mine, 2), pair)]
            start = lax.fori_loop(0, prompt, lambda p, total: total + counts_ref[p], jnp.int32(0))
            low, high = local_count(start), local_count(start + counts_ref[prompt])
            tiles = lax.div(high - low + TILE_BLOCKS - 1, TILE_BLOCKS)
            if not steps:
                @pl.when(tiles == 0)
                def _():
                    state[pair, 0:1] = jnp.full((1, 2 * size), NEG, F32)
                    state[pair, 1:2] = jnp.zeros((1, 2 * size), F32)
                    acc[pair] = jnp.zeros((HD, 2 * size), F32)

            for t in range(1, max_tiles + 1):
                @pl.when(tiles == t)
                def _(t=t):
                    one_pass(n, pair, low, high, t)

            return 0

        lax.fori_loop(0, 2, prompt_of, 0)
        lses = []
        for pair in range(2):
            m, l = state[pair, 0:1], state[pair, 1:2]
            some = l > 0.0
            safe = jnp.where(some, l, 1.0)
            lses.append(jnp.where(some, m * EXP_SCALE + jnp.log(safe) * LOG2E, NEG))
            out = acc[pair] * (1.0 / safe)
            if steps:
                outs[0][pair] = out
                outs[1][pair] = jnp.broadcast_to(lses[pair], (8, 2 * size))
            else:
                stage[n, pair * HD:(pair + 1) * HD] = out.astype(BF16)
        if not steps:
            stage[n, 2 * HD:] = stat_tile(lses)
        return 0

    def offset_of(n):
        offset = jnp.int32(offsets[0])
        for i in range(1, count):
            offset = jnp.where(n == i, offsets[i], offset)
        return offset

    lax.fori_loop(0, count, chunk, 0)
    if not steps:
        copies = []
        for n in range(count):
            copied(copies, stage.at[n], outs[n])
            later.append(copies[-1])
        for copy in copies:
            copy.wait()


def attend(h, offsets, steps, counts, slots, kv3, arrived, queries):
    count = len(offsets)
    if steps:
        size = queries[0].shape[1] * GROUP // (GROUP + 2)
        out_shape = [
            jax.ShapeDtypeStruct((2, HD, 2 * size), F32),
            jax.ShapeDtypeStruct((2, 8, 2 * size), F32),
        ]
    else:
        size = queries[0].shape[1]
        out_shape = [jax.ShapeDtypeStruct((2 * HD + STAT_ROWS, 2 * size), BF16)] * count
    blocks = kv3.shape[0]
    max_tiles = -(-(-(-MAXB // lax.axis_size("sample")) * QUAD) // TILE_BLOCKS)
    work = count * 2 * size * blocks * BLK
    return pl.pallas_call(
        functools.partial(attend_kernel, h, offsets, steps, max_tiles),
        out_shape=out_shape,
        in_specs=[SMEM, SMEM, ANY] + [ANY] * len(arrived) + [ANY] * len(queries),
        out_specs=[VMEM if steps else ANY] * len(out_shape),
        scratch_shapes=[
            pltpu.VMEM((blocks + max_tiles * TILE_BLOCKS // QUAD, QUAD, BLK, 2 * HD), BF16),
            pltpu.VMEM((count, QUAD, size, HD), BF16),
            pltpu.VMEM((QUAD, 2 * size // GROUP, HD), BF16),
            pltpu.VMEM((2, 8, 2 * size), F32),
            pltpu.VMEM((2, HD, 2 * size), F32),
            pltpu.VMEM((1 if steps else count, 2 * HD + STAT_ROWS, 2 * size), BF16),
            pltpu.VMEM((max_tiles * TILE, 2 * size), F32),
            pltpu.VMEM((max_tiles * TILE, 2 * size), BF16),
            pltpu.SemaphoreType.DMA((2 * QUAD + 2 * count + 8,)),
        ],
        compiler_params=params(48),
        cost_estimate=cost((10**10 if h else 5 * 10**8) if steps else (10**10 if h else 2 * 10**9), 4 << 20),
        name="attend_own" if steps else "attend_others",
    )(counts, slots, kv3, *arrived, *queries)


def lse_of(ref, pair):
    tail = ref[2 * HD:2 * HD + STAT_ROWS].astype(F32)[3 * pair:3 * pair + 3]
    return tail[0:1] + tail[1:2] + tail[2:3]


def stat_tile(lses):
    place = lax.broadcasted_iota(jnp.int32, (STAT_ROWS, lses[0].shape[1]), 0)
    stats = jnp.zeros(place.shape, F32)
    for pair, lse in enumerate(lses):
        coarse = lse.astype(BF16).astype(F32)
        middle = (lse - coarse).astype(BF16).astype(F32)
        for i, piece in enumerate((coarse, middle, lse - coarse - middle)):
            stats = jnp.where(place == 3 * pair + i, piece, stats)
    return stats.astype(BF16)


def merge_kernel(one_ref, two_ref, out_ref):
    lses = []
    for pair in range(2):
        one, two = lse_of(one_ref, pair), lse_of(two_ref, pair)
        top = jnp.maximum(one, two)
        w1, w2 = jnp.exp2(one - top), jnp.exp2(two - top)
        total = w1 + w2
        scale = 1.0 / total
        rows = slice(pair * HD, (pair + 1) * HD)
        merged = one_ref[rows].astype(F32) * (w1 * scale) + two_ref[rows].astype(F32) * (w2 * scale)
        out_ref[rows] = merged.astype(BF16)
        lses.append(top + jnp.log(total) * LOG2E)
    out_ref[2 * HD:] = stat_tile(lses)


def merge(one, two):
    return pl.pallas_call(
        merge_kernel,
        out_shape=jax.ShapeDtypeStruct(one.shape, BF16),
        in_specs=[VMEM, VMEM],
        out_specs=VMEM,
        compiler_params=params(16),
        cost_estimate=cost(0, 1024),
        name="merge",
    )(one, two)


def finish_kernel(steps, own_ref, own_lse_ref, *refs):
    parts, outs = refs[:-QUAD], refs[-QUAD:]
    size = own_ref.shape[2]
    rows = size // (2 * GROUP)
    for pair in range(2):
        lses = [own_lse_ref[pair, 0:1]]
        for ref in parts:
            lses.append(lse_of(ref, pair))
        top = functools.reduce(jnp.maximum, lses)
        shares = [jnp.exp2(lse - top) for lse in lses]
        scale = 1.0 / functools.reduce(jnp.add, shares)
        total = own_ref[pair] * (shares[0] * scale)
        for ref, share in zip(parts, shares[1:]):
            total = total + ref[pair * HD:(pair + 1) * HD].astype(F32) * (share * scale)
        wide = total.T.reshape(2, GROUP, rows // 8, 8, HD)
        mean = jnp.sum(wide, axis=(0, 2)) * (steps / (2.0 * rows))
        flat = mean.reshape(GROUP * 8, HD)
        place = lax.broadcasted_iota(jnp.int32, flat.shape, 0) & 7
        up, down = pltpu.roll(flat, 4, 0), pltpu.roll(flat, GROUP * 8 - 4, 0)
        flat = flat + jnp.where(place < 4, down, up)
        dev = wide - flat.reshape(GROUP, 8, HD)[None, :, None]
        coarse = flat.astype(BF16).astype(F32)
        carried = jnp.where(place < 4, coarse, flat - coarse).astype(BF16)
        dev = dev.reshape(2, size // 2, HD).astype(BF16)
        for half in range(2):
            out = outs[2 * pair + half]
            out[0:size // 2] = dev[half]
            out[size // 2:] = carried


def finish(steps, own, own_lse, parts):
    size = own.shape[2]
    return pl.pallas_call(
        functools.partial(finish_kernel, steps),
        out_shape=[jax.ShapeDtypeStruct((size // 2 + GROUP * 8, HD), BF16)] * QUAD,
        in_specs=[VMEM] * (2 + len(parts)),
        out_specs=[VMEM] * QUAD,
        compiler_params=params(48),
        cost_estimate=cost(0, 1024),
        name="finish",
    )(own, own_lse, *parts)


def emit_kernel(*refs):
    msgs, (att_ref, dev_ref) = refs[:-2], refs[-2:]
    samples, steps, _ = att_ref.shape
    rows = samples * steps
    mine = lax.rem(lax.axis_index("sample"), QUAD)
    for h in range(HPD):
        for k in range(QUAD):
            msg = msgs[h * QUAD + k]
            head = jnp.bitwise_xor(mine, k) * HPD + h
            means = msg[GROUP * rows:].astype(F32)
            for g in range(GROUP):
                dev = msg[g * rows:(g + 1) * rows].astype(F32)
                pair = means[g * 8:(g + 1) * 8]
                mean = pair + pltpu.roll(pair, 4, 0)
                att = (dev.reshape(rows // 8, 8, HD) + mean[None]).reshape(samples, steps, HD)
                cols = lanes((head * GROUP + g) * HD, HD)
                att_ref[:, :, cols] = att.astype(BF16)
                dev_ref[:, :, cols] = dev.reshape(samples, steps, HD).astype(BF16)


def emit(msgs, shape):
    return pl.pallas_call(
        emit_kernel,
        out_shape=[jax.ShapeDtypeStruct(shape, BF16)] * 2,
        in_specs=[VMEM] * len(msgs),
        out_specs=[VMEM] * 2,
        compiler_params=params(32),
        cost_estimate=cost(1 << 20, 2 << 20),
        name="emit",
    )(*msgs)


def shards(prompt_kv, prompt_blocks, slot_prompt, queries, new_kv):
    nsample = lax.axis_size("sample")
    quads = nsample // QUAD
    samples, steps, width = queries.shape
    rows = samples * steps

    def across(array, k):
        return lax.ppermute(array, "sample", [(i, i ^ k) for i in range(nsample)])

    def along(array, shift):
        return lax.ppermute(
            array, "sample", [(i, (i + shift * QUAD) % nsample) for i in range(nsample)]
        )

    kv3 = prompt_kv.reshape(prompt_kv.shape[0], BLK, prompt_kv.shape[-1])
    msgs = pack_queries(queries, new_kv)
    def tied(value, *others):
        return lax.optimization_barrier((value, others))[0]

    near, *far = pack_kv(kv3.reshape(-1, kv3.shape[-1]))
    msgs = [msgs[0]] + [across(msgs[k], k) for k in range(1, QUAD)]
    near = across(tied(near, msgs), 1).reshape(HPD, -1, BLK, 2 * HD)
    own = jnp.stack([jnp.stack([m[h, :GROUP * rows] for m in msgs]) for h in range(HPD)])
    first_hop = {shift: along(own, shift) for shift in ((-1, 1) if quads > 2 else (-1,))}
    asked = []
    for h in range(HPD):
        ahead = (quads - 1 + (1 - h % 2)) // 2 if quads > 2 else quads - 1
        held = {}
        for shift, hops in ((-1, ahead), (1, quads - 1 - ahead)):
            for s in range(1, hops + 1):
                block = first_hop[shift][h] if s == 1 else block
                if s == 2 and h:
                    block = tied(block, asked[h - 1])
                if s > 1:
                    block = along(block, shift)
                held[-shift * s % quads] = block
        asked.append(held)
    arrived = []
    for h in range(HPD):
        sources = far[h * (QUAD - 2):(h + 1) * (QUAD - 2)]
        if h:
            sources = tied(sources, arrived[-1], first_hop, near)
        arrived.append([across(block, 2 + i) for i, block in enumerate(sources)])

    def chains(h):
        far_right = (quads - 1 + (1 - h % 2)) // 2
        pair = ((1, far_right), (-1, quads - 1 - far_right))
        return [c for c in sorted(pair, key=lambda x: x[1]) if c[1]]

    def others(h, gate):
        received = arrived[h] if gate is None else tied(arrived[h], gate, asked[h])
        blocks = [near] + [block.reshape(-1, BLK, 2 * HD) for block in received]

        def some(offsets, inputs):
            partial = attend(h, offsets, 0, prompt_blocks, slot_prompt, kv3, blocks, inputs)
            return dict(zip(offsets, partial))

        shift, hops = chains(h)[-1]
        lead = shift * hops % quads
        parts = some((lead,), [asked[h][lead]])
        ahead = along(parts[lead], shift)
        rest = tuple(o for o in sorted(asked[h]) if o != lead)
        if rest:
            parts.update(some(rest, tied([asked[h][o] for o in rest], parts[lead])))
        return blocks, parts, ahead

    def summed(h, parts, ahead):
        back, turned = [], ahead
        for shift, hops in chains(h)[::-1]:
            block = ahead if not back else along(parts[shift * hops % quads], shift)
            for s in range(hops - 1, 0, -1):
                block = merge(parts[shift * s % quads], block)
                if s == hops - 1 and not back:
                    turned = block
                block = along(block, shift)
            back.append(block)
        return back, turned

    def finished(h, mine, back):
        done = finish(steps, *mine, back)
        if final:
            done = tied(done, final[-1])
        return [done[0]] + [across(done[k], k) for k in range(1, QUAD)]

    final, gate, before = [], None, None
    for h in range(HPD):
        blocks, parts, ahead = others(h, gate)
        back, turned = summed(h, parts, ahead)
        if before is not None:
            mine, earlier = before
            final.append(finished(h - 1, mine, tied(earlier, parts, turned)))
        late = tied(msgs, parts, asked[h + 1:h + 2])
        mine = attend(h, (0,), steps, prompt_blocks, slot_prompt, kv3, blocks, late)
        before = mine, back
        gate = mine[0], turned
    final.append(finished(HPD - 1, *before))
    return tuple(emit([m for per_head in final for m in per_head], queries.shape))


def solution(mesh):
    placed = (
        P("groups", "sample", None, None),
        P("groups"),
        P("groups"),
        P(("groups", "sample"), None, None),
        P(("groups", "sample"), None, None),
    )
    return jax.shard_map(
        shards,
        mesh=mesh,
        in_specs=placed,
        out_specs=(P(("groups", "sample"), None, None), P(("groups", "sample"), None, None)),
        check_vma=False,
    )
```

```python
import functools
import math

import jax
import jax.numpy as jnp
from jax import lax
from jax.experimental import pallas as pl
from jax.experimental.pallas import tpu as pltpu
from jax.sharding import PartitionSpec as P

HEADS = 64
KVH = 8
HD = 128
BLK = 32
MAXB = 128
QUAD = 4
HPD = KVH // QUAD
GROUP = HEADS // KVH
TILE_BLOCKS = 4
TILE = TILE_BLOCKS * BLK
STAT_ROWS = 16
NEG = -1e30
LOG2E = math.log2(math.e)
EXP_SCALE = LOG2E / math.sqrt(HD)
F32 = jnp.float32
BF16 = jnp.bfloat16
ANY = pl.BlockSpec(memory_space=pl.ANY)
VMEM = pl.BlockSpec(memory_space=pltpu.VMEM)
SMEM = pl.BlockSpec(memory_space=pltpu.SMEM)


def lanes(start, size):
    return pl.ds(pl.multiple_of(start, 128), size)


def params(mib):
    return pltpu.CompilerParams(vmem_limit_bytes=mib << 20)


def cost(flops, nbytes, trans=0):
    return pl.CostEstimate(flops=flops, bytes_accessed=nbytes, transcendentals=trans)


def pack_queries_kernel(q_hbm, new_hbm, *refs):
    outs, (q_ref, new_ref, sem) = refs[:-3], refs[-3:]
    copies = [
        pltpu.make_async_copy(q_hbm, q_ref, sem.at[0]),
        pltpu.make_async_copy(new_hbm, new_ref, sem.at[1]),
    ]
    for copy in copies:
        copy.start()
    for copy in copies:
        copy.wait()
    mine = lax.rem(lax.axis_index("sample"), QUAD)
    rows = q_ref.shape[0] * q_ref.shape[1]

    def column(ref, head):
        return ref[:, :, lanes(head * HD, HD)].astype(F32).reshape(rows, HD).astype(BF16)

    for k in range(QUAD):
        for h in range(HPD):
            head = jnp.bitwise_xor(mine, k) * HPD + h
            for g in range(GROUP):
                outs[k][h, g * rows:(g + 1) * rows] = column(q_ref, head * GROUP + g)
            base = GROUP * rows
            outs[k][h, base:base + rows] = column(new_ref, head)
            outs[k][h, base + rows:base + 2 * rows] = column(new_ref, KVH + head)


def pack_queries(queries, new_kv):
    rows = queries.shape[0] * queries.shape[1]
    return pl.pallas_call(
        pack_queries_kernel,
        out_shape=[jax.ShapeDtypeStruct((HPD, (GROUP + 2) * rows, HD), BF16)] * QUAD,
        in_specs=[ANY, ANY],
        out_specs=[VMEM] * QUAD,
        scratch_shapes=[
            pltpu.VMEM(queries.shape, BF16),
            pltpu.VMEM(new_kv.shape, BF16),
            pltpu.SemaphoreType.DMA((2,)),
        ],
        compiler_params=params(56),
        cost_estimate=cost(0, 2 << 20),
        name="pack_queries",
    )(queries, new_kv)


def pack_kv_kernel(kv_ref, near, *refs):
    far, sem = refs[:-1], refs[-1]
    mine = lax.rem(lax.axis_index("sample"), QUAD)
    copies = []
    for h in range(HPD):
        for k in range(1, QUAD):
            head = jnp.bitwise_xor(mine, k) * HPD + h
            out = near.at[h] if k == 1 else far[h * (QUAD - 2) + k - 2]
            for part in range(2):
                copies.append(
                    pltpu.make_async_copy(
                        kv_ref.at[:, lanes((part * KVH + head) * HD, HD)],
                        out.at[:, part * HD:(part + 1) * HD],
                        sem.at[len(copies)],
                    )
                )
    for copy in copies:
        copy.start()
    for copy in copies:
        copy.wait()


def pack_kv(kv2):
    tokens, count = kv2.shape[0], HPD * (QUAD - 2)
    return pl.pallas_call(
        pack_kv_kernel,
        out_shape=[jax.ShapeDtypeStruct((HPD, tokens, 2 * HD), BF16)]
        + [jax.ShapeDtypeStruct((tokens, 2 * HD), BF16)] * count,
        in_specs=[ANY],
        out_specs=[ANY] * (1 + count),
        scratch_shapes=[pltpu.SemaphoreType.DMA((2 * HPD * (QUAD - 1),))],
        compiler_params=params(16),
        cost_estimate=cost(0, 6 << 20),
        name="pack_kv",
    )(kv2)


def scores_of(keys, query):
    return lax.dot_general(keys, query, (((1,), (1,)), ((), ())), preferred_element_type=F32)


def values_by(values, weights):
    return lax.dot_general(values, weights, (((0,), (0,)), ((), ())), preferred_element_type=F32)


def attend_kernel(h, offsets, steps, max_tiles, counts_ref, slots_ref, kv_ref, near, *refs):
    far, refs = refs[:QUAD - 2], refs[QUAD - 2:]
    count = len(offsets)
    nq = QUAD if steps else count
    queries, refs = refs[:nq], refs[nq:]
    nout = 2 if steps else count
    outs, refs = refs[:nout], refs[nout:]
    held, asked, fresh, state, acc, stage, scores, weights, sem = refs
    nsample = lax.axis_size("sample")
    quads = nsample // QUAD
    index = lax.axis_index("sample")
    quad, mine = lax.div(index, QUAD), lax.rem(index, QUAD)
    blocks = kv_ref.shape[0]
    size = asked.shape[2]

    first_copies = []

    def copied(copies, source, target):
        copies.append(pltpu.make_async_copy(source, target, sem.at[len(first_copies) + len(later)]))
        copies[-1].start()

    later = []
    for n in range(nq):
        if steps:
            copied(first_copies, queries[n].at[h, 0:size], asked.at[0, n])
            copied(first_copies, queries[n].at[h, size:], fresh.at[n])
        else:
            copied(first_copies, queries[n], asked.at[n])
    for part in range(2):
        copied(
            later,
            kv_ref.at[:, :, lanes((part * KVH + mine * HPD + h) * HD, HD)],
            held.at[0:blocks, mine, :, part * HD:(part + 1) * HD],
        )
    for k in range(1, QUAD):
        source = near.at[h] if k == 1 else far[k - 2]
        copied(later, source, held.at[0:blocks, jnp.bitwise_xor(mine, k)])
    held[blocks:] = jnp.zeros_like(held[blocks:])
    for copy in first_copies:
        copy.wait()

    def fresh_state(pair):
        parts = []
        for half in range(2):
            slot = 2 * pair + half
            rows = size // GROUP
            s = scores_of(fresh[slot, 0:rows], asked[0, slot])
            key = lax.broadcasted_iota(jnp.int32, s.shape, 0)
            row = lax.broadcasted_iota(jnp.int32, s.shape, 1) & (rows - 1)
            shift = steps.bit_length() - 1
            seen = ((row >> shift) == (key >> shift)) & ((row & (steps - 1)) >= (key & (steps - 1)))
            s = jnp.where(seen, s, NEG)
            m = jnp.max(s, axis=0, keepdims=True)
            p = jnp.exp2((s - m) * EXP_SCALE)
            l = jnp.sum(p, axis=0, keepdims=True)
            parts.append((m, l, values_by(fresh[slot, rows:], p.astype(BF16))))
        m, l, out = (jnp.concatenate(x, axis=1) for x in zip(*parts))
        state[pair, 0:1] = m
        state[pair, 1:2] = l
        acc[pair] = out

    if steps:
        for pair in range(2):
            fresh_state(pair)
    for copy in later:
        copy.wait()
    flat = held.reshape(held.shape[0] * QUAD * BLK, 2 * HD)

    def local_count(block):
        inside = jnp.clip(lax.rem(block, nsample) - QUAD * quad, 0, QUAD)
        return QUAD * lax.div(block, nsample) + inside

    def one_pass(n, pair, low, high, tiles):
        tokens = tiles * TILE
        row = pl.multiple_of(low * BLK, BLK)
        halves = [slice(half * size, (half + 1) * size) for half in range(2)]
        tops = []
        for half, cols in enumerate(halves):
            top = None
            s = scores_of(flat[pl.ds(row, tokens), 0:HD], asked[n, 2 * pair + half])
            for t in range(tiles):
                tile = s[t * TILE:(t + 1) * TILE]
                if t == tiles - 1:
                    token = lax.broadcasted_iota(jnp.int32, tile.shape, 0)
                    tile = jnp.where(token < (high - low - t * TILE_BLOCKS) * BLK, tile, NEG)
                scores[t * TILE:(t + 1) * TILE, cols] = tile
                part = jnp.max(tile.reshape(TILE // 8, 8, size), axis=0)
                top = part if top is None else jnp.maximum(top, part)
            tops.append(top)
        for half, cols in enumerate(halves):
            m = jnp.max(tops[half], axis=0, keepdims=True)
            if steps:
                before = state[pair, 0:1, cols]
                m = jnp.maximum(m, before)
            shift = m * EXP_SCALE
            total = None
            for b in range(tokens // BLK):
                p = jnp.exp2(scores[b * BLK:(b + 1) * BLK, cols] * EXP_SCALE - shift)
                weights[b * BLK:(b + 1) * BLK, cols] = p.astype(BF16)
                part = jnp.sum(p.reshape(BLK // 8, 8, size), axis=0)
                total = part if total is None else total + part
            l = jnp.sum(total, axis=0, keepdims=True)
            out = values_by(flat[pl.ds(row, tokens), HD:2 * HD], weights[0:tokens, cols])
            if steps:
                alpha = jnp.exp2(before * EXP_SCALE - shift)
                l = l + alpha * state[pair, 1:2, cols]
                out = out + alpha * acc[pair, :, cols]
            state[pair, 0:1, cols] = m
            state[pair, 1:2, cols] = l
            acc[pair, :, cols] = out

    def chunk(n, _):
        offset = jnp.int32(0) if steps else offset_of(n)
        home = lax.rem(quad + offset, quads)

        def prompt_of(pair, _):
            prompt = slots_ref[QUAD * home + 2 * jnp.bitwise_xor(lax.div(mine, 2), pair)]
            start = lax.fori_loop(0, prompt, lambda p, total: total + counts_ref[p], jnp.int32(0))
            low, high = local_count(start), local_count(start + counts_ref[prompt])
            tiles = lax.div(high - low + TILE_BLOCKS - 1, TILE_BLOCKS)
            if not steps:
                @pl.when(tiles == 0)
                def _():
                    state[pair, 0:1] = jnp.full((1, 2 * size), NEG, F32)
                    state[pair, 1:2] = jnp.zeros((1, 2 * size), F32)
                    acc[pair] = jnp.zeros((HD, 2 * size), F32)

            for t in range(1, max_tiles + 1):
                @pl.when(tiles == t)
                def _(t=t):
                    one_pass(n, pair, low, high, t)

            return 0

        lax.fori_loop(0, 2, prompt_of, 0)
        lses = []
        for pair in range(2):
            m, l = state[pair, 0:1], state[pair, 1:2]
            some = l > 0.0
            safe = jnp.where(some, l, 1.0)
            lses.append(jnp.where(some, m * EXP_SCALE + jnp.log(safe) * LOG2E, NEG))
            out = acc[pair] * (1.0 / safe)
            if steps:
                outs[0][pair] = out
                outs[1][pair] = jnp.broadcast_to(lses[pair], (8, 2 * size))
            else:
                stage[n, pair * HD:(pair + 1) * HD] = out.astype(BF16)
        if not steps:
            stage[n, 2 * HD:] = stat_tile(lses)
        return 0

    def offset_of(n):
        offset = jnp.int32(offsets[0])
        for i in range(1, count):
            offset = jnp.where(n == i, offsets[i], offset)
        return offset

    lax.fori_loop(0, count, chunk, 0)
    if not steps:
        copies = []
        for n in range(count):
            copied(copies, stage.at[n], outs[n])
            later.append(copies[-1])
        for copy in copies:
            copy.wait()


def attend(h, offsets, steps, counts, slots, kv3, arrived, queries):
    count = len(offsets)
    if steps:
        size = queries[0].shape[1] * GROUP // (GROUP + 2)
        out_shape = [
            jax.ShapeDtypeStruct((2, HD, 2 * size), F32),
            jax.ShapeDtypeStruct((2, 8, 2 * size), F32),
        ]
    else:
        size = queries[0].shape[1]
        out_shape = [jax.ShapeDtypeStruct((2 * HD + STAT_ROWS, 2 * size), BF16)] * count
    blocks = kv3.shape[0]
    max_tiles = -(-(-(-MAXB // lax.axis_size("sample")) * QUAD) // TILE_BLOCKS)
    work = count * 2 * size * blocks * BLK
    return pl.pallas_call(
        functools.partial(attend_kernel, h, offsets, steps, max_tiles),
        out_shape=out_shape,
        in_specs=[SMEM, SMEM, ANY] + [ANY] * len(arrived) + [ANY] * len(queries),
        out_specs=[VMEM if steps else ANY] * len(out_shape),
        scratch_shapes=[
            pltpu.VMEM((blocks + max_tiles * TILE_BLOCKS // QUAD, QUAD, BLK, 2 * HD), BF16),
            pltpu.VMEM((count, QUAD, size, HD), BF16),
            pltpu.VMEM((QUAD, 2 * size // GROUP, HD), BF16),
            pltpu.VMEM((2, 8, 2 * size), F32),
            pltpu.VMEM((2, HD, 2 * size), F32),
            pltpu.VMEM((1 if steps else count, 2 * HD + STAT_ROWS, 2 * size), BF16),
            pltpu.VMEM((max_tiles * TILE, 2 * size), F32),
            pltpu.VMEM((max_tiles * TILE, 2 * size), BF16),
            pltpu.SemaphoreType.DMA((2 * QUAD + 2 * count + 8,)),
        ],
        compiler_params=params(48),
        cost_estimate=cost(5 * 10**8 if steps else (10**10 if h else 2 * 10**9), 4 << 20),
        name="attend_own" if steps else "attend_others",
    )(counts, slots, kv3, *arrived, *queries)


def lse_of(ref, pair):
    tail = ref[2 * HD:2 * HD + STAT_ROWS].astype(F32)[3 * pair:3 * pair + 3]
    return tail[0:1] + tail[1:2] + tail[2:3]


def stat_tile(lses):
    place = lax.broadcasted_iota(jnp.int32, (STAT_ROWS, lses[0].shape[1]), 0)
    stats = jnp.zeros(place.shape, F32)
    for pair, lse in enumerate(lses):
        coarse = lse.astype(BF16).astype(F32)
        middle = (lse - coarse).astype(BF16).astype(F32)
        for i, piece in enumerate((coarse, middle, lse - coarse - middle)):
            stats = jnp.where(place == 3 * pair + i, piece, stats)
    return stats.astype(BF16)


def merge_kernel(one_ref, two_ref, out_ref):
    lses = []
    for pair in range(2):
        one, two = lse_of(one_ref, pair), lse_of(two_ref, pair)
        top = jnp.maximum(one, two)
        w1, w2 = jnp.exp2(one - top), jnp.exp2(two - top)
        total = w1 + w2
        scale = 1.0 / total
        rows = slice(pair * HD, (pair + 1) * HD)
        merged = one_ref[rows].astype(F32) * (w1 * scale) + two_ref[rows].astype(F32) * (w2 * scale)
        out_ref[rows] = merged.astype(BF16)
        lses.append(top + jnp.log(total) * LOG2E)
    out_ref[2 * HD:] = stat_tile(lses)


def merge(one, two):
    return pl.pallas_call(
        merge_kernel,
        out_shape=jax.ShapeDtypeStruct(one.shape, BF16),
        in_specs=[VMEM, VMEM],
        out_specs=VMEM,
        compiler_params=params(16),
        cost_estimate=cost(0, 1024),
        name="merge",
    )(one, two)


def finish_kernel(steps, own_ref, own_lse_ref, *refs):
    parts, outs = refs[:-QUAD], refs[-QUAD:]
    size = own_ref.shape[2]
    rows = size // (2 * GROUP)
    for pair in range(2):
        lses = [own_lse_ref[pair, 0:1]]
        for ref in parts:
            lses.append(lse_of(ref, pair))
        top = functools.reduce(jnp.maximum, lses)
        shares = [jnp.exp2(lse - top) for lse in lses]
        scale = 1.0 / functools.reduce(jnp.add, shares)
        total = own_ref[pair] * (shares[0] * scale)
        for ref, share in zip(parts, shares[1:]):
            total = total + ref[pair * HD:(pair + 1) * HD].astype(F32) * (share * scale)
        wide = total.T.reshape(2, GROUP, rows // 8, 8, HD)
        mean = jnp.sum(wide, axis=(0, 2)) * (steps / (2.0 * rows))
        flat = mean.reshape(GROUP * 8, HD)
        place = lax.broadcasted_iota(jnp.int32, flat.shape, 0) & 7
        up, down = pltpu.roll(flat, 4, 0), pltpu.roll(flat, GROUP * 8 - 4, 0)
        flat = flat + jnp.where(place < 4, down, up)
        dev = wide - flat.reshape(GROUP, 8, HD)[None, :, None]
        coarse = flat.astype(BF16).astype(F32)
        carried = jnp.where(place < 4, coarse, flat - coarse).astype(BF16)
        dev = dev.reshape(2, size // 2, HD).astype(BF16)
        for half in range(2):
            out = outs[2 * pair + half]
            out[0:size // 2] = dev[half]
            out[size // 2:] = carried


def finish(steps, own, own_lse, parts):
    size = own.shape[2]
    return pl.pallas_call(
        functools.partial(finish_kernel, steps),
        out_shape=[jax.ShapeDtypeStruct((size // 2 + GROUP * 8, HD), BF16)] * QUAD,
        in_specs=[VMEM] * (2 + len(parts)),
        out_specs=[VMEM] * QUAD,
        compiler_params=params(48),
        cost_estimate=cost(0, 1024),
        name="finish",
    )(own, own_lse, *parts)


def emit_kernel(*refs):
    msgs, (att_ref, dev_ref) = refs[:-2], refs[-2:]
    samples, steps, _ = att_ref.shape
    rows = samples * steps
    mine = lax.rem(lax.axis_index("sample"), QUAD)
    for h in range(HPD):
        for k in range(QUAD):
            msg = msgs[h * QUAD + k]
            head = jnp.bitwise_xor(mine, k) * HPD + h
            means = msg[GROUP * rows:].astype(F32)
            for g in range(GROUP):
                dev = msg[g * rows:(g + 1) * rows].astype(F32)
                pair = means[g * 8:(g + 1) * 8]
                mean = pair + pltpu.roll(pair, 4, 0)
                att = (dev.reshape(rows // 8, 8, HD) + mean[None]).reshape(samples, steps, HD)
                cols = lanes((head * GROUP + g) * HD, HD)
                att_ref[:, :, cols] = att.astype(BF16)
                dev_ref[:, :, cols] = dev.reshape(samples, steps, HD).astype(BF16)


def emit(msgs, shape):
    return pl.pallas_call(
        emit_kernel,
        out_shape=[jax.ShapeDtypeStruct(shape, BF16)] * 2,
        in_specs=[VMEM] * len(msgs),
        out_specs=[VMEM] * 2,
        compiler_params=params(32),
        cost_estimate=cost(1 << 20, 2 << 20),
        name="emit",
    )(*msgs)


def shards(prompt_kv, prompt_blocks, slot_prompt, queries, new_kv):
    nsample = lax.axis_size("sample")
    quads = nsample // QUAD
    samples, steps, width = queries.shape
    rows = samples * steps

    def across(array, k):
        return lax.ppermute(array, "sample", [(i, i ^ k) for i in range(nsample)])

    def along(array, shift):
        return lax.ppermute(
            array, "sample", [(i, (i + shift * QUAD) % nsample) for i in range(nsample)]
        )

    kv3 = prompt_kv.reshape(prompt_kv.shape[0], BLK, prompt_kv.shape[-1])
    msgs = pack_queries(queries, new_kv)
    def tied(value, *others):
        return lax.optimization_barrier((value, others))[0]

    near, *far = pack_kv(kv3.reshape(-1, kv3.shape[-1]))
    msgs = [msgs[0]] + [across(msgs[k], k) for k in range(1, QUAD)]
    near = across(tied(near, msgs), 1).reshape(HPD, -1, BLK, 2 * HD)
    own = jnp.stack([jnp.stack([m[h, :GROUP * rows] for m in msgs]) for h in range(HPD)])
    first_hop = {shift: along(own, shift) for shift in ((-1, 1) if quads > 2 else (-1,))}
    asked = []
    for h in range(HPD):
        ahead = (quads - 1 + (1 - h % 2)) // 2 if quads > 2 else quads - 1
        held = {}
        for shift, hops in ((-1, ahead), (1, quads - 1 - ahead)):
            for s in range(1, hops + 1):
                block = first_hop[shift][h] if s == 1 else block
                if s == 2 and h:
                    block = tied(block, asked[h - 1])
                if s > 1:
                    block = along(block, shift)
                held[-shift * s % quads] = block
        asked.append(held)
    arrived = []
    for h in range(HPD):
        sources = far[h * (QUAD - 2):(h + 1) * (QUAD - 2)]
        if h:
            sources = tied(sources, first_hop[-1], near)
        arrived.append([across(block, 2 + i) for i, block in enumerate(sources)])

    def chains(h):
        far_right = (quads - 1 + (1 - h % 2)) // 2
        pair = ((1, far_right), (-1, quads - 1 - far_right))
        return [c for c in sorted(pair, key=lambda x: x[1]) if c[1]]

    def others(h, gate):
        received = arrived[h] if gate is None else tied(arrived[h], gate, asked[h])
        blocks = [near] + [block.reshape(-1, BLK, 2 * HD) for block in received]

        def some(offsets, inputs):
            partial = attend(h, offsets, 0, prompt_blocks, slot_prompt, kv3, blocks, inputs)
            return dict(zip(offsets, partial))

        shift, hops = chains(h)[-1]
        lead = shift * hops % quads
        parts = some((lead,), [asked[h][lead]])
        ahead = along(parts[lead], shift)
        rest = tuple(o for o in sorted(asked[h]) if o != lead)
        if rest:
            parts.update(some(rest, tied([asked[h][o] for o in rest], parts[lead])))
        return blocks, parts, ahead

    def summed(h, parts, ahead):
        back, turned = [], ahead
        for shift, hops in chains(h)[::-1]:
            block = ahead if not back else along(parts[shift * hops % quads], shift)
            for s in range(hops - 1, 0, -1):
                block = merge(parts[shift * s % quads], block)
                if s == hops - 1 and not back:
                    turned = block
                block = along(block, shift)
            back.append(block)
        return back, turned

    def finished(h, mine, back):
        done = finish(steps, *mine, back)
        return [done[0]] + [across(done[k], k) for k in range(1, QUAD)]

    final, gate, before = [], None, None
    for h in range(HPD):
        blocks, parts, ahead = others(h, gate)
        if before is not None:
            mine, back = before
            final.append(finished(h - 1, mine, tied(back, parts)))
        late = tied(msgs, parts, asked[h + 1:h + 2], final[-1:])
        mine = attend(h, (0,), steps, prompt_blocks, slot_prompt, kv3, blocks, late)
        back, turned = summed(h, parts, ahead)
        before = mine, back
        gate = mine[0], turned
    final.append(finished(HPD - 1, *before))
    return tuple(emit([m for per_head in final for m in per_head], queries.shape))


def solution(mesh):
    placed = (
        P("groups", "sample", None, None),
        P("groups"),
        P("groups"),
        P(("groups", "sample"), None, None),
        P(("groups", "sample"), None, None),
    )
    return jax.shard_map(
        shards,
        mesh=mesh,
        in_specs=placed,
        out_specs=(P(("groups", "sample"), None, None), P(("groups", "sample"), None, None)),
        check_vma=False,
    )
```
